32 devices in a mesh: dp: 8 (over z, x), tensor: 4 (over y, core).
Axes of the slice: x: 2, y: 2, z: 4, core: 2. Of those that a mesh axis runs over, the one named last changes fastest.
Arguments:
- block_input: bfloat16 [8192, 768], P(('dp', 'tensor')), may hold values from -6 to 6
- out_cotangent: bfloat16 [8192, 768], P(('dp', 'tensor')), may hold values from -6 to 6
- seq_lengths: int32 [8, 4], replicated, may hold values from 1 to 682, 1024 in all within a row
- pack_order: int32 [8], replicated, may hold values from 0 to 7, each once
- ln1_gain: float32 [768], replicated, may hold values from 0.5 to 1.5
- ln1_bias: float32 [768], replicated, may hold values from -1.5 to 1.5
- qkv_weight: float32 [768, 3, 768], P('dp', None, 'tensor'), may hold values from -0.21875 to 0.21875
- qv_bias: float32 [2, 768], P(None, 'tensor'), may hold values from -1.5 to 1.5
- attn_out_weight: float32 [768, 768], P('tensor', 'dp'), may hold values from -1.75 to 1.75
- attn_out_bias: float32 [768], replicated, may hold values from -1.5 to 1.5
- ln2_gain: float32 [768], replicated, may hold values from 0.5 to 1.5
- ln2_bias: float32 [768], replicated, may hold values from -1.5 to 1.5
- fc_weight: float32 [768, 3072], P('dp', 'tensor'), may hold values from -0.21875 to 0.21875
- fc_bias: float32 [3072], P('tensor'), may hold values from -1.5 to 1.5
- proj_weight: float32 [3072, 768], P('tensor', 'dp'), may hold values from -0.109375 to 0.109375
- proj_bias: float32 [768], replicated, may hold values from -1.5 to 1.5
Outputs:
- block_output: bfloat16 [8192, 768], P(('dp', 'tensor'))
- input_grad: bfloat16 [8192, 768], P(('dp', 'tensor'))
- ln1_gain_grad: float32 [768], replicated
- ln1_bias_grad: float32 [768], replicated
- qkv_weight_grad: float32 [768, 3, 768], P('dp', None, 'tensor')
- qv_bias_grad: float32 [2, 768], P(None, 'tensor')
- attn_out_weight_grad: float32 [768, 768], P('tensor', 'dp')
- attn_out_bias_grad: float32 [768], replicated
- ln2_gain_grad: float32 [768], replicated
- ln2_bias_grad: float32 [768], replicated
- fc_weight_grad: float32 [768, 3072], P('dp', 'tensor')
- fc_bias_grad: float32 [3072], P('tensor')
- proj_weight_grad: float32 [3072, 768], P('tensor', 'dp')
- proj_bias_grad: float32 [768], replicated
The draws below stay inside these ranges and needn't reach their ends.
Inputs may be any that keep to these rules, and one draw needn't show every extreme that they name: `seq_lengths`: each row gives the lengths of the 4 sequences of one pack in order, sums to 1024, and its largest entry is 682. `pack_order`: a permutation of the 8 packs.
All inputs are finite; a program needn't handle non-finite values.
Results may differ from the reference program's by a relative error of at most 0.017.
Values may be sent and summed in bfloat16 or wider, within the bound.
A program may use at most 128 MiB of HBM per device.

```python
import math
import jax
import jax.numpy as jnp
import numpy as np
from jax import lax

D = 768
HEADS = 12
FF = 3072
TOK_DEV = 1024
SEQS = 4
HEAD_DIM = 64
PACKS = 8
TOKENS = 8192
PIECE = 32
QBLOCK = 512


def spiked(entries, stream_key, source, target, shards_of, factor):
    owner, partner = [(jnp.arange(entries.shape[dim]) // (entries.shape[dim] // shards_of)).reshape([-1 if axis == dim else 1 for axis in range(entries.ndim)]) for dim in (source, target)]
    chosen = jax.random.permutation(stream_key, shards_of)[partner]
    strong = (owner == chosen) | (owner == (partner + shards_of // 2) % shards_of)
    return jnp.where(strong, factor * entries, entries)


def block_scale(stream_key, dims, shards, least, top_value):
    gain = 1.0
    for position, blocks in shards:
        heights = jax.random.uniform(jax.random.fold_in(jax.random.fold_in(stream_key, 6), position), (blocks,), jnp.float32, least / len(shards), top_value / len(shards))
        gain = gain * jnp.repeat(jnp.exp(heights), dims[position] // blocks).reshape((-1,) + (1,) * (len(dims) - 1 - position))
    return gain


def split_up(count, total, bound, skew):
    portions = [(1 << 20) // math.isqrt(standing ** skew) + 1 for standing in range(2, count + 1)]
    rest, counts = total - bound - (count - 1), [1] * (count - 1)
    while rest > 0:
        movable = [i for i in range(count - 1) if counts[i] < bound]
        mass, left = sum([portions[i] for i in movable]), rest
        for i in movable:
            extra = min(bound - counts[i], max(1, left * portions[i] // mass), rest)
            counts[i] = counts[i] + extra
            rest = rest - extra
    return np.array([bound] + counts)


def ragged_sizes(key, number_of, total, reach, skew):
    if number_of == 2:
        one = jax.random.randint(key, (), max(1, total - reach), min(reach, total - 1) + 1)
        return jnp.stack([one, total - one])
    tallies = jnp.asarray(split_up(number_of, total, reach, skew), jnp.int32)
    couples = (number_of - 1) // 2
    source_of, sink = tallies[1:1 + 2 * couples:2], tallies[2:2 + 2 * couples:2]
    slack = jnp.minimum(source_of - 1, reach - sink)
    passed = jax.random.randint(jax.random.fold_in(key, 1), (couples,), 0, 1 << 20) % (slack + 1)
    tallies = tallies.at[1:1 + 2 * couples:2].set(source_of - passed).at[2:2 + 2 * couples:2].set(sink + passed)
    return tallies[jax.random.permutation(jax.random.fold_in(key, 2), number_of)]


def normal_values(stream_key, dims, scale, limit, pieces=(), kind=jnp.bfloat16):
    array = scale * jax.random.normal(stream_key, dims, jnp.float32)
    if pieces:
        array = array * block_scale(stream_key, dims, pieces, -0.22, 0.18)
    return jnp.clip(array, -limit, limit).astype(kind)


def gaussian_with(key, dims, width, reach, split, heavy, held_as=jnp.bfloat16):
    result = width * jax.random.normal(key, dims, jnp.float32)
    if split:
        result = result * block_scale(key, dims, split, -0.22, 0.18)
    return jnp.clip(spiked(result, jax.random.fold_in(key, 3), *heavy), -reach, reach).astype(held_as)


def setup_inputs(seed: int = 0) -> dict:
    streams_of = jax.random.split(jax.random.key(seed), 17)
    block_input = normal_values(streams_of[0], (TOKENS, D), 1.0, 6.0, ((0, 32),))
    out_cotangent = gaussian_with(streams_of[1], (TOKENS, D), 1.0, 6.0, ((0, 32),), (0, 1, 32, 2.75))
    seq_lengths = jax.vmap(lambda own: ragged_sizes(own, SEQS, TOK_DEV, 2 * TOK_DEV // 3, 2))(jax.random.split(streams_of[2], PACKS)).reshape((PACKS, SEQS)).astype(jnp.int32)
    pack_order = jax.random.permutation(streams_of[3], PACKS).astype(jnp.int32)
    ln1_gain = jnp.clip(1.0 + 0.1 * jax.random.normal(streams_of[4], (D,), jnp.float32), 0.5, 1.5)
    ln1_bias = normal_values(streams_of[5], (D,), 0.3, 1.5, (), jnp.float32)
    qkv_weight = normal_values(streams_of[6], (D, 3, D), D ** -0.5, 0.21875, ((0, 8), (2, 4)), jnp.float32)
    qv_bias = normal_values(streams_of[7], (2, D), 0.3, 1.5, ((1, 4),), jnp.float32)
    attn_out_weight = normal_values(streams_of[8], (D, D), (D // 64) ** -0.5, 1.75, ((0, 4), (1, 8)), jnp.float32)
    attn_out_bias = normal_values(streams_of[9], (D,), 0.3, 1.5, (), jnp.float32)
    ln2_gain = jnp.clip(1.0 + 0.1 * jax.random.normal(streams_of[10], (D,), jnp.float32), 0.5, 1.5)
    ln2_bias = normal_values(streams_of[11], (D,), 0.3, 1.5, (), jnp.float32)
    fc_weight = normal_values(streams_of[12], (D, FF), D ** -0.5, 0.21875, ((0, 8), (1, 4)), jnp.float32)
    fc_bias = normal_values(streams_of[13], (FF,), 0.3, 1.5, ((0, 4),), jnp.float32)
    proj_weight = normal_values(streams_of[14], (FF, D), FF ** -0.5, 0.109375, ((0, 4), (1, 8)), jnp.float32)
    proj_bias = normal_values(streams_of[15], (D,), 0.3, 1.5, (), jnp.float32)
    return dict(block_input=block_input, out_cotangent=out_cotangent, seq_lengths=seq_lengths, pack_order=pack_order, ln1_gain=ln1_gain, ln1_bias=ln1_bias, qkv_weight=qkv_weight, qv_bias=qv_bias, attn_out_weight=attn_out_weight, attn_out_bias=attn_out_bias, ln2_gain=ln2_gain, ln2_bias=ln2_bias, fc_weight=fc_weight, fc_bias=fc_bias, proj_weight=proj_weight, proj_bias=proj_bias)


@jax.custom_vjp
def low(v):
    return lax.optimization_barrier(v.astype(jnp.bfloat16)).astype(jnp.float32)

@jax.custom_vjp
def low_back(v):
    return v

def low_keep(v):
    return (low(v), None)

def low_pass(kept, grad):
    return (grad,)

def back_keep(v):
    return (v, None)

def back_low(kept, grad):
    return (low(grad),)
low.defvjp(low_keep, low_pass)
low_back.defvjp(back_keep, back_low)
EPSILON = 1e-05
MASKED = -1e+30
PRECISE = lax.Precision.HIGHEST

def product(left_side, right_side):
    return jnp.dot(left_side, right_side, precision=PRECISE)

def layer_norm(values, norm_gain, norm_bias):
    row_mean = lax.optimization_barrier(jnp.mean(values, axis=-1, keepdims=True))
    row_var = lax.optimization_barrier(jnp.mean(values * values, axis=-1, keepdims=True)) - row_mean * row_mean
    return (values - row_mean) * lax.rsqrt(row_var + EPSILON) * norm_gain + norm_bias

def gelu_curve(values):
    return 0.5 * values * (1.0 + jnp.tanh(0.7978845608028654 * (values + 0.044715 * values * values * values)))

def attend_block(query_rows, keys_all, values_all, segment, begin_row):
    row_pos = begin_row + jnp.arange(QBLOCK, dtype=jnp.int32)
    col_pos = jnp.arange(TOK_DEV, dtype=jnp.int32)
    row_segment = lax.dynamic_slice_in_dim(segment, begin_row, QBLOCK)
    allowed = (col_pos[None, :] <= row_pos[:, None]) & (segment[None, :] == row_segment[:, None])
    raw_scores = jnp.einsum('qhd,khd->hqk', query_rows, keys_all, precision=PRECISE) * HEAD_DIM ** (-0.5)
    scores = jnp.where(allowed[None], low_back(raw_scores), MASKED)
    row_peak = lax.optimization_barrier(jnp.max(scores, axis=-1, keepdims=True))
    weights = jnp.exp(scores - row_peak)
    probs = low(weights / lax.optimization_barrier(jnp.sum(weights, axis=-1, keepdims=True)))
    return jnp.einsum('hqk,khd->qhd', probs, values_all, precision=PRECISE)

def attention(queries, keys_all, values_all, segment):
    head_queries = queries.reshape(TOK_DEV, HEADS, HEAD_DIM)
    head_keys = keys_all.reshape(TOK_DEV, HEADS, HEAD_DIM)
    head_values = values_all.reshape(TOK_DEV, HEADS, HEAD_DIM)

    def one_block(block_index):
        begin_row = block_index * QBLOCK
        query_rows = lax.dynamic_slice_in_dim(head_queries, begin_row, QBLOCK)
        return attend_block(query_rows, head_keys, head_values, segment, begin_row)
    outputs = lax.map(jax.checkpoint(one_block), jnp.arange(TOK_DEV // QBLOCK, dtype=jnp.int32))
    return outputs.reshape(TOK_DEV, D)

def pack_forward(params, packed_rows, segment):
    ln1_gain, ln1_bias, qkv_weight, qv_bias, attn_out_weight, attn_out_bias, ln2_gain, ln2_bias, fc_weight, fc_bias, proj_weight, proj_bias = params
    normed_one = low(layer_norm(packed_rows, ln1_gain, ln1_bias))
    queries = low_back(low(product(normed_one, low(qkv_weight[:, 0, :])) + qv_bias[0]))
    keys_all = low_back(low(product(normed_one, low(qkv_weight[:, 1, :]))))
    values_all = low_back(low(product(normed_one, low(qkv_weight[:, 2, :])) + qv_bias[1]))
    attended = low_back(low(attention(queries, keys_all, values_all, segment)))
    attn_branch = low_back(product(attended, low(attn_out_weight)))
    resid_one = packed_rows + attn_branch + attn_out_bias
    normed_two = low(layer_norm(resid_one, ln2_gain, ln2_bias))
    upper_pre = low_back(product(normed_two, low(fc_weight)) + fc_bias)
    activated = low(gelu_curve(upper_pre))
    mlp_branch = low_back(product(activated, low(proj_weight)))
    return resid_one + mlp_branch + proj_bias

def forward(params, tokens, segments, inverse, pack_order):
    groups = TOK_DEV // (PACKS * PIECE)
    arranged = tokens.reshape(PACKS, groups, PACKS, PIECE, D)
    packed = jnp.transpose(arranged[:, :, inverse], (2, 1, 0, 3, 4)).reshape(PACKS, TOK_DEV, D)

    def one_pack(inputs_pair):
        return pack_forward(params, inputs_pair[0], inputs_pair[1])
    results = lax.map(jax.checkpoint(one_pack), (packed, segments))
    spread = jnp.transpose(results.reshape(PACKS, groups, PACKS, PIECE, D), (2, 1, 0, 3, 4))
    return spread[:, :, pack_order].reshape(TOKENS, D)

def reference(block_input, out_cotangent, seq_lengths, pack_order, ln1_gain, ln1_bias, qkv_weight, qv_bias, attn_out_weight, attn_out_bias, ln2_gain, ln2_bias, fc_weight, fc_bias, proj_weight, proj_bias):
    inverse = jnp.argsort(pack_order).astype(jnp.int32)
    seq_ends = jnp.cumsum(seq_lengths, axis=1)
    positions = jnp.arange(TOK_DEV, dtype=jnp.int32)
    segments = lax.optimization_barrier(jnp.sum((positions[None, :, None] >= seq_ends[:, None, :]).astype(jnp.int32), axis=2)).astype(jnp.int32)
    params = (ln1_gain, ln1_bias, qkv_weight, qv_bias, attn_out_weight, attn_out_bias, ln2_gain, ln2_bias, fc_weight, fc_bias, proj_weight, proj_bias)
    tokens = block_input.astype(jnp.float32)

    def whole(param_tuple, token_rows):
        return forward(param_tuple, token_rows, segments, inverse, pack_order)
    output, pullback = jax.vjp(whole, params, tokens)
    param_grads, token_grad = pullback(out_cotangent.astype(jnp.float32))
    return (output.astype(jnp.bfloat16), token_grad.astype(jnp.bfloat16), param_grads[0], param_grads[1], param_grads[2], param_grads[3], param_grads[4], param_grads[5], param_grads[6], param_grads[7], param_grads[8], param_grads[9], param_grads[10], param_grads[11])
```

```python
import functools

import jax
import jax.numpy as jnp
from jax import lax
from jax.experimental import pallas as pl
from jax.experimental.pallas import tpu as pltpu
from jax.sharding import Mesh
from jax.sharding import PartitionSpec as P

HEAD_DIM = 64
EPSILON = 1e-05
MASKED = -1e30
BF = jnp.bfloat16
F32 = jnp.float32
MESH = pl.DeviceIdType.MESH
CURVE = 0.7978845608028654
CUBE = 0.044715

CHUNKS = 2
STEP = 32

QKV, OUT, FC, PROJ = "wqkv", "wo", "w1", "w2"
H1, GF, H2, DR = "h1", "gf", "h2", "dr"

NN = ((1,), (0,))
NT = ((1,), (1,))
TN = ((0,), (0,))


class Refs(dict):
    __getattr__ = dict.__getitem__


def dot(left_side, right_side, form):
    return lax.dot_general(
        left_side, right_side, (form, ((), ())), preferred_element_type=F32
    )


def kernel(cfg, *refs):
    (n, packs, L, S, D, HC, FH, inside) = cfg
    names = cfg_names(cfg)
    r = Refs(zip(names, refs))
    slabs, hslabs = (r.slab0, r.slab1), (r.hslab0, r.hslab1)
    backs = (r.back0, r.back1) if inside else None
    NH = HC // HEAD_DIM
    NZ = n // 2
    WR = D // n
    PR = L // n
    CR = L // CHUNKS
    B = L

    hi = lax.axis_index("hi")
    lo = lax.axis_index("lo")
    t = lax.axis_index("tensor")
    z, xx = hi // 2, hi % 2
    y, c = t // 2, t % 2
    dev = lambda h, tt: (h, lo, tt)
    mate = dev(hi, 2 * y + 1 - c)
    ynb = dev(hi, 2 * (1 - y) + c)
    ymate = dev(hi, 2 * (1 - y) + 1 - c)
    xnb = dev(2 * z + 1 - xx, t)

    def zdev(k):
        return dev(2 * ((z + k) % NZ) + xx, t)

    def block_of(k):
        return 2 * ((y + k // 2) % 2) + (c + k % 2) % 2

    def rows(start, size, mult=None):
        return pl.ds(pl.multiple_of(start, mult or size), size)

    def block_rows(k):
        return rows(block_of(k) * B, B)

    def rcopy(src, dst, send, recv, target):
        return pltpu.make_async_remote_copy(
            src_ref=src,
            dst_ref=dst,
            send_sem=send,
            recv_sem=recv,
            device_id=target,
            device_id_type=MESH,
        )

    barrier = pltpu.get_barrier_semaphore()
    peers = [dev((hi + k) % n, t) for k in range(1, n)] + [mate, ynb, ymate]
    for peer in peers:
        pl.semaphore_signal(barrier, inc=1, device_id=peer, device_id_type=MESH)

    def a2a(tag, k, source, target):
        sem = r.a2a_sem
        to = (hi + k) % n
        return rcopy(source(to), target(hi), sem.at[0, tag, k - 1], sem.at[1, tag, k - 1], dev(to, t))

    def a2a_in_copy(tag, k):
        return a2a(
            tag,
            k,
            lambda to: r.sent.at[tag, to],
            lambda me: r.came.at[tag, rows(me * PR, PR)],
        )

    def a2a_out_copy(tag, k):
        return a2a(
            2 + tag,
            k,
            lambda to: r.made.at[tag, rows(to * PR, PR)],
            lambda me: backs[tag].at[me],
        )

    def pick_pieces(tag, source):
        def one(k, _):
            where = jnp.int32(0)
            for j in range(n):
                where = jnp.where(r.order[j] == k, j, where)
            r.sent[tag, k] = source[where]
            return 0

        lax.fori_loop(0, n, one, 0)
        r.came[tag, rows(hi * PR, PR)] = r.sent[tag, hi]

    if inside:
        pick_pieces(0, r.x)
    pl.semaphore_wait(barrier, len(peers))
    if inside:
        for k in range(1, n):
            a2a_in_copy(0, k).start()
        pick_pieces(1, r.g)
    else:
        r.came[0] = r.x[...]
        r.came[1] = r.g[...]

    WG = (QKV, OUT, FC, PROJ)

    def wslot(name, ref, slot):
        where = rows(slot * WR, WR, 16)
        return ref.at[:, where] if name == QKV else ref.at[where]

    def wg_z(name, k):
        sem = r.wg_sem
        a = WG.index(name)
        own = wslot(name, r[name], hi)
        return rcopy(own, own, sem.at[0, a, k], sem.at[1, a, k], zdev(k))

    def wg_x(name, k):
        sem = r.wg_sem
        a = WG.index(name)
        slot = wslot(name, r[name], 2 * ((z - k + NZ) % NZ) + xx)
        return rcopy(slot, slot, sem.at[0, a, NZ + k], sem.at[1, a, NZ + k], xnb)

    def wg_start(name):
        for k in range(1, NZ):
            wg_z(name, k).start()
        wg_x(name, 0).start()

    def wg_forward(name):
        for k in range(1, NZ):
            wg_z(name, k).wait_recv()
            wg_x(name, k).start()

    def wg_wait(name):
        for k in range(NZ):
            wg_x(name, k).wait_recv()

    def wg_drain(name):
        for k in range(1, NZ):
            wg_z(name, k).wait_send()
        for k in range(NZ):
            wg_x(name, k).wait_send()

    own_w = rows(hi * WR, WR, 16)
    for i in range(3):
        r.wqkv[i, own_w] = r.qkv_in[:, i, :].astype(BF)
    r.w1[own_w] = r.fc_in[...].astype(BF)
    r.turn[...] = jnp.zeros_like(r.turn)
    r.turn[:, :WR] = r.proj_in[...].astype(F32)
    for i in range(FH // 256):
        r.w2[own_w, i * 256 : (i + 1) * 256] = r.turn[i * 256 : (i + 1) * 256].T[:WR].astype(BF)
    r.turn[:HC, :WR] = r.out_in[...].astype(F32)
    r.wo[own_w] = r.turn[:256].T[:WR, :HC].astype(BF)

    AG = (H1, GF, H2, DR)

    def ag(name, kind, ch):
        sem = r.ag_sem
        a = AG.index(name)
        full = r[name]
        if kind == 2:
            where = rows(block_of(2) * B + ch * CR, CR)
        else:
            where = rows(t * B + ch * CR, CR)
        target = ynb if kind == 0 else mate
        part = full.at[where]
        return rcopy(part, part, sem.at[0, a, kind, ch], sem.at[1, a, kind, ch], target)

    def ag_send(name, ch):
        ag(name, 0, ch).start()
        ag(name, 1, ch).start()

    def ag_forward(name, ch):
        ag(name, 0, ch).wait_recv()
        ag(name, 2, ch).start()

    def ag_arrive(name, k):
        for ch in range(CHUNKS):
            if k == 1:
                ag(name, 1, ch).wait_recv()
            elif k == 2:
                ag_forward(name, ch)
            else:
                ag(name, 2, ch).wait_recv()

    def ag_drain(name):
        for kind in range(3):
            for ch in range(CHUNKS):
                ag(name, kind, ch).wait_send()

    def rs_bufs(tag):
        if tag == 3:
            return r.msy, r.mry, r.keepy, r.ysy, r.yry
        return r.msc, r.mrc, r.keepc, r.ysc, r.yrc

    def rs_m(tag, i):
        ms, mr, _, _, _ = rs_bufs(tag)
        sem = r.rs_sem
        return rcopy(ms.at[i], mr.at[i], sem.at[0, tag, i], sem.at[1, tag, i], mate)

    def rs_y(tag, ch):
        _, _, _, ys, yr = rs_bufs(tag)
        sem = r.rs_sem
        where = pl.ds(ch * CR, CR)
        return rcopy(ys.at[where], yr.at[where], sem.at[0, tag, 2 + ch], sem.at[1, tag, 2 + ch], ynb)

    def rs_put(tag, k, value, at=None):
        ms, _, keep, _, _ = rs_bufs(tag)
        where = slice(None) if at is None else at
        i = 0 if k >= 2 else 1
        if k % 2:
            ms[i, where] = value.astype(BF)
        else:
            keep[i, where] = value

    def rs_ship(tag):
        _, mr, keep, ys, _ = rs_bufs(tag)
        rs_m(tag, 0).wait_recv()
        for ch in range(CHUNKS):

            def one(s, _):
                at = rows(ch * CR + s * STEP, STEP)
                ys[at] = (keep[0, at] + mr[0, at].astype(F32)).astype(BF)
                return 0

            lax.fori_loop(0, CR // STEP, one, 0)
            rs_y(tag, ch).start()

    def rs_total(tag, at):
        _, mr, keep, _, yr = rs_bufs(tag)
        return keep[1, at] + mr[1, at].astype(F32) + yr[at].astype(F32)

    def rs_drain(tag):
        for i in range(2):
            rs_m(tag, i).wait_send()
        for ch in range(CHUNKS):
            rs_y(tag, ch).wait_send()

    GR = {name: "g" + name for name in WG}

    def gr_x(name, k):
        sem = r.gr_sem
        a = WG.index(name)
        slot = wslot(name, r[GR[name]], 2 * k + 1 - xx)
        return rcopy(slot, r[name + "_xr"].at[k], sem.at[0, a, k], sem.at[1, a, k], xnb)

    def gr_z(name, k):
        sem = r.gr_sem
        a = WG.index(name)
        return rcopy(
            r[name + "_zs"].at[k - 1],
            r[name + "_zr"].at[k - 1],
            sem.at[0, a, NZ + k],
            sem.at[1, a, NZ + k],
            zdev(k),
        )

    def gr_start(name):
        for k in range(NZ):
            gr_x(name, k).start()

    def gr_mid(name):
        for k in range(NZ):
            gr_x(name, k).wait_recv()
        for k in range(1, NZ):
            to = (z + k) % NZ
            mine = wslot(name, r[GR[name]], 2 * to + xx)[...].astype(F32)
            r[name + "_zs"][k - 1] = (mine + r[name + "_xr"][to].astype(F32)).astype(BF)
            gr_z(name, k).start()

    def gr_finish(name):
        total = wslot(name, r[GR[name]], hi)[...].astype(F32) + r[name + "_xr"][z].astype(F32)
        for k in range(1, NZ):
            gr_z(name, k).wait_recv()
            total = total + r[name + "_zr"][k - 1].astype(F32)
        return total

    def gr_drain(name):
        for k in range(NZ):
            gr_x(name, k).wait_send()
        for k in range(1, NZ):
            gr_z(name, k).wait_send()

    tpeers = [mate, ynb, ymate]
    SHARED = (24, 16)

    def sm_t(tag, i):
        sem = r.sm_sem
        part = slabs[tag].at[t]
        return rcopy(part, part, sem.at[0, tag, i], sem.at[1, tag, i], tpeers[i])

    def sm_h(tag, k):
        sem = r.sm_sem
        part = hslabs[tag].at[hi]
        return rcopy(part, part, sem.at[0, tag, 3 + k], sem.at[1, tag, 3 + k], dev((hi + k) % n, t))

    def spread(tag, at, value):
        for j in range(value.shape[1] // 128):
            slabs[tag][t, at + j : at + j + 1] = value[:, j * 128 : (j + 1) * 128]

    def sm_start(tag):
        for i in range(3):
            sm_t(tag, i).start()

    def sm_mid(tag):
        for i in range(3):
            sm_t(tag, i).wait_recv()
        slab, hslab = slabs[tag], hslabs[tag]
        total = slab[0]
        for i in range(1, 4):
            total = total + slab[i]
        if tag == 0:
            keep = lax.broadcasted_iota(jnp.int32, total.shape, 0) < SHARED[0]
            total = jnp.where(keep, total, slab[t])
        hslab[hi] = total
        for k in range(1, n):
            sm_h(tag, k).start()

    def sm_finish(tag):
        for k in range(1, n):
            sm_h(tag, k).wait_recv()
        hslab = hslabs[tag]
        total = hslab[0]
        for k in range(1, n):
            total = total + hslab[k]
        return total

    def sm_drain(tag):
        for i in range(3):
            sm_t(tag, i).wait_send()
        for k in range(1, n):
            sm_h(tag, k).wait_send()

    def fold(value):
        return jnp.sum(value.reshape(value.shape[0] // 8, 8, value.shape[1]), axis=0)

    for slab in slabs:
        slab[t] = jnp.zeros(slab.shape[1:], F32)
    r.acc[...] = jnp.zeros_like(r.acc)
    r.acc_f[...] = jnp.zeros_like(r.acc_f)
    r.acc_h[...] = jnp.zeros_like(r.acc_h)

    if inside:
        for k in range(1, n):
            a2a_in_copy(0, k).wait_recv()
    wg_start(QKV)

    def norm_step(values, at, gain, bias, cen, scale):
        mean = jnp.mean(values, axis=1, keepdims=True)
        var = jnp.mean(values * values, axis=1, keepdims=True) - mean * mean
        inv = lax.rsqrt(var + EPSILON)
        centered = (values - mean) * inv
        cen[at] = centered
        scale[at] = inv
        return (centered * gain + bias).astype(BF)

    def norm_back(grad, at, gain, cen, scale, acc_at):
        centered = cen[at]
        r.acc[acc_at] += fold(grad * centered)
        r.acc[acc_at + 1] += fold(grad)
        scaled = grad * gain
        return scale[at] * (
            scaled
            - jnp.mean(scaled, axis=1, keepdims=True)
            - centered * jnp.mean(scaled * centered, axis=1, keepdims=True)
        )

    for ch in range(CHUNKS):

        def one(s, _):
            at = rows(ch * CR + s * STEP, STEP)
            values = r.came[0, at].astype(F32)
            r.h1[rows(t * B + ch * CR + s * STEP, STEP)] = norm_step(
                values, at, r.ln1g[...], r.ln1b[...], r.cen1, r.scale1
            )
            return 0

        lax.fori_loop(0, CR // STEP, one, 0)
        ag_send(H1, ch)

    if inside:
        for k in range(1, n):
            a2a_in_copy(1, k).start()
    wg_forward(QKV)
    wg_start(OUT)
    wg_start(FC)
    wg_wait(QKV)

    lane = lax.broadcasted_iota(jnp.int32, (1, HC), 1)

    def head_mask(h):
        return (lane >= h * HEAD_DIM) & (lane < (h + 1) * HEAD_DIM)

    def project(s, _):
        @pl.when(s == 1)
        def _():
            ag_arrive(H1, 1)

        @pl.when(s == 2)
        def _():
            ag_arrive(H1, 2)

        @pl.when(s == 3)
        def _():
            ag_arrive(H1, 3)

        b = block_of(s)
        at = rows(b * B, B)
        hidden = r.h1[at]
        q = dot(hidden, r.wqkv[0], NN) + r.qvb[0:1]
        q = (q.astype(BF).astype(F32) * HEAD_DIM ** (-0.5)).astype(BF)
        for h in range(NH):
            r.qm[b, h * B : (h + 1) * B] = jnp.where(head_mask(h), q, jnp.zeros_like(q))
        k = dot(hidden, r.wqkv[1], NN)
        r.k[at] = k.astype(BF)
        r.kt[:, at] = k.T.astype(BF)
        v = dot(hidden, r.wqkv[2], NN) + r.qvb[1:2]
        r.v[at] = v.astype(BF)
        r.vt[:, at] = v.T.astype(BF)
        return 0

    lax.fori_loop(0, 4, project, 0)

    if inside:
        for k in range(1, n):
            a2a_in_copy(1, k).wait_recv()

    def own_grad(s, _):
        at = rows(s * STEP, STEP)
        value = r.came[1, at]
        r.gf[rows(t * B + s * STEP, STEP)] = value
        r.acc[5] += fold(value.astype(F32))
        return 0

    lax.fori_loop(0, B // STEP, own_grad, 0)
    for ch in range(CHUNKS):
        ag_send(GF, ch)
    wg_forward(OUT)
    wg_start(PROJ)

    pack = hi * (packs // n) + lo

    def attend(i):
        pos = i * B + lax.broadcasted_iota(jnp.int32, (1, B), 1)
        first = jnp.zeros((1, B), jnp.int32)
        end = jnp.int32(0)
        for s in range(r.lengths.shape[1]):
            length = r.lengths[pack, s]
            end = end + length
            first = first + jnp.where(pos >= end, length, 0)

        def scores(j, peak):
            key_pos = j * B + lax.broadcasted_iota(jnp.int32, (B, B), 0)
            allowed = (key_pos >= first) & (key_pos <= pos)
            keys = r.k[rows(j * B, B)]
            peaks = []
            for h in range(NH):
                raw = dot(keys, r.qm[i, h * B : (h + 1) * B], NT)
                raw = jnp.where(allowed, raw, MASKED)
                r.score[j, :, h * B : (h + 1) * B] = raw
                peaks.append(jnp.max(raw, axis=0, keepdims=True))
            return jnp.maximum(peak, jnp.concatenate(peaks, axis=1))

        peak = lax.fori_loop(0, i + 1, scores, jnp.full((1, NH * B), MASKED, F32))
        r.att[...] = jnp.zeros_like(r.att)

        def weigh(j, total):
            totals = []
            for h in range(NH):
                cols = slice(h * B, (h + 1) * B)
                weight = jnp.exp(r.score[j, :, cols] - peak[:, cols])
                totals.append(jnp.sum(weight, axis=0, keepdims=True))
                low = weight.astype(BF)
                r.e[i, j, :, cols] = low
                part = slice(h * HEAD_DIM, (h + 1) * HEAD_DIM)
                r.att[part] += dot(r.vt[part, rows(j * B, B)], low, NN)
            return total + jnp.concatenate(totals, axis=1)

        total = lax.fori_loop(0, i + 1, weigh, jnp.zeros((1, NH * B), F32))
        inverse = 1.0 / total
        for h in range(NH):
            part = slice(h * HEAD_DIM, (h + 1) * HEAD_DIM)
            own = inverse[:, h * B : (h + 1) * B]
            r.att[part] = r.att[part] * own
            r.inv[i, h : h + 1] = own
        out = r.att[...].T
        at = rows(i * B, B)
        r.a[at] = out
        r.al[at] = out.astype(BF)

    def attend_step(s, _):
        k = 3 - s
        i = block_of(k)
        attend(i)

        @pl.when(s == 0)
        def _():
            wg_wait(OUT)

        part = dot(r.al[rows(i * B, B)], r.wo[...], NT)

        @pl.when(s == 0)
        def _():
            rs_put(0, 3, part)
            rs_m(0, 0).start()

        @pl.when(s == 1)
        def _():
            rs_put(0, 2, part)
            rs_ship(0)

        @pl.when(s == 2)
        def _():
            rs_put(0, 1, part)
            rs_m(0, 1).start()

        @pl.when(s == 3)
        def _():
            rs_put(0, 0, part)

        return 0

    lax.fori_loop(0, 4, attend_step, 0)
    wg_forward(FC)

    rs_m(0, 1).wait_recv()
    for ch in range(CHUNKS):
        rs_y(0, ch).wait_recv()

        def one(s, _):
            at = rows(ch * CR + s * STEP, STEP)
            values = r.came[0, at].astype(F32) + rs_total(0, at) + r.aob[...]
            r.res[at] = values
            r.h2[rows(t * B + ch * CR + s * STEP, STEP)] = norm_step(
                values, at, r.ln2g[...], r.ln2b[...], r.cen2, r.scale2
            )
            return 0

        lax.fori_loop(0, CR // STEP, one, 0)
        ag_send(H2, ch)
    rs_drain(0)
    ag_arrive(GF, 1)
    ag_arrive(GF, 2)
    wg_forward(PROJ)
    ag_arrive(GF, 3)
    wg_wait(FC)
    wg_wait(PROJ)

    def feed(s, _):
        @pl.when(s == 1)
        def _():
            ag_arrive(H2, 1)

        @pl.when(s == 2)
        def _():
            ag_arrive(H2, 2)

        @pl.when(s == 3)
        def _():
            ag_arrive(H2, 3)

        at = block_rows(s)
        hidden = r.h2[at]
        grad = r.gf[at]
        for j in range(FH // 256):
            cols = slice(j * 256, (j + 1) * 256)
            u = dot(hidden, r.w1[:, cols], NN) + r.fcb[:, cols]
            dz = dot(grad, r.w2[:, cols], NN)
            square = u * u
            half = 0.5 + 0.5 * jnp.tanh(u * (CURVE + (CURVE * CUBE) * square))
            act = u * half
            r.zz[at, cols] = act.astype(BF)
            slope = half + act * (1.0 - half) * (2.0 * CURVE + (6.0 * CURVE * CUBE) * square)
            low = (dz * slope).astype(BF)
            r.du[at, cols] = low
            r.acc_f[:, cols] += fold(low.astype(F32))
        part = dot(r.du[at], r.w1[...], NT)

        @pl.when(s == 0)
        def _():
            rs_put(1, 0, part)

        @pl.when(s == 1)
        def _():
            rs_put(1, 1, part)
            rs_m(1, 1).start()

        @pl.when(s == 2)
        def _():
            rs_put(1, 2, part)

        @pl.when(s == 3)
        def _():
            rs_put(1, 3, part)
            rs_m(1, 0).start()

        return 0

    lax.fori_loop(0, 4, feed, 0)
    rs_ship(1)

    def grad_tiles(left, right, out, form=TN):
        def one(i, _):
            at = rows(i * 256, 256)
            out[at] = dot(left[:, at], right[...], form).astype(BF)
            return 0

        lax.fori_loop(0, D // 256, one, 0)

    grad_tiles(r.gf, r.zz, r.gw2)
    gr_start(PROJ)
    grad_tiles(r.h2, r.du, r.gw1)
    gr_start(FC)

    rs_m(1, 1).wait_recv()
    for ch in range(CHUNKS):
        rs_y(1, ch).wait_recv()

        def one(s, _):
            at = rows(ch * CR + s * STEP, STEP)
            back = norm_back(rs_total(1, at), at, r.ln2g[...], r.cen2, r.scale2, 2)
            grad = r.came[1, at].astype(F32) + back
            r.dres[at] = grad
            r.acc[4] += fold(grad)
            r.dr[rows(t * B + ch * CR + s * STEP, STEP)] = grad.astype(BF)
            return 0

        lax.fori_loop(0, CR // STEP, one, 0)
        ag_send(DR, ch)
    rs_drain(1)

    def upper(s, _):
        k = 3 - s
        part = dot(r.zz[block_rows(k)], r.w2[...], NT)

        @pl.when(s == 0)
        def _():
            rs_put(3, 3, part)
            rs_m(3, 0).start()

        @pl.when(s == 1)
        def _():
            rs_put(3, 2, part)

        @pl.when(s == 2)
        def _():
            rs_put(3, 1, part)
            rs_m(3, 1).start()

        @pl.when(s == 3)
        def _():
            rs_put(3, 0, part)

        return 0

    lax.fori_loop(0, 4, upper, 0)
    gr_mid(PROJ)
    gr_mid(FC)

    r.dk[...] = jnp.zeros_like(r.dk)
    r.dv[...] = jnp.zeros_like(r.dv)

    def attend_back(s, _):
        @pl.when(s == 1)
        def _():
            ag_arrive(DR, 1)

        @pl.when(s == 2)
        def _():
            ag_arrive(DR, 2)
            rs_ship(3)

        @pl.when(s == 3)
        def _():
            ag_arrive(DR, 3)

        i = block_of(s)
        at = rows(i * B, B)
        da = dot(r.dr[at], r.wo[...], NN).astype(BF).astype(F32)
        by_row = r.inv[i].T
        scale = by_row[:, NH - 1 : NH]
        for h in range(NH - 1):
            scale = jnp.where(head_mask(h), by_row[:, h : h + 1], scale)
        low = (da * scale).astype(BF)
        for h in range(NH):
            r.dam[h * B : (h + 1) * B] = jnp.where(head_mask(h), low, jnp.zeros_like(low))
        lined = (low.astype(F32) * r.a[at]).T
        deltas = [
            jnp.sum(lined[h * HEAD_DIM : (h + 1) * HEAD_DIM], axis=0, keepdims=True)
            for h in range(NH)
        ]
        r.att[...] = jnp.zeros_like(r.att)

        def over_keys(j, _):
            kr = rows(j * B, B)
            values = r.v[kr]
            for h in range(NH):
                cols = slice(h * B, (h + 1) * B)
                dp = dot(values, r.dam[cols], NT)
                ds = (r.e[i, j, :, cols].astype(F32) * (dp - deltas[h])).astype(BF)
                r.ds[:, cols] = ds
                part = slice(h * HEAD_DIM, (h + 1) * HEAD_DIM)
                r.att[part] += dot(r.kt[part, kr], ds, NN)
            r.dk[kr] += dot(r.ds[...], r.qm[i], NN)
            r.dv[kr] += dot(r.e[i, j], r.dam[...], NN)
            return 0

        lax.fori_loop(0, i + 1, over_keys, 0)
        dq = (r.att[...].T * HEAD_DIM ** (-0.5)).astype(BF)
        r.dqkv[0, at] = dq
        return 0

    lax.fori_loop(0, 4, attend_back, 0)

    def round_kv(b, _):
        at = rows(b * B, B)
        dv = r.dv[at].astype(BF)
        r.dqkv[1, at] = r.dk[at].astype(BF)
        r.dqkv[2, at] = dv
        r.acc_h[0] += fold(r.dqkv[0, at].astype(F32))
        r.acc_h[1] += fold(dv.astype(F32))
        return 0

    lax.fori_loop(0, 4, round_kv, 0)

    def lower(s, _):
        k = 3 - s
        at = block_rows(k)
        part = dot(r.dqkv[0, at], r.wqkv[0], NT)
        part = part + dot(r.dqkv[1, at], r.wqkv[1], NT)
        part = part + dot(r.dqkv[2, at], r.wqkv[2], NT)

        @pl.when(s == 0)
        def _():
            rs_put(2, 3, part)
            rs_m(2, 0).start()

        @pl.when(s == 1)
        def _():
            rs_put(2, 2, part)
            rs_ship(2)

        @pl.when(s == 2)
        def _():
            rs_put(2, 1, part)
            rs_m(2, 1).start()

        @pl.when(s == 3)
        def _():
            rs_put(2, 0, part)

        return 0

    lax.fori_loop(0, 4, lower, 0)

    def grad_qkv(i, _):
        at = rows(i * 256, 256)
        left = r.h1[:, at]
        for j in range(3):
            r.gwqkv[j, at] = dot(left, r.dqkv[j], TN).astype(BF)
        return 0

    lax.fori_loop(0, D // 256, grad_qkv, 0)
    gr_start(QKV)
    grad_tiles(r.dr, r.al, r.gwo)
    gr_start(OUT)

    rs_m(3, 1).wait_recv()
    for ch in range(CHUNKS):
        rs_y(3, ch).wait_recv()

    def finish_up(s, _):
        at = rows(s * STEP, STEP)
        r.made[0, at] = (r.res[at] + rs_total(3, at) + r.pjb[...]).astype(BF)
        return 0

    lax.fori_loop(0, B // STEP, finish_up, 0)
    if inside:
        for k in range(1, n):
            a2a_out_copy(0, k).start()
        r.back0[hi] = r.made[0, rows(hi * PR, PR)]
    else:
        r.out_y[...] = r.made[0]

    def line(value):
        return jnp.sum(value, axis=0, keepdims=True)

    for j, at in enumerate((5, 2, 3, 4)):
        spread(0, 6 * j, line(r.acc[at]))
    spread(0, 24, line(r.acc_f[...]))
    pad = jnp.zeros((1, 256 - HC), F32)
    for j in range(2):
        spread(0, 30 + 2 * j, jnp.concatenate([line(r.acc_h[j]), pad], axis=1))
    sm_start(0)

    rs_m(2, 1).wait_recv()
    for ch in range(CHUNKS):
        rs_y(2, ch).wait_recv()

        def one(s, _):
            at = rows(ch * CR + s * STEP, STEP)
            back = norm_back(rs_total(2, at), at, r.ln1g[...], r.cen1, r.scale1, 0)
            r.made[1, at] = (r.dres[at] + back).astype(BF)
            return 0

        lax.fori_loop(0, CR // STEP, one, 0)
    rs_drain(2)
    rs_drain(3)
    if inside:
        for k in range(1, n):
            a2a_out_copy(1, k).start()
        r.back1[hi] = r.made[1, rows(hi * PR, PR)]
    else:
        r.out_x[...] = r.made[1]
    for j in range(2):
        spread(1, 6 * j, line(r.acc[j]))
    sm_start(1)
    sm_mid(0)
    gr_mid(QKV)
    gr_mid(OUT)
    sm_mid(1)

    r.out_w2[...] = gr_finish(PROJ)
    r.out_w1[...] = gr_finish(FC)

    def put_back(tag, out):
        for k in range(1, n):
            a2a_out_copy(tag, k).wait_recv()

        def one(j, _):
            out[j] = backs[tag][r.order[j]]
            return 0

        lax.fori_loop(0, n, one, 0)

    if inside:
        put_back(0, r.out_y)
    r.out_early[...] = sm_finish(0)
    r.out_qkv[...] = gr_finish(QKV)
    r.out_wo[...] = gr_finish(OUT)
    r.out_late[...] = sm_finish(1)
    if inside:
        put_back(1, r.out_x)

    for name in WG:
        wg_drain(name)
        gr_drain(name)
    for name in AG:
        ag_drain(name)
    for tag in range(2):
        sm_drain(tag)
        if inside:
            for k in range(1, n):
                a2a_in_copy(tag, k).wait_send()
                a2a_out_copy(tag, k).wait_send()


def inputs():
    vmem = pl.BlockSpec(memory_space=pltpu.VMEM)
    smem = pl.BlockSpec(memory_space=pltpu.SMEM)
    return Refs(
        order=smem,
        lengths=smem,
        x=vmem,
        g=vmem,
        ln1g=vmem,
        ln1b=vmem,
        qkv_in=vmem,
        qvb=vmem,
        out_in=vmem,
        aob=vmem,
        ln2g=vmem,
        ln2b=vmem,
        fc_in=vmem,
        fcb=vmem,
        proj_in=vmem,
        pjb=vmem,
    )


def outputs(cfg):
    (n, packs, L, S, D, HC, FH, inside) = cfg
    WR = D // n
    tokens = (n, L // n, D) if inside else (L, D)
    return Refs(
        out_y=(tokens, BF),
        out_x=(tokens, BF),
        out_qkv=((3, WR, HC), F32),
        out_wo=((WR, HC), F32),
        out_w1=((WR, FH), F32),
        out_w2=((WR, FH), F32),
        out_early=((40, 128), F32),
        out_late=((16, 128), F32),
    )


def scratch(cfg):
    (n, packs, L, S, D, HC, FH, inside) = cfg
    NH = HC // HEAD_DIM
    NZ = n // 2
    WR = D // n
    V = pltpu.VMEM
    sem = pltpu.SemaphoreType.DMA
    blocks = S // L
    made = Refs(
        came=V((2, L, D), BF),
        made=V((2, L, D), BF),
        wqkv=V((3, D, HC), BF),
        wo=V((D, HC), BF),
        w1=V((D, FH), BF),
        w2=V((D, FH), BF),
        turn=V((FH, 128), F32),
        h1=V((S, D), BF),
        gf=V((S, D), BF),
        h2=V((S, D), BF),
        dr=V((S, D), BF),
        cen1=V((L, D), F32),
        cen2=V((L, D), F32),
        scale1=V((L, 1), F32),
        scale2=V((L, 1), F32),
        res=V((L, D), F32),
        dres=V((L, D), F32),
        qm=V((blocks, NH * L, HC), BF),
        k=V((S, HC), BF),
        v=V((S, HC), BF),
        kt=V((HC, S), BF),
        vt=V((HC, S), BF),
        score=V((blocks, L, NH * L), F32),
        e=V((blocks, blocks, L, NH * L), BF),
        att=V((HC, L), F32),
        inv=V((blocks, 8, L), F32),
        a=V((S, HC), F32),
        al=V((S, HC), BF),
        dam=V((NH * L, HC), BF),
        ds=V((L, NH * L), BF),
        dk=V((S, HC), F32),
        dv=V((S, HC), F32),
        dqkv=V((3, S, HC), BF),
        zz=V((S, FH), BF),
        du=V((S, FH), BF),
        acc=V((6, 8, D), F32),
        acc_f=V((8, FH), F32),
        acc_h=V((2, 8, HC), F32),
        slab0=V((4, 40, 128), F32),
        slab1=V((4, 16, 128), F32),
        hslab0=V((n, 40, 128), F32),
        hslab1=V((n, 16, 128), F32),
    )
    if inside:
        made.update(
            sent=V((2, n, L // n, D), BF),
            back0=V((n, L // n, D), BF),
            back1=V((n, L // n, D), BF),
            a2a_sem=sem((2, 4, n - 1)),
        )
    for late in "cy":
        made["ms" + late] = V((2, L, D), BF)
        made["mr" + late] = V((2, L, D), BF)
        made["keep" + late] = V((2, L, D), F32)
        made["ys" + late] = V((L, D), BF)
        made["yr" + late] = V((L, D), BF)
    for name, slot in ((QKV, (3, WR, HC)), (OUT, (WR, HC)), (FC, (WR, FH)), (PROJ, (WR, FH))):
        made["g" + name] = V(slot[:-2] + (D, slot[-1]), BF)
        made[name + "_xr"] = V((NZ,) + slot, BF)
        made[name + "_zs"] = V((NZ - 1,) + slot, BF)
        made[name + "_zr"] = V((NZ - 1,) + slot, BF)
    made.update(
        wg_sem=sem((2, 4, 2 * NZ)),
        gr_sem=sem((2, 4, 2 * NZ)),
        ag_sem=sem((2, 4, 3, CHUNKS)),
        rs_sem=sem((2, 4, 2 + CHUNKS)),
        sm_sem=sem((2, 2, 3 + n)),
    )
    return made


def cfg_names(cfg):
    return tuple(inputs()) + tuple(outputs(cfg)) + tuple(scratch(cfg))


def local(
    n,
    block_input,
    out_cotangent,
    seq_lengths,
    pack_order,
    ln1_gain,
    ln1_bias,
    qkv_weight,
    qv_bias,
    attn_out_weight,
    attn_out_bias,
    ln2_gain,
    ln2_bias,
    fc_weight,
    fc_bias,
    proj_weight,
    proj_bias,
):
    L, D = block_input.shape
    packs = pack_order.shape[0]
    HC = qv_bias.shape[1]
    FH = fc_bias.shape[0]
    S = L * lax.axis_size("tensor")
    outer = packs // n
    inside = outer == 1
    cfg = (n, packs, L, S, D, HC, FH, inside)
    tokens = (block_input, out_cotangent)
    weights = (qkv_weight, attn_out_weight, fc_weight, proj_weight)
    if inside:
        tokens = [v.reshape(n, L // n, D) for v in tokens]
    else:
        slots = jnp.arange(packs, dtype=jnp.int32)
        chosen = (pack_order[None, :] == slots[:, None]).astype(BF)

        def pick(which, v):
            return (
                jnp.dot(which, v.reshape(packs, -1), preferred_element_type=F32)
                .astype(BF)
                .reshape(L, D)
            )

        tokens = [
            lax.all_to_all(
                pick(chosen, v), ("hi", "lo"), split_axis=0, concat_axis=0, tiled=True
            )
            for v in tokens
        ]
        weights = [
            lax.all_gather(w.astype(BF), "lo", axis=axis, tiled=True)
            for w, axis in zip(weights, (0, 1, 0, 1))
        ]
    row = lambda v: v.reshape(1, -1)
    outs = outputs(cfg)
    made = pl.pallas_call(
        functools.partial(kernel, cfg),
        out_shape=[jax.ShapeDtypeStruct(shape, kind) for shape, kind in outs.values()],
        in_specs=list(inputs().values()),
        out_specs=[pl.BlockSpec(memory_space=pltpu.VMEM)] * len(outs),
        scratch_shapes=list(scratch(cfg).values()),
        compiler_params=pltpu.CompilerParams(
            collective_id=0, has_side_effects=True, vmem_limit_bytes=63 * 2**20
        ),
    )(
        pack_order,
        seq_lengths,
        *tokens,
        row(ln1_gain),
        row(ln1_bias),
        weights[0],
        qv_bias,
        weights[1],
        row(attn_out_bias),
        row(ln2_gain),
        row(ln2_bias),
        weights[2],
        row(fc_bias),
        weights[3],
        row(proj_bias),
    )
    g = Refs(zip(outs, made))
    out_y, out_x = g.out_y, g.out_x
    qkv_sum = jnp.transpose(g.out_qkv, (1, 0, 2))
    out_sum = g.out_wo.T
    fc_sum = g.out_w1
    proj_sum = g.out_w2.T
    early, late = g.out_early, g.out_late
    if inside:
        out_y, out_x = out_y.reshape(L, D), out_x.reshape(L, D)
    else:
        out_y, out_x = [
            pick(
                chosen.T,
                lax.all_to_all(v, ("hi", "lo"), split_axis=0, concat_axis=0, tiled=True),
            )
            for v in (out_y, out_x)
        ]
        qkv_sum, out_sum, fc_sum, proj_sum = [
            lax.psum_scatter(w, "lo", scatter_dimension=axis, tiled=True)
            for w, axis in ((qkv_sum, 0), (out_sum, 1), (fc_sum, 0), (proj_sum, 1))
        ]
        early, late = lax.psum((early, late), "lo")
    vec = D // 128
    shared = [early[j * vec : (j + 1) * vec].reshape(D) for j in range(4)]
    fc_bias_sum = early[4 * vec : 4 * vec + FH // 128].reshape(FH)
    head = 4 * vec + FH // 128
    qv_sum = early[head : head + 4].reshape(2, 256)[:, :HC]
    return (
        out_y,
        out_x,
        late[:vec].reshape(D),
        late[vec : 2 * vec].reshape(D),
        qkv_sum,
        qv_sum,
        out_sum,
        shared[3],
        shared[1],
        shared[2],
        fc_sum,
        fc_bias_sum,
        proj_sum,
        shared[0],
    )


def solution(mesh):
    groups, members = mesh.shape["dp"], mesh.shape["tensor"]
    n = min(8, groups)
    cut = Mesh(mesh.devices.reshape(n, groups // n, members), ("hi", "lo", "tensor"))
    dp = ("hi", "lo")
    return jax.shard_map(
        functools.partial(local, n),
        mesh=cut,
        in_specs=(
            P(("hi", "lo", "tensor"), None),
            P(("hi", "lo", "tensor"), None),
            P(),
            P(),
            P(),
            P(),
            P(dp, None, "tensor"),
            P(None, "tensor"),
            P("tensor", dp),
            P(),
            P(),
            P(),
            P(dp, "tensor"),
            P("tensor"),
            P("tensor", dp),
            P(),
        ),
        out_specs=(
            P(("hi", "lo", "tensor"), None),
            P(("hi", "lo", "tensor"), None),
            P(),
            P(),
            P(dp, None, "tensor"),
            P(None, "tensor"),
            P("tensor", dp),
            P(),
            P(),
            P(),
            P(dp, "tensor"),
            P("tensor"),
            P("tensor", dp),
            P(),
        ),
        check_vma=False,
    )
```

```python
import functools

import jax
import jax.numpy as jnp
from jax import lax
from jax.experimental import pallas as pl
from jax.experimental.pallas import tpu as pltpu
from jax.sharding import Mesh
from jax.sharding import PartitionSpec as P

HEAD_DIM = 64
EPSILON = 1e-05
MASKED = -1e30
BF = jnp.bfloat16
F32 = jnp.float32
MESH = pl.DeviceIdType.MESH
CURVE = 0.7978845608028654
CUBE = 0.044715

CHUNKS = 2
STEP = 32

QKV, OUT, FC, PROJ = "wqkv", "wo", "w1", "w2"
H1, GF, H2, DR = "h1", "gf", "h2", "dr"
X_IN, G_IN = "x", "g"
OUT_Y, OUT_X, OUT_QKV, OUT_WO = "out_y", "out_x", "out_qkv", "out_wo"
OUT_W1, OUT_W2, OUT_EARLY, OUT_LATE = "out_w1", "out_w2", "out_early", "out_late"

NN = ((1,), (0,))
NT = ((1,), (1,))
TN = ((0,), (0,))


class Refs(dict):
    __getattr__ = dict.__getitem__


def dot(left_side, right_side, form):
    return lax.dot_general(
        left_side, right_side, (form, ((), ())), preferred_element_type=F32
    )


def kernel(cfg, *refs):
    (n, packs, L, S, D, HC, FH, inside) = cfg
    names = cfg_names(cfg)
    r = Refs(zip(names, refs))
    slabs, hslabs = (r.slab0, r.slab1), (r.hslab0, r.hslab1)
    backs = (r.back0, r.back1) if inside else None
    NH = HC // HEAD_DIM
    NZ = n // 2
    WR = D // n
    PR = L // n
    CR = L // CHUNKS
    B = L

    hi = lax.axis_index("hi")
    lo = lax.axis_index("lo")
    t = lax.axis_index("tensor")
    z, xx = hi // 2, hi % 2
    y, c = t // 2, t % 2
    dev = lambda h, tt: (h, lo, tt)
    mate = dev(hi, 2 * y + 1 - c)
    ynb = dev(hi, 2 * (1 - y) + c)
    ymate = dev(hi, 2 * (1 - y) + 1 - c)
    xnb = dev(2 * z + 1 - xx, t)

    def zdev(k):
        return dev(2 * ((z + k) % NZ) + xx, t)

    def block_of(k):
        return 2 * ((y + k // 2) % 2) + (c + k % 2) % 2

    def rows(start, size, mult=None):
        return pl.ds(pl.multiple_of(start, mult or size), size)

    def block_rows(k):
        return rows(block_of(k) * B, B)

    def rcopy(src, dst, send, recv, target):
        return pltpu.make_async_remote_copy(
            src_ref=src,
            dst_ref=dst,
            send_sem=send,
            recv_sem=recv,
            device_id=target,
            device_id_type=MESH,
        )

    LOADS = (X_IN, G_IN, QKV, OUT, FC, PROJ)

    def load(name):
        return pltpu.make_async_copy(r[name + "_hbm"], r[name + "_in"], r.load_sem.at[LOADS.index(name)])

    for name in LOADS:
        load(name).start()

    barrier = pltpu.get_barrier_semaphore()
    peers = [dev((hi + k) % n, t) for k in range(1, n)] + [mate, ynb, ymate]
    for peer in peers:
        pl.semaphore_signal(barrier, inc=1, device_id=peer, device_id_type=MESH)

    def a2a(tag, k, source, target):
        sem = r.a2a_sem
        to = (hi + k) % n
        return rcopy(source(to), target(hi), sem.at[0, tag, k - 1], sem.at[1, tag, k - 1], dev(to, t))

    def a2a_in_copy(tag, k):
        return a2a(
            tag,
            k,
            lambda to: r.sent.at[tag, to],
            lambda me: r.came.at[tag, rows(me * PR, PR)],
        )

    def a2a_out_copy(tag, k):
        return a2a(
            2 + tag,
            k,
            lambda to: r.made.at[tag, rows(to * PR, PR)],
            lambda me: backs[tag].at[me],
        )

    def pick_pieces(tag, source):
        def one(k, _):
            where = jnp.int32(0)
            for j in range(n):
                where = jnp.where(r.order[j] == k, j, where)
            r.sent[tag, k] = source[where]
            return 0

        lax.fori_loop(0, n, one, 0)
        r.came[tag, rows(hi * PR, PR)] = r.sent[tag, hi]

    load(X_IN).wait()
    if inside:
        pick_pieces(0, r.x_in)
    pl.semaphore_wait(barrier, len(peers))
    if inside:
        for k in range(1, n):
            a2a_in_copy(0, k).start()
    else:
        r.came[0] = r.x_in[...]
    for j, vec in enumerate((r.ln1g, r.ln1b, r.aob, r.ln2g, r.ln2b, r.pjb, r.fcb)):
        for i in range(vec.shape[0]):
            r.vecs[j : j + 1, i * 128 : (i + 1) * 128] = vec[i : i + 1]

    WG = (QKV, OUT, FC, PROJ)
    middle = (z == 1) | (z == 2)
    side = z // 2
    near, far_mid, far_end = z + 1 - 2 * (z % 2), 2 - side, 3 - 3 * side
    Z_FROM = (near, far_mid, far_end)
    near_dev = dev(2 * near + xx, t)

    def wslot(name, ref, slot):
        where = rows(slot * WR, WR, 16)
        return ref.at[:, where] if name == QKV else ref.at[where]

    def wg_z(name, i):
        sem = r.wg_sem
        a = WG.index(name)
        if i < 2:
            slot = wslot(name, r[name], hi)
            target = (near_dev, dev(2 * far_mid + xx, t))[i]
            recv = (0, jnp.where(middle, 1, 2))[i]
        else:
            slot = wslot(name, r[name], 2 * Z_FROM[i - 1] + xx)
            target = near_dev
            recv = i - 1
        return rcopy(slot, slot, sem.at[0, a, i], sem.at[1, a, recv], target)

    def wg_in(name, i):
        sem = r.wg_sem
        a = WG.index(name)
        slot = wslot(name, r[name], 2 * Z_FROM[i] + xx)
        return rcopy(slot, slot, sem.at[0, a, 3], sem.at[1, a, i], near_dev)

    def wg_x(name, i):
        sem = r.wg_sem
        a = WG.index(name)
        slot = wslot(name, r[name], 2 * (Z_FROM + (z,))[i] + xx)
        return rcopy(slot, slot, sem.at[0, a, 4 + i], sem.at[1, a, 4 + i], xnb)

    def wg_start(name):
        wg_z(name, 0).start()
        wg_z(name, 1).start()

    def wg_first(name):
        wg_in(name, 0).wait_recv()
        wg_x(name, 0).start()

        @pl.when(middle)
        def _():
            for i in (1, 2):
                wg_in(name, i).wait_recv()
                wg_z(name, i + 1).start()
                wg_x(name, i).start()

    def wg_second(name):
        @pl.when(jnp.logical_not(middle))
        def _():
            for i in (1, 2):
                wg_in(name, i).wait_recv()
                wg_x(name, i).start()

    def wg_wait(name):
        for i in range(NZ):
            wg_x(name, i).wait_recv()

    def wg_drain(name):
        for i in range(2):
            wg_z(name, i).wait_send()
        for i in range(NZ):
            wg_x(name, i).wait_send()

        @pl.when(middle)
        def _():
            for i in (2, 3):
                wg_z(name, i).wait_send()

    own_w = rows(hi * WR, WR, 16)
    for name in WG:
        load(name).wait()
    for i in range(3):
        r.wqkv[i, own_w] = r.wqkv_in[i].astype(BF)
    r.w1[own_w] = r.w1_in[...].astype(BF)
    r.w2[own_w] = r.w2_in[...].astype(BF)
    r.turn[...] = jnp.zeros_like(r.turn)
    r.turn[:HC, :WR] = r.wo_in[...].astype(F32)
    r.wo[own_w] = r.turn[...].T[:WR, :HC].astype(BF)
    for name in WG:
        wg_x(name, 3).start()

    load(G_IN).wait()
    if inside:
        pick_pieces(1, r.g_in)
    else:
        r.came[1] = r.g_in[...]

    AG = (H1, GF, H2, DR)

    def ag(name, kind, ch):
        sem = r.ag_sem
        a = AG.index(name)
        full = r[name]
        if kind == 2:
            where = rows(block_of(2) * B + ch * CR, CR)
        else:
            where = rows(t * B + ch * CR, CR)
        target = ynb if kind == 0 else mate
        part = full.at[where]
        return rcopy(part, part, sem.at[0, a, kind, ch], sem.at[1, a, kind, ch], target)

    def ag_send(name, ch):
        ag(name, 0, ch).start()
        ag(name, 1, ch).start()

    def ag_forward(name, ch):
        ag(name, 0, ch).wait_recv()
        ag(name, 2, ch).start()

    def ag_arrive(name, k):
        for ch in range(CHUNKS):
            if k == 1:
                ag(name, 1, ch).wait_recv()
            elif k == 2:
                ag_forward(name, ch)
            else:
                ag(name, 2, ch).wait_recv()

    def ag_drain(name):
        for kind in range(3):
            for ch in range(CHUNKS):
                ag(name, kind, ch).wait_send()

    def rs_bufs(tag):
        if tag == 3:
            return r.msy, r.mry, r.keepy, r.ysy, r.yry
        return r.msc, r.mrc, r.keepc, r.ysc, r.yrc

    def rs_m(tag, i):
        ms, mr, _, _, _ = rs_bufs(tag)
        sem = r.rs_sem
        return rcopy(ms.at[i], mr.at[i], sem.at[0, tag, i], sem.at[1, tag, i], mate)

    def rs_y(tag, ch):
        _, _, _, ys, yr = rs_bufs(tag)
        sem = r.rs_sem
        where = pl.ds(ch * CR, CR)
        return rcopy(ys.at[where], yr.at[where], sem.at[0, tag, 2 + ch], sem.at[1, tag, 2 + ch], ynb)

    def rs_put(tag, k, value, at=None):
        ms, _, keep, _, _ = rs_bufs(tag)
        where = slice(None) if at is None else at
        i = 0 if k >= 2 else 1
        if k % 2:
            ms[i, where] = value.astype(BF)
        else:
            keep[i, where] = value

    def rs_ship(tag):
        _, mr, keep, ys, _ = rs_bufs(tag)
        rs_m(tag, 0).wait_recv()
        for ch in range(CHUNKS):

            def one(s, _):
                at = rows(ch * CR + s * STEP, STEP)
                ys[at] = (keep[0, at] + mr[0, at].astype(F32)).astype(BF)
                return 0

            lax.fori_loop(0, CR // STEP, one, 0)
            rs_y(tag, ch).start()

    def rs_total(tag, at):
        _, mr, keep, _, yr = rs_bufs(tag)
        return keep[1, at] + mr[1, at].astype(F32) + yr[at].astype(F32)

    def rs_drain(tag):
        for i in range(2):
            rs_m(tag, i).wait_send()
        for ch in range(CHUNKS):
            rs_y(tag, ch).wait_send()

    GR = {name: "g" + name for name in WG}

    def gr_x(name, k):
        sem = r.gr_sem
        a = WG.index(name)
        slot = wslot(name, r[GR[name]], 2 * k + 1 - xx)
        return rcopy(slot, r[name + "_xr"].at[k], sem.at[0, a, k], sem.at[1, a, k], xnb)

    def gr_z(name, k):
        sem = r.gr_sem
        a = WG.index(name)
        return rcopy(
            r[name + "_zs"].at[k - 1],
            r[name + "_zr"].at[k - 1],
            sem.at[0, a, NZ + k],
            sem.at[1, a, NZ + k],
            zdev(k),
        )

    def gr_start(name):
        for k in range(NZ):
            gr_x(name, k).start()

    def gr_mid(name):
        for k in range(NZ):
            gr_x(name, k).wait_recv()
        for k in range(1, NZ):
            to = (z + k) % NZ
            mine = wslot(name, r[GR[name]], 2 * to + xx)[...].astype(F32)
            r[name + "_zs"][k - 1] = (mine + r[name + "_xr"][to].astype(F32)).astype(BF)
            gr_z(name, k).start()

    def gr_finish(name):
        total = wslot(name, r[GR[name]], hi)[...].astype(F32) + r[name + "_xr"][z].astype(F32)
        for k in range(1, NZ):
            gr_z(name, k).wait_recv()
            total = total + r[name + "_zr"][k - 1].astype(F32)
        return total

    def gr_drain(name):
        for k in range(NZ):
            gr_x(name, k).wait_send()
        for k in range(1, NZ):
            gr_z(name, k).wait_send()

    tpeers = [mate, ynb, ymate]
    SHARED = (32, 16)

    def sm_t(tag, i):
        sem = r.sm_sem
        part = slabs[tag].at[t]
        return rcopy(part, part, sem.at[0, tag, i], sem.at[1, tag, i], tpeers[i])

    def sm_h(tag, k):
        sem = r.sm_sem
        part = hslabs[tag].at[hi]
        return rcopy(part, part, sem.at[0, tag, 3 + k], sem.at[1, tag, 3 + k], dev((hi + k) % n, t))

    def spread(tag, at, value):
        for j in range(value.shape[1] // 128):
            slabs[tag][t, at + j : at + j + 1] = value[:, j * 128 : (j + 1) * 128]

    def sm_start(tag):
        for i in range(3):
            sm_t(tag, i).start()

    def sm_mid(tag):
        for i in range(3):
            sm_t(tag, i).wait_recv()
        slab, hslab = slabs[tag], hslabs[tag]
        total = slab[0]
        for i in range(1, 4):
            total = total + slab[i]
        if tag == 0:
            keep = lax.broadcasted_iota(jnp.int32, total.shape, 0) < SHARED[0]
            total = jnp.where(keep, total, slab[t])
        hslab[hi] = total
        for k in range(1, n):
            sm_h(tag, k).start()

    def sm_finish(tag):
        for k in range(1, n):
            sm_h(tag, k).wait_recv()
        hslab = hslabs[tag]
        total = hslab[0]
        for k in range(1, n):
            total = total + hslab[k]
        return total

    def sm_drain(tag):
        for i in range(3):
            sm_t(tag, i).wait_send()
        for k in range(1, n):
            sm_h(tag, k).wait_send()

    def fold(value):
        return jnp.sum(value.reshape(value.shape[0] // 8, 8, value.shape[1]), axis=0)

    for slab in slabs:
        slab[t] = jnp.zeros(slab.shape[1:], F32)
    r.acc[...] = jnp.zeros_like(r.acc)
    r.acc_f[...] = jnp.zeros_like(r.acc_f)
    r.acc_h[...] = jnp.zeros_like(r.acc_h)

    if inside:
        for k in range(1, n):
            a2a_in_copy(0, k).wait_recv()
    wg_start(QKV)
    wg_start(OUT)

    def norm_step(values, at, gain, bias, cen, scale):
        mean = jnp.mean(values, axis=1, keepdims=True)
        var = jnp.mean(values * values, axis=1, keepdims=True) - mean * mean
        inv = lax.rsqrt(var + EPSILON)
        centered = (values - mean) * inv
        cen[at] = centered
        scale[at] = inv
        return (centered * gain + bias).astype(BF)

    def norm_back(grad, at, gain, cen, scale, acc_at):
        centered = cen[at]
        r.acc[acc_at] += fold(grad * centered)
        r.acc[acc_at + 1] += fold(grad)
        scaled = grad * gain
        return scale[at] * (
            scaled
            - jnp.mean(scaled, axis=1, keepdims=True)
            - centered * jnp.mean(scaled * centered, axis=1, keepdims=True)
        )

    for ch in range(CHUNKS):

        def one(s, _):
            at = rows(ch * CR + s * STEP, STEP)
            values = r.came[0, at].astype(F32)
            r.h1[rows(t * B + ch * CR + s * STEP, STEP)] = norm_step(
                values, at, r.vecs[0:1], r.vecs[1:2], r.cen1, r.scale1
            )
            return 0

        lax.fori_loop(0, CR // STEP, one, 0)
        ag_send(H1, ch)

    if inside:
        for k in range(1, n):
            a2a_in_copy(1, k).start()
    wg_first(QKV)
    wg_first(OUT)
    wg_start(FC)
    wg_start(PROJ)
    wg_second(QKV)
    wg_second(OUT)
    wg_wait(QKV)

    lane = lax.broadcasted_iota(jnp.int32, (1, HC), 1)

    def head_mask(h):
        return (lane >= h * HEAD_DIM) & (lane < (h + 1) * HEAD_DIM)

    def project(s, _):
        @pl.when(s == 1)
        def _():
            ag_arrive(H1, 1)

        @pl.when(s == 2)
        def _():
            ag_arrive(H1, 2)

        @pl.when(s == 3)
        def _():
            ag_arrive(H1, 3)

        b = block_of(s)
        at = rows(b * B, B)
        hidden = r.h1[at]
        q = dot(hidden, r.wqkv[0], NN) + r.qvb[0:1]
        q = (q.astype(BF).astype(F32) * HEAD_DIM ** (-0.5)).astype(BF)
        for h in range(NH):
            r.qm[b, h * B : (h + 1) * B] = jnp.where(head_mask(h), q, jnp.zeros_like(q))
        k = dot(hidden, r.wqkv[1], NN)
        r.k[at] = k.astype(BF)
        r.kt[:, at] = k.T.astype(BF)
        v = dot(hidden, r.wqkv[2], NN) + r.qvb[1:2]
        r.v[at] = v.astype(BF)
        r.vt[:, at] = v.T.astype(BF)
        return 0

    lax.fori_loop(0, 4, project, 0)

    if inside:
        for k in range(1, n):
            a2a_in_copy(1, k).wait_recv()

    def own_grad(s, _):
        at = rows(s * STEP, STEP)
        value = r.came[1, at]
        r.gf[rows(t * B + s * STEP, STEP)] = value
        r.acc[5] += fold(value.astype(F32))
        return 0

    lax.fori_loop(0, B // STEP, own_grad, 0)
    for ch in range(CHUNKS):
        ag_send(GF, ch)
    wg_first(FC)

    pack = hi * (packs // n) + lo

    def attend(i):
        pos = i * B + lax.broadcasted_iota(jnp.int32, (1, B), 1)
        first = jnp.zeros((1, B), jnp.int32)
        end = jnp.int32(0)
        for s in range(r.lengths.shape[0]):
            length = r.lengths[s, pack]
            end = end + length
            first = first + jnp.where(pos >= end, length, 0)

        def scores(j, peak):
            key_pos = j * B + lax.broadcasted_iota(jnp.int32, (B, B), 0)
            allowed = (key_pos >= first) & (key_pos <= pos)
            keys = r.k[rows(j * B, B)]
            peaks = []
            for h in range(NH):
                raw = dot(keys, r.qm[i, h * B : (h + 1) * B], NT)
                raw = jnp.where(allowed, raw, MASKED)
                r.score[j, :, h * B : (h + 1) * B] = raw
                peaks.append(jnp.max(raw, axis=0, keepdims=True))
            return jnp.maximum(peak, jnp.concatenate(peaks, axis=1))

        peak = lax.fori_loop(0, i + 1, scores, jnp.full((1, NH * B), MASKED, F32))
        r.att[...] = jnp.zeros_like(r.att)

        def weigh(j, total):
            totals = []
            for h in range(NH):
                cols = slice(h * B, (h + 1) * B)
                weight = jnp.exp(r.score[j, :, cols] - peak[:, cols])
                totals.append(jnp.sum(weight, axis=0, keepdims=True))
                low = weight.astype(BF)
                r.e[i, j, :, cols] = low
                part = slice(h * HEAD_DIM, (h + 1) * HEAD_DIM)
                r.att[part] += dot(r.vt[part, rows(j * B, B)], low, NN)
            return total + jnp.concatenate(totals, axis=1)

        total = lax.fori_loop(0, i + 1, weigh, jnp.zeros((1, NH * B), F32))
        inverse = 1.0 / total
        for h in range(NH):
            part = slice(h * HEAD_DIM, (h + 1) * HEAD_DIM)
            own = inverse[:, h * B : (h + 1) * B]
            r.att[part] = r.att[part] * own
            r.inv[i, h : h + 1] = own
        out = r.att[...].T
        at = rows(i * B, B)
        r.a[at] = out
        r.al[at] = out.astype(BF)

    def attend_step(s, _):
        k = 3 - s
        i = block_of(k)
        attend(i)

        @pl.when(s == 0)
        def _():
            wg_wait(OUT)

        part = dot(r.al[rows(i * B, B)], r.wo[...], NT)

        @pl.when(s == 0)
        def _():
            rs_put(0, 3, part)
            rs_m(0, 0).start()

        @pl.when(s == 1)
        def _():
            rs_put(0, 2, part)
            rs_ship(0)
            wg_second(FC)

        @pl.when(s == 2)
        def _():
            rs_put(0, 1, part)
            rs_m(0, 1).start()
            wg_first(PROJ)

        @pl.when(s == 3)
        def _():
            rs_put(0, 0, part)

        return 0

    lax.fori_loop(0, 4, attend_step, 0)

    rs_m(0, 1).wait_recv()
    for ch in range(CHUNKS):
        rs_y(0, ch).wait_recv()

        def one(s, _):
            at = rows(ch * CR + s * STEP, STEP)
            values = r.came[0, at].astype(F32) + rs_total(0, at) + r.vecs[2:3]
            r.res[at] = values
            r.h2[rows(t * B + ch * CR + s * STEP, STEP)] = norm_step(
                values, at, r.vecs[3:4], r.vecs[4:5], r.cen2, r.scale2
            )
            return 0

        lax.fori_loop(0, CR // STEP, one, 0)
        ag_send(H2, ch)
    rs_drain(0)
    ag_arrive(GF, 1)
    ag_arrive(GF, 2)
    wg_second(PROJ)
    ag_arrive(GF, 3)
    wg_wait(FC)
    wg_wait(PROJ)

    def feed(s, _):
        @pl.when(s == 1)
        def _():
            ag_arrive(H2, 1)

        @pl.when(s == 2)
        def _():
            ag_arrive(H2, 2)

        @pl.when(s == 3)
        def _():
            ag_arrive(H2, 3)

        at = block_rows(s)
        hidden = r.h2[at]
        grad = r.gf[at]
        for j in range(FH // 256):
            cols = slice(j * 256, (j + 1) * 256)
            u = dot(hidden, r.w1[:, cols], NN) + r.vecs[6:7, cols]
            dz = dot(grad, r.w2[:, cols], NN)
            square = u * u
            half = 0.5 + 0.5 * jnp.tanh(u * (CURVE + (CURVE * CUBE) * square))
            act = u * half
            r.zz[at, cols] = act.astype(BF)
            slope = half + act * (1.0 - half) * (2.0 * CURVE + (6.0 * CURVE * CUBE) * square)
            low = (dz * slope).astype(BF)
            r.du[at, cols] = low
            r.acc_f[:, cols] += fold(low.astype(F32))
        part = dot(r.du[at], r.w1[...], NT)

        @pl.when(s == 0)
        def _():
            rs_put(1, 0, part)

        @pl.when(s == 1)
        def _():
            rs_put(1, 1, part)
            rs_m(1, 1).start()

        @pl.when(s == 2)
        def _():
            rs_put(1, 2, part)

        @pl.when(s == 3)
        def _():
            rs_put(1, 3, part)
            rs_m(1, 0).start()

        return 0

    lax.fori_loop(0, 4, feed, 0)
    rs_ship(1)

    def grad_tiles(left, right, out, form=TN):
        def one(i, _):
            at = rows(i * 256, 256)
            out[at] = dot(left[:, at], right[...], form).astype(BF)
            return 0

        lax.fori_loop(0, D // 256, one, 0)

    grad_tiles(r.gf, r.zz, r.gw2)
    gr_start(PROJ)
    grad_tiles(r.h2, r.du, r.gw1)
    gr_start(FC)

    rs_m(1, 1).wait_recv()
    for ch in range(CHUNKS):
        rs_y(1, ch).wait_recv()

        def one(s, _):
            at = rows(ch * CR + s * STEP, STEP)
            back = norm_back(rs_total(1, at), at, r.vecs[3:4], r.cen2, r.scale2, 2)
            grad = r.came[1, at].astype(F32) + back
            r.dres[at] = grad
            r.acc[4] += fold(grad)
            r.dr[rows(t * B + ch * CR + s * STEP, STEP)] = grad.astype(BF)
            return 0

        lax.fori_loop(0, CR // STEP, one, 0)
        ag_send(DR, ch)
    rs_drain(1)

    def upper(s, _):
        k = 3 - s
        part = dot(r.zz[block_rows(k)], r.w2[...], NT)

        @pl.when(s == 0)
        def _():
            rs_put(3, 3, part)
            rs_m(3, 0).start()

        @pl.when(s == 1)
        def _():
            rs_put(3, 2, part)

        @pl.when(s == 2)
        def _():
            rs_put(3, 1, part)
            rs_m(3, 1).start()

        @pl.when(s == 3)
        def _():
            rs_put(3, 0, part)

        return 0

    lax.fori_loop(0, 4, upper, 0)
    gr_mid(PROJ)
    gr_mid(FC)

    r.dk[...] = jnp.zeros_like(r.dk)
    r.dv[...] = jnp.zeros_like(r.dv)

    def attend_back(s, _):
        @pl.when(s == 1)
        def _():
            ag_arrive(DR, 1)

        @pl.when(s == 2)
        def _():
            ag_arrive(DR, 2)
            rs_ship(3)

        @pl.when(s == 3)
        def _():
            ag_arrive(DR, 3)
            grad_tiles(r.dr, r.al, r.gwo)
            gr_start(OUT)

        i = block_of(s)
        at = rows(i * B, B)
        da = dot(r.dr[at], r.wo[...], NN).astype(BF).astype(F32)
        by_row = r.inv[i].T
        scale = by_row[:, NH - 1 : NH]
        for h in range(NH - 1):
            scale = jnp.where(head_mask(h), by_row[:, h : h + 1], scale)
        low = (da * scale).astype(BF)
        for h in range(NH):
            r.dam[h * B : (h + 1) * B] = jnp.where(head_mask(h), low, jnp.zeros_like(low))
        lined = (low.astype(F32) * r.a[at]).T
        deltas = [
            jnp.sum(lined[h * HEAD_DIM : (h + 1) * HEAD_DIM], axis=0, keepdims=True)
            for h in range(NH)
        ]
        r.att[...] = jnp.zeros_like(r.att)

        def over_keys(j, _):
            kr = rows(j * B, B)
            values = r.v[kr]
            for h in range(NH):
                cols = slice(h * B, (h + 1) * B)
                dp = dot(values, r.dam[cols], NT)
                ds = (r.e[i, j, :, cols].astype(F32) * (dp - deltas[h])).astype(BF)
                r.ds[:, cols] = ds
                part = slice(h * HEAD_DIM, (h + 1) * HEAD_DIM)
                r.att[part] += dot(r.kt[part, kr], ds, NN)
            r.dk[kr] += dot(r.ds[...], r.qm[i], NN)
            r.dv[kr] += dot(r.e[i, j], r.dam[...], NN)
            return 0

        lax.fori_loop(0, i + 1, over_keys, 0)
        dq = (r.att[...].T * HEAD_DIM ** (-0.5)).astype(BF)
        r.dqkv[0, at] = dq
        return 0

    lax.fori_loop(0, 4, attend_back, 0)

    def round_kv(b, _):
        at = rows(b * B, B)
        dv = r.dv[at].astype(BF)
        r.dqkv[1, at] = r.dk[at].astype(BF)
        r.dqkv[2, at] = dv
        r.acc_h[0] += fold(r.dqkv[0, at].astype(F32))
        r.acc_h[1] += fold(dv.astype(F32))
        return 0

    lax.fori_loop(0, 4, round_kv, 0)

    def lower(s, _):
        k = 3 - s
        at = block_rows(k)
        part = dot(r.dqkv[0, at], r.wqkv[0], NT)
        part = part + dot(r.dqkv[1, at], r.wqkv[1], NT)
        part = part + dot(r.dqkv[2, at], r.wqkv[2], NT)

        @pl.when(s == 0)
        def _():
            rs_put(2, 3, part)
            rs_m(2, 0).start()

        @pl.when(s == 1)
        def _():
            rs_put(2, 2, part)
            rs_ship(2)

        @pl.when(s == 2)
        def _():
            rs_put(2, 1, part)
            rs_m(2, 1).start()

        @pl.when(s == 3)
        def _():
            rs_put(2, 0, part)

        return 0

    lax.fori_loop(0, 4, lower, 0)

    def grad_qkv(i, _):
        at = rows(i * 256, 256)
        left = r.h1[:, at]
        for j in range(3):
            r.gwqkv[j, at] = dot(left, r.dqkv[j], TN).astype(BF)
        return 0

    lax.fori_loop(0, D // 256, grad_qkv, 0)
    gr_start(QKV)

    rs_m(3, 1).wait_recv()
    for ch in range(CHUNKS):
        rs_y(3, ch).wait_recv()

    def finish_up(s, _):
        at = rows(s * STEP, STEP)
        r.made[0, at] = (r.res[at] + rs_total(3, at) + r.vecs[5:6]).astype(BF)
        return 0

    lax.fori_loop(0, B // STEP, finish_up, 0)
    if inside:
        for k in range(1, n):
            a2a_out_copy(0, k).start()
        r.back0[hi] = r.made[0, rows(hi * PR, PR)]
    else:
        r.out_y_v[...] = r.made[0]

    def line(value):
        return jnp.sum(value, axis=0, keepdims=True)

    for j, at in enumerate((5, 2, 3, 4)):
        spread(0, 8 * j, line(r.acc[at]))
    spread(0, 32, line(r.acc_f[...]))
    pad = jnp.zeros((1, 256 - HC), F32)
    for j in range(2):
        spread(0, 40 + 2 * j, jnp.concatenate([line(r.acc_h[j]), pad], axis=1))
    sm_start(0)

    rs_m(2, 1).wait_recv()
    for ch in range(CHUNKS):
        rs_y(2, ch).wait_recv()

        def one(s, _):
            at = rows(ch * CR + s * STEP, STEP)
            back = norm_back(rs_total(2, at), at, r.vecs[0:1], r.cen1, r.scale1, 0)
            r.made[1, at] = (r.dres[at] + back).astype(BF)
            return 0

        lax.fori_loop(0, CR // STEP, one, 0)
    rs_drain(2)
    rs_drain(3)
    if inside:
        for k in range(1, n):
            a2a_out_copy(1, k).start()
        r.back1[hi] = r.made[1, rows(hi * PR, PR)]
    else:
        r.out_x_v[...] = r.made[1]
    for j in range(2):
        spread(1, 8 * j, line(r.acc[j]))
    sm_start(1)
    sm_mid(0)
    gr_mid(QKV)
    gr_mid(OUT)
    sm_mid(1)

    OUTS = tuple(outputs(cfg))

    def store(name):
        return pltpu.make_async_copy(r[name + "_v"], r[name], r.store_sem.at[OUTS.index(name)])

    def put_back(tag, out):
        for k in range(1, n):
            a2a_out_copy(tag, k).wait_recv()

        def one(j, _):
            out[j] = backs[tag][r.order[j]]
            return 0

        lax.fori_loop(0, n, one, 0)

    r.out_w2_v[...] = gr_finish(PROJ)
    store(OUT_W2).start()
    r.out_w1_v[...] = gr_finish(FC)
    store(OUT_W1).start()
    if inside:
        put_back(0, r.out_y_v)
    store(OUT_Y).start()
    r.turn[...] = jnp.zeros_like(r.turn)
    r.turn[:WR, :HC] = gr_finish(OUT)
    r.out_wo_v[...] = r.turn[...].T[:HC, :WR]
    store(OUT_WO).start()
    r.out_early_v[...] = sm_finish(0)
    store(OUT_EARLY).start()
    if inside:
        put_back(1, r.out_x_v)
    store(OUT_X).start()
    r.out_late_v[...] = sm_finish(1)
    store(OUT_LATE).start()
    r.out_qkv_v[...] = gr_finish(QKV)
    store(OUT_QKV).start()

    for name in WG:
        wg_drain(name)
        gr_drain(name)
    for name in AG:
        ag_drain(name)
    for name in OUTS:
        store(name).wait()
    for tag in range(2):
        sm_drain(tag)
        if inside:
            for k in range(1, n):
                a2a_in_copy(tag, k).wait_send()
                a2a_out_copy(tag, k).wait_send()


def settle(*refs):
    early, late = refs[6:8]
    whole, small = refs[8:14], refs[14:22]
    for i in range(6):
        whole[i][...] = refs[i][...]
    for j in range(4):
        small[j][...] = early[8 * j : 8 * j + small[j].shape[0]]
    for j in range(2):
        small[4 + j][...] = late[8 * j : 8 * j + small[4 + j].shape[0]]
    small[6][...] = early[32 : 32 + small[6].shape[0]]
    heads = small[7]
    for j in range(2):
        heads[j : j + 1, :128] = early[40 + 2 * j : 41 + 2 * j]
        heads[j : j + 1, 128:] = early[41 + 2 * j : 42 + 2 * j, : heads.shape[1] - 128]


def inputs():
    vmem = pl.BlockSpec(memory_space=pltpu.VMEM)
    smem = pl.BlockSpec(memory_space=pltpu.SMEM)
    hbm = pl.BlockSpec(memory_space=pl.ANY)
    return Refs(
        order=smem,
        lengths=smem,
        x_hbm=hbm,
        g_hbm=hbm,
        ln1g=vmem,
        ln1b=vmem,
        wqkv_hbm=hbm,
        qvb=vmem,
        wo_hbm=hbm,
        aob=vmem,
        ln2g=vmem,
        ln2b=vmem,
        w1_hbm=hbm,
        fcb=vmem,
        w2_hbm=hbm,
        pjb=vmem,
    )


def outputs(cfg):
    (n, packs, L, S, D, HC, FH, inside) = cfg
    WR = D // n
    tokens = (n, L // n, D) if inside else (L, D)
    return Refs(
        out_y=(tokens, BF),
        out_x=(tokens, BF),
        out_qkv=((3, WR, HC), F32),
        out_wo=((HC, WR), F32),
        out_w1=((WR, FH), F32),
        out_w2=((WR, FH), F32),
        out_early=((48, 128), F32),
        out_late=((16, 128), F32),
    )


def scratch(cfg):
    (n, packs, L, S, D, HC, FH, inside) = cfg
    NH = HC // HEAD_DIM
    NZ = n // 2
    WR = D // n
    V = pltpu.VMEM
    sem = pltpu.SemaphoreType.DMA
    blocks = S // L
    tokens = (n, L // n, D) if inside else (L, D)
    kind = F32 if inside else BF
    made = Refs(
        came=V((2, L, D), BF),
        made=V((2, L, D), BF),
        wqkv=V((3, D, HC), BF),
        wo=V((D, HC), BF),
        w1=V((D, FH), BF),
        w2=V((D, FH), BF),
        turn=V((256, 256), F32),
        vecs=V((8, D), F32),
        x_in=V(tokens, BF),
        g_in=V(tokens, BF),
        wqkv_in=V((3, WR, HC), kind),
        wo_in=V((HC, WR), kind),
        w1_in=V((WR, FH), kind),
        w2_in=V((WR, FH), kind),
        load_sem=sem((6,)),
        store_sem=sem((8,)),
        h1=V((S, D), BF),
        gf=V((S, D), BF),
        h2=V((S, D), BF),
        dr=V((S, D), BF),
        cen1=V((L, D), F32),
        cen2=V((L, D), F32),
        scale1=V((L, 1), F32),
        scale2=V((L, 1), F32),
        res=V((L, D), F32),
        dres=V((L, D), F32),
        qm=V((blocks, NH * L, HC), BF),
        k=V((S, HC), BF),
        v=V((S, HC), BF),
        kt=V((HC, S), BF),
        vt=V((HC, S), BF),
        score=V((blocks, L, NH * L), F32),
        e=V((blocks, blocks, L, NH * L), BF),
        att=V((HC, L), F32),
        inv=V((blocks, 8, L), F32),
        a=V((S, HC), F32),
        al=V((S, HC), BF),
        dam=V((NH * L, HC), BF),
        ds=V((L, NH * L), BF),
        dk=V((S, HC), F32),
        dv=V((S, HC), F32),
        dqkv=V((3, S, HC), BF),
        zz=V((S, FH), BF),
        du=V((S, FH), BF),
        acc=V((6, 8, D), F32),
        acc_f=V((8, FH), F32),
        acc_h=V((2, 8, HC), F32),
        slab0=V((4, 48, 128), F32),
        slab1=V((4, 16, 128), F32),
        hslab0=V((n, 48, 128), F32),
        hslab1=V((n, 16, 128), F32),
    )
    for name, (shape, dtype) in outputs(cfg).items():
        made[name + "_v"] = V(shape, dtype)
    if inside:
        made.update(
            sent=V((2, n, L // n, D), BF),
            back0=V((n, L // n, D), BF),
            back1=V((n, L // n, D), BF),
            a2a_sem=sem((2, 4, n - 1)),
        )
    for late in "cy":
        made["ms" + late] = V((2, L, D), BF)
        made["mr" + late] = V((2, L, D), BF)
        made["keep" + late] = V((2, L, D), F32)
        made["ys" + late] = V((L, D), BF)
        made["yr" + late] = V((L, D), BF)
    for name, slot in ((QKV, (3, WR, HC)), (OUT, (WR, HC)), (FC, (WR, FH)), (PROJ, (WR, FH))):
        made["g" + name] = V(slot[:-2] + (D, slot[-1]), BF)
        made[name + "_xr"] = V((NZ,) + slot, BF)
        made[name + "_zs"] = V((NZ - 1,) + slot, BF)
        made[name + "_zr"] = V((NZ - 1,) + slot, BF)
    made.update(
        wg_sem=sem((2, 4, 2 * NZ)),
        gr_sem=sem((2, 4, 2 * NZ)),
        ag_sem=sem((2, 4, 3, CHUNKS)),
        rs_sem=sem((2, 4, 2 + CHUNKS)),
        sm_sem=sem((2, 2, 3 + n)),
    )
    return made


def cfg_names(cfg):
    return tuple(inputs()) + tuple(outputs(cfg)) + tuple(scratch(cfg))


def local(
    n,
    block_input,
    out_cotangent,
    seq_lengths,
    pack_order,
    ln1_gain,
    ln1_bias,
    qkv_weight,
    qv_bias,
    attn_out_weight,
    attn_out_bias,
    ln2_gain,
    ln2_bias,
    fc_weight,
    fc_bias,
    proj_weight,
    proj_bias,
):
    L, D = block_input.shape
    packs = pack_order.shape[0]
    HC = qv_bias.shape[1]
    FH = fc_bias.shape[0]
    S = L * lax.axis_size("tensor")
    outer = packs // n
    inside = outer == 1
    cfg = (n, packs, L, S, D, HC, FH, inside)
    tokens = (block_input, out_cotangent)
    weights = (qkv_weight, attn_out_weight, fc_weight, proj_weight)
    if inside:
        tokens = [v.reshape(n, L // n, D) for v in tokens]
    else:
        slots = jnp.arange(packs, dtype=jnp.int32)
        chosen = (pack_order[None, :] == slots[:, None]).astype(BF)

        def pick(which, v):
            return (
                jnp.dot(which, v.reshape(packs, -1), preferred_element_type=F32)
                .astype(BF)
                .reshape(L, D)
            )

        tokens = [
            lax.all_to_all(
                pick(chosen, v), ("hi", "lo"), split_axis=0, concat_axis=0, tiled=True
            )
            for v in tokens
        ]
        weights = [
            lax.all_gather(w.astype(BF), "lo", axis=axis, tiled=True)
            for w, axis in zip(weights, (0, 1, 0, 1))
        ]
    row = lambda v: v.reshape(-1, 128)
    outs = outputs(cfg)
    made = pl.pallas_call(
        functools.partial(kernel, cfg),
        out_shape=[jax.ShapeDtypeStruct(shape, kind) for shape, kind in outs.values()],
        in_specs=list(inputs().values()),
        out_specs=[pl.BlockSpec(memory_space=pl.ANY)] * len(outs),
        scratch_shapes=list(scratch(cfg).values()),
        compiler_params=pltpu.CompilerParams(
            collective_id=0, has_side_effects=True, vmem_limit_bytes=63 * 2**20
        ),
    )(
        pack_order,
        seq_lengths.T,
        *tokens,
        row(ln1_gain),
        row(ln1_bias),
        jnp.transpose(weights[0], (1, 0, 2)),
        qv_bias,
        weights[1],
        row(attn_out_bias),
        row(ln2_gain),
        row(ln2_bias),
        weights[2],
        row(fc_bias),
        weights[3].T,
        row(proj_bias),
    )
    g = Refs(zip(outs, made))
    if not inside:
        exchange = lambda v: pick(
            chosen.T,
            lax.all_to_all(v, ("hi", "lo"), split_axis=0, concat_axis=0, tiled=True),
        )
        share = lambda v, axis: lax.psum_scatter(v, "lo", scatter_dimension=axis, tiled=True)
        g.out_y, g.out_x = exchange(g.out_y), exchange(g.out_x)
        g.out_qkv, g.out_wo = share(g.out_qkv, 1), share(g.out_wo, 1)
        g.out_w1, g.out_w2 = share(g.out_w1, 0), share(g.out_w2, 0)
        g.out_early, g.out_late = lax.psum((g.out_early, g.out_late), "lo")
    whole = [g.out_y.reshape(L, D), g.out_x.reshape(L, D), g.out_qkv, g.out_wo, g.out_w1, g.out_w2]
    vec = D // 128
    vmem = pl.BlockSpec(memory_space=pltpu.VMEM)
    settled = pl.pallas_call(
        settle,
        out_shape=[jax.ShapeDtypeStruct(v.shape, v.dtype) for v in whole]
        + [jax.ShapeDtypeStruct((vec, 128), F32)] * 6
        + [jax.ShapeDtypeStruct((FH // 128, 128), F32), jax.ShapeDtypeStruct((2, HC), F32)],
        in_specs=[vmem] * 8,
        out_specs=[vmem] * 14,
    )(*whole, g.out_early, g.out_late)
    out_y, out_x, qkv_sum, out_sum, fc_sum, proj_sum = settled[:6]
    pjb, ln2g, ln2b, aob, ln1g, ln1b = [v.reshape(D) for v in settled[6:12]]
    return (
        out_y,
        out_x,
        ln1g,
        ln1b,
        jnp.transpose(qkv_sum, (1, 0, 2)),
        settled[13],
        out_sum,
        aob,
        ln2g,
        ln2b,
        fc_sum,
        settled[12].reshape(FH),
        proj_sum.T,
        pjb,
    )


def solution(mesh):
    groups, members = mesh.shape["dp"], mesh.shape["tensor"]
    n = min(8, groups)
    cut = Mesh(mesh.devices.reshape(n, groups // n, members), ("hi", "lo", "tensor"))
    dp = ("hi", "lo")
    return jax.shard_map(
        functools.partial(local, n),
        mesh=cut,
        in_specs=(
            P(("hi", "lo", "tensor"), None),
            P(("hi", "lo", "tensor"), None),
            P(),
            P(),
            P(),
            P(),
            P(dp, None, "tensor"),
            P(None, "tensor"),
            P("tensor", dp),
            P(),
            P(),
            P(),
            P(dp, "tensor"),
            P("tensor"),
            P("tensor", dp),
            P(),
        ),
        out_specs=(
            P(("hi", "lo", "tensor"), None),
            P(("hi", "lo", "tensor"), None),
            P(),
            P(),
            P(dp, None, "tensor"),
            P(None, "tensor"),
            P("tensor", dp),
            P(),
            P(),
            P(),
            P(dp, "tensor"),
            P("tensor"),
            P("tensor", dp),
            P(),
        ),
        check_vma=False,
    )
```

```python
import functools

import jax
import jax.numpy as jnp
from jax import lax
from jax.experimental import pallas as pl
from jax.experimental.pallas import tpu as pltpu
from jax.sharding import Mesh
from jax.sharding import PartitionSpec as P

HEAD_DIM = 64
EPSILON = 1e-05
MASKED = -1e30
BF = jnp.bfloat16
F32 = jnp.float32
MESH = pl.DeviceIdType.MESH
CURVE = 0.7978845608028654
CUBE = 0.044715

CHUNKS = 2
STEP = 32

PAIR, LAST, OUT, FC, PROJ = "wa", "wb", "wo", "w1", "w2"
QKV = "wqkv"
H1, GF, H2, DR = "h1", "gf", "h2", "dr"
X_IN, G_IN = "x", "g"
OUT_Y, OUT_X, OUT_QKV, OUT_WO = "out_y", "out_x", "out_qkv", "out_wo"
OUT_W1, OUT_W2, OUT_EARLY, OUT_LATE = "out_w1", "out_w2", "out_early", "out_late"

NN = ((1,), (0,))
NT = ((1,), (1,))
TN = ((0,), (0,))


class Refs(dict):
    __getattr__ = dict.__getitem__


def dot(left_side, right_side, form):
    return lax.dot_general(
        left_side, right_side, (form, ((), ())), preferred_element_type=F32
    )


def kernel(cfg, *refs):
    (n, packs, L, S, D, HC, FH, inside) = cfg
    names = cfg_names(cfg)
    r = Refs(zip(names, refs))
    slabs, hslabs = (r.slab0, r.slab1), (r.hslab0, r.hslab1)
    backs = (r.back0, r.back1) if inside else None
    NH = HC // HEAD_DIM
    LW = HEAD_DIM
    PW = HC - LW
    NZ = n // 2
    WR = D // n
    PR = L // n
    CR = L // CHUNKS
    B = L
    KS = 2
    KB = KS * B

    hi = lax.axis_index("hi")
    lo = lax.axis_index("lo")
    t = lax.axis_index("tensor")
    z, xx = hi // 2, hi % 2
    y, c = t // 2, t % 2
    dev = lambda h, tt: (h, lo, tt)
    mate = dev(hi, 2 * y + 1 - c)
    ynb = dev(hi, 2 * (1 - y) + c)
    ymate = dev(hi, 2 * (1 - y) + 1 - c)
    xnb = dev(2 * z + 1 - xx, t)

    def zdev(k):
        return dev(2 * ((z + k) % NZ) + xx, t)

    def block_of(k):
        return 2 * ((y + k // 2) % 2) + (c + k % 2) % 2

    def rows(start, size, mult=None):
        return pl.ds(pl.multiple_of(start, mult or size), size)

    def block_rows(k):
        return rows(block_of(k) * B, B)

    def rcopy(src, dst, send, recv, target):
        return pltpu.make_async_remote_copy(
            src_ref=src,
            dst_ref=dst,
            send_sem=send,
            recv_sem=recv,
            device_id=target,
            device_id_type=MESH,
        )

    LOADS = (X_IN, G_IN, QKV, OUT, FC, PROJ)

    def load(name):
        return pltpu.make_async_copy(r[name + "_hbm"], r[name + "_in"], r.load_sem.at[LOADS.index(name)])

    for name in LOADS:
        load(name).start()

    barrier = pltpu.get_barrier_semaphore()
    peers = [dev((hi + k) % n, t) for k in range(1, n)] + [mate, ynb, ymate]
    for peer in peers:
        pl.semaphore_signal(barrier, inc=1, device_id=peer, device_id_type=MESH)

    def a2a(tag, k, source, target):
        sem = r.a2a_sem
        to = (hi + k) % n
        return rcopy(source(to), target(hi), sem.at[0, tag, k - 1], sem.at[1, tag, k - 1], dev(to, t))

    def a2a_in_copy(tag, k):
        return a2a(
            tag,
            k,
            lambda to: r.sent.at[tag, to],
            lambda me: r.came.at[tag, rows(me * PR, PR)],
        )

    def a2a_out_copy(tag, k):
        return a2a(
            2 + tag,
            k,
            lambda to: r.made.at[tag, rows(to * PR, PR)],
            lambda me: backs[tag].at[me],
        )

    def pick_pieces(tag, source):
        def one(k, _):
            where = jnp.int32(0)
            for j in range(n):
                where = jnp.where(r.order[j] == k, j, where)
            r.sent[tag, k] = source[where]
            return 0

        lax.fori_loop(0, n, one, 0)
        r.came[tag, rows(hi * PR, PR)] = r.sent[tag, hi]

    load(X_IN).wait()
    if inside:
        pick_pieces(0, r.x_in)
    pl.semaphore_wait(barrier, len(peers))
    if inside:
        for k in range(1, n):
            a2a_in_copy(0, k).start()
    else:
        r.came[0] = r.x_in[...]
    for j, vec in enumerate((r.ln1g, r.ln1b, r.aob, r.ln2g, r.ln2b, r.pjb, r.fcb)):
        for i in range(vec.shape[0]):
            r.vecs[j : j + 1, i * 128 : (i + 1) * 128] = vec[i : i + 1]

    WG = (PAIR, LAST, OUT, FC, PROJ)
    STRAIGHT = (PAIR, LAST, OUT)
    middle = (z == 1) | (z == 2)
    side = z // 2
    near, far_mid, far_end = z + 1 - 2 * (z % 2), 2 - side, 3 - 3 * side
    Z_FROM = (near, far_mid, far_end)
    near_dev = dev(2 * near + xx, t)

    def wslot(name, ref, slot):
        return ref.at[rows(slot * WR, WR, 16)]

    def wg_z(name, i):
        sem = r.wg_sem
        a = WG.index(name)
        if i < 2:
            slot = wslot(name, r[name], hi)
            target = (near_dev, dev(2 * far_mid + xx, t))[i]
            recv = (0, jnp.where(middle, 1, 2))[i]
        elif name in STRAIGHT:
            slot = wslot(name, r[name], hi)
            target = dev(2 * far_end + xx, t)
            recv = jnp.where(middle, 1, 2)
        else:
            slot = wslot(name, r[name], 2 * Z_FROM[i - 1] + xx)
            target = near_dev
            recv = i - 1
        return rcopy(slot, slot, sem.at[0, a, i], sem.at[1, a, recv], target)

    def wg_in(name, i):
        sem = r.wg_sem
        a = WG.index(name)
        slot = wslot(name, r[name], 2 * Z_FROM[i] + xx)
        return rcopy(slot, slot, sem.at[0, a, 3], sem.at[1, a, i], near_dev)

    def wg_x(name, i):
        sem = r.wg_sem
        a = WG.index(name)
        slot = wslot(name, r[name], 2 * (Z_FROM + (z,))[i] + xx)
        return rcopy(slot, slot, sem.at[0, a, 4 + i], sem.at[1, a, 4 + i], xnb)

    def wg_start(name):
        wg_z(name, 0).start()
        wg_z(name, 1).start()

    def wg_first(name):
        wg_in(name, 0).wait_recv()
        wg_x(name, 0).start()
        if name in STRAIGHT:
            return

        @pl.when(middle)
        def _():
            for i in (1, 2):
                wg_in(name, i).wait_recv()
                wg_z(name, i + 1).start()
                wg_x(name, i).start()

    def wg_second(name):
        if name in STRAIGHT:
            for i in (1, 2):
                wg_in(name, i).wait_recv()
                wg_x(name, i).start()
            return

        @pl.when(jnp.logical_not(middle))
        def _():
            for i in (1, 2):
                wg_in(name, i).wait_recv()
                wg_x(name, i).start()

    def wg_wait(name):
        for i in range(NZ):
            wg_x(name, i).wait_recv()

    def wg_drain(name):
        for i in range(2):
            wg_z(name, i).wait_send()
        for i in range(NZ):
            wg_x(name, i).wait_send()
        if name in STRAIGHT:
            wg_z(name, 2).wait_send()
            return

        @pl.when(middle)
        def _():
            for i in (2, 3):
                wg_z(name, i).wait_send()

    own_w = rows(hi * WR, WR, 16)
    load(QKV).wait()
    for i in range(3):
        part = r.wqkv_in[i].astype(BF)
        r.wa[own_w, i * PW : (i + 1) * PW] = part[:, :PW]
        r.wb[own_w, i * LW : (i + 1) * LW] = part[:, PW:]
    for name in (PAIR, LAST):
        wg_x(name, 3).start()
        wg_z(name, 0).start()
    for name in LOADS[3:]:
        load(name).wait()
    r.w1[own_w] = r.w1_in[...].astype(BF)
    r.w2[own_w] = r.w2_in[...].astype(BF)
    r.turn[...] = jnp.zeros_like(r.turn)
    r.turn[:HC, :WR] = r.wo_in[...].astype(F32)
    r.wo[own_w] = r.turn[...].T[:WR, :HC].astype(BF)
    for name in (OUT, FC, PROJ):
        wg_x(name, 3).start()
    wg_z(OUT, 0).start()
    load(G_IN).wait()
    if inside:
        pick_pieces(1, r.g_in)
    else:
        r.came[1] = r.g_in[...]

    AG = (H1, GF, H2, DR)

    def ag(name, kind, ch):
        sem = r.ag_sem
        a = AG.index(name)
        full = r[name]
        if kind == 2:
            where = rows(block_of(2) * B + ch * CR, CR)
        else:
            where = rows(t * B + ch * CR, CR)
        target = ynb if kind == 0 else mate
        part = full.at[where]
        return rcopy(part, part, sem.at[0, a, kind, ch], sem.at[1, a, kind, ch], target)

    def ag_send(name, ch):
        ag(name, 0, ch).start()
        ag(name, 1, ch).start()

    def ag_forward(name, ch):
        ag(name, 0, ch).wait_recv()
        ag(name, 2, ch).start()

    def ag_arrive(name, k):
        for ch in range(CHUNKS):
            if k == 1:
                ag(name, 1, ch).wait_recv()
            elif k == 2:
                ag_forward(name, ch)
            else:
                ag(name, 2, ch).wait_recv()

    def ag_drain(name):
        for kind in range(3):
            for ch in range(CHUNKS):
                ag(name, kind, ch).wait_send()

    def rs_bufs(tag):
        if tag == 3:
            return r.msy, r.mry, r.keepy, r.ysy, r.yry
        return r.msc, r.mrc, r.keepc, r.ysc, r.yrc

    def rs_m(tag, i):
        ms, mr, _, _, _ = rs_bufs(tag)
        sem = r.rs_sem
        return rcopy(ms.at[i], mr.at[i], sem.at[0, tag, i], sem.at[1, tag, i], mate)

    def rs_y(tag, ch):
        _, _, _, ys, yr = rs_bufs(tag)
        sem = r.rs_sem
        where = pl.ds(ch * CR, CR)
        return rcopy(ys.at[where], yr.at[where], sem.at[0, tag, 2 + ch], sem.at[1, tag, 2 + ch], ynb)

    def rs_put(tag, k, value, at=None):
        ms, _, keep, _, _ = rs_bufs(tag)
        where = slice(None) if at is None else at
        i = 0 if k >= 2 else 1
        if k % 2:
            ms[i, where] = value.astype(BF)
        else:
            keep[i, where] = value

    def rs_ship(tag):
        _, mr, keep, ys, _ = rs_bufs(tag)
        rs_m(tag, 0).wait_recv()
        for ch in range(CHUNKS):

            def one(s, _):
                at = rows(ch * CR + s * STEP, STEP)
                ys[at] = (keep[0, at] + mr[0, at].astype(F32)).astype(BF)
                return 0

            lax.fori_loop(0, CR // STEP, one, 0)
            rs_y(tag, ch).start()

    def rs_total(tag, at):
        _, mr, keep, _, yr = rs_bufs(tag)
        return keep[1, at] + mr[1, at].astype(F32) + yr[at].astype(F32)

    def rs_drain(tag):
        for i in range(2):
            rs_m(tag, i).wait_send()
        for ch in range(CHUNKS):
            rs_y(tag, ch).wait_send()

    GR = {name: "g" + name for name in WG}

    def gr_x(name, k):
        sem = r.gr_sem
        a = WG.index(name)
        slot = wslot(name, r[GR[name]], 2 * k + 1 - xx)
        return rcopy(slot, r[name + "_xr"].at[k], sem.at[0, a, k], sem.at[1, a, k], xnb)

    def gr_z(name, i):
        sem = r.gr_sem
        a = WG.index(name)
        to_mid, to_end = dev(2 * far_mid + xx, t), dev(2 * far_end + xx, t)
        if name == PROJ:
            to, source = (near_dev, to_mid, to_end)[i], i
            recv = 0 if i == 0 else jnp.where(middle, 1, 2)
        else:
            to = {0: near_dev, 2: near_dev, 3: near_dev, 1: to_mid, 4: to_end}[i]
            source = {0: 0, 2: 1, 3: 2, 1: 1, 4: 2}[i]
            recv = 1 if i == 4 else i
        part = r[name + "_zs"].at[source]
        return rcopy(part, r[name + "_zr"].at[recv], sem.at[0, a, NZ + i], sem.at[1, a, NZ + recv], to)

    def gr_zin(name, i):
        sem = r.gr_sem
        a = WG.index(name)
        part = r[name + "_zr"].at[i]
        return rcopy(part, part, sem.at[0, a, NZ], sem.at[1, a, NZ + i], near_dev)

    def gr_start(name):
        for k in range(NZ):
            gr_x(name, k).start()

    def gr_pair(name, to):
        mine = wslot(name, r[GR[name]], 2 * to + xx)[...].astype(F32)
        return mine + r[name + "_xr"][to].astype(F32)

    def gr_mid(name):
        for k in range(NZ):
            gr_x(name, k).wait_recv()
        zs = r[name + "_zs"]
        zs[0] = gr_pair(name, near).astype(BF)
        gr_z(name, 0).start()
        if name == PROJ:
            for i in (1, 2):
                zs[i] = gr_pair(name, Z_FROM[i]).astype(BF)
                gr_z(name, i).start()
            return

        @pl.when(jnp.logical_not(middle))
        def _():
            zs[1] = gr_pair(name, far_mid).astype(BF)
            gr_z(name, 2).start()
            zs[2] = gr_pair(name, far_end).astype(BF)
            gr_z(name, 3).start()

    def gr_far(name):
        @pl.when(middle)
        def _():
            zs, zr = r[name + "_zs"], r[name + "_zr"]
            gr_zin(name, 2).wait_recv()
            zs[1] = (gr_pair(name, far_mid) + zr[2].astype(F32)).astype(BF)
            gr_z(name, 1).start()
            gr_zin(name, 3).wait_recv()
            zs[2] = (gr_pair(name, far_end) + zr[3].astype(F32)).astype(BF)
            gr_z(name, 4).start()

    def gr_finish(name):
        total = gr_pair(name, z)
        for i in range(3 if name == PROJ else 2):
            gr_zin(name, i).wait_recv()
            total = total + r[name + "_zr"][i].astype(F32)
        return total

    def gr_drain(name):
        for k in range(NZ):
            gr_x(name, k).wait_send()
        gr_z(name, 0).wait_send()
        if name == PROJ:
            gr_z(name, 1).wait_send()
            gr_z(name, 2).wait_send()
            return

        @pl.when(middle)
        def _():
            gr_z(name, 1).wait_send()
            gr_z(name, 4).wait_send()

        @pl.when(jnp.logical_not(middle))
        def _():
            gr_z(name, 2).wait_send()
            gr_z(name, 3).wait_send()

    tpeers = [mate, ynb, ymate]
    SHARED = (32, 16)

    def sm_t(tag, i):
        sem = r.sm_sem
        part = slabs[tag].at[t]
        return rcopy(part, part, sem.at[0, tag, i], sem.at[1, tag, i], tpeers[i])

    def sm_h(tag, k):
        sem = r.sm_sem
        part = hslabs[tag].at[hi]
        return rcopy(part, part, sem.at[0, tag, 3 + k], sem.at[1, tag, 3 + k], dev((hi + k) % n, t))

    def spread(tag, at, value):
        for j in range(value.shape[1] // 128):
            slabs[tag][t, at + j : at + j + 1] = value[:, j * 128 : (j + 1) * 128]

    def sm_start(tag):
        for i in range(3):
            sm_t(tag, i).start()

    def sm_mid(tag):
        for i in range(3):
            sm_t(tag, i).wait_recv()
        slab, hslab = slabs[tag], hslabs[tag]
        total = slab[0]
        for i in range(1, 4):
            total = total + slab[i]
        if tag == 0:
            keep = lax.broadcasted_iota(jnp.int32, total.shape, 0) < SHARED[0]
            total = jnp.where(keep, total, slab[t])
        hslab[hi] = total
        for k in range(1, n):
            sm_h(tag, k).start()

    def sm_finish(tag):
        for k in range(1, n):
            sm_h(tag, k).wait_recv()
        hslab = hslabs[tag]
        total = hslab[0]
        for k in range(1, n):
            total = total + hslab[k]
        return total

    def sm_drain(tag):
        for i in range(3):
            sm_t(tag, i).wait_send()
        for k in range(1, n):
            sm_h(tag, k).wait_send()

    def fold(value):
        return jnp.sum(value.reshape(value.shape[0] // 8, 8, value.shape[1]), axis=0)

    for slab in slabs:
        slab[t] = jnp.zeros(slab.shape[1:], F32)
    r.acc[...] = jnp.zeros_like(r.acc)
    r.acc_f[...] = jnp.zeros_like(r.acc_f)
    r.acc_a[...] = jnp.zeros_like(r.acc_a)
    r.acc_b[...] = jnp.zeros_like(r.acc_b)

    if inside:
        for k in range(1, n):
            a2a_in_copy(0, k).wait_recv()
    for name in STRAIGHT:
        wg_z(name, 1).start()
        wg_z(name, 2).start()

    def norm_step(values, at, gain, bias, cen, scale):
        mean = jnp.mean(values, axis=1, keepdims=True)
        var = jnp.mean(values * values, axis=1, keepdims=True) - mean * mean
        inv = lax.rsqrt(var + EPSILON)
        centered = (values - mean) * inv
        cen[at] = centered
        scale[at] = inv
        return (centered * gain + bias).astype(BF)

    def norm_back(grad, at, gain, cen, scale, acc_at):
        centered = cen[at]
        r.acc[acc_at] += fold(grad * centered)
        r.acc[acc_at + 1] += fold(grad)
        scaled = grad * gain
        return scale[at] * (
            scaled
            - jnp.mean(scaled, axis=1, keepdims=True)
            - centered * jnp.mean(scaled * centered, axis=1, keepdims=True)
        )

    for ch in range(CHUNKS):

        def one(s, _):
            at = rows(ch * CR + s * STEP, STEP)
            values = r.came[0, at].astype(F32)
            r.h1[rows(t * B + ch * CR + s * STEP, STEP)] = norm_step(
                values, at, r.vecs[0:1], r.vecs[1:2], r.cen1, r.scale1
            )
            return 0

        lax.fori_loop(0, CR // STEP, one, 0)
        ag_send(H1, ch)

    for name in STRAIGHT:
        wg_first(name)
    wg_second(PAIR)
    ag_arrive(H1, 1)
    ag_arrive(H1, 2)
    wg_second(LAST)
    wg_second(OUT)
    if inside:
        for k in range(1, n):
            a2a_in_copy(1, k).start()
    wg_start(FC)
    wg_wait(PAIR)
    wg_wait(LAST)

    lane = lax.broadcasted_iota(jnp.int32, (1, PW), 1)

    def head_mask(h):
        return (lane >= h * HEAD_DIM) & (lane < (h + 1) * HEAD_DIM)

    def project(s, _):
        @pl.when(s == 3)
        def _():
            ag_arrive(H1, 3)

        b = block_of(s)
        at = rows(b * B, B)
        hidden = r.h1[at]

        def scaled(q):
            return (q.astype(BF).astype(F32) * HEAD_DIM ** (-0.5)).astype(BF)

        both = dot(hidden, r.wa[...], NN)
        q = scaled(both[:, :PW] + r.qvb[0:1, :PW])
        for h in range(NH - 1):
            r.qa[b, h * B : (h + 1) * B] = jnp.where(head_mask(h), q, jnp.zeros_like(q))
        k = both[:, PW : 2 * PW]
        r.ka[at] = k.astype(BF)
        r.kt[:PW, at] = k.T.astype(BF)
        v = both[:, 2 * PW :] + r.qvb[1:2, :PW]
        r.va[at] = v.astype(BF)
        r.vt[:PW, at] = v.T.astype(BF)
        last = dot(hidden, r.wb[...], NN)
        r.qb[b] = scaled(last[:, :LW] + r.qvb[0:1, PW:])
        r.kb[at] = last[:, LW : 2 * LW].astype(BF)
        r.vb[at] = (last[:, 2 * LW :] + r.qvb[1:2, PW:]).astype(BF)
        turned = last.T
        r.kt[PW:, at] = turned[LW : 2 * LW].astype(BF)
        r.vt[PW:, at] = (turned[2 * LW :] + r.vbt[...]).astype(BF)
        return 0

    bias_last = jnp.concatenate([r.qvb[1:2, PW:], jnp.zeros((1, LW), F32)], axis=1)
    r.vbt[...] = jnp.broadcast_to(bias_last, (8, 2 * LW)).T[:LW, :1]
    lax.fori_loop(0, 4, project, 0)
    wg_start(PROJ)

    def own_grad(s, _):
        at = rows(s * STEP, STEP)
        value = r.came[1, at]
        r.gf[rows(t * B + s * STEP, STEP)] = value
        r.acc[5] += fold(value.astype(F32))
        return 0

    def grad_in():
        if inside:
            for k in range(1, n):
                a2a_in_copy(1, k).wait_recv()
        lax.fori_loop(0, B // STEP, own_grad, 0)
        for ch in range(CHUNKS):
            ag_send(GF, ch)


    pack = hi * (packs // n) + lo

    def attend(i):
        pos = i * B + lax.broadcasted_iota(jnp.int32, (1, B), 1)
        first = jnp.zeros((1, B), jnp.int32)
        end = jnp.int32(0)
        for s in range(r.lengths.shape[0]):
            length = r.lengths[s, pack]
            end = end + length
            first = first + jnp.where(pos >= end, length, 0)

        def scores(j, peak):
            key_pos = j * KB + lax.broadcasted_iota(jnp.int32, (KB, B), 0)
            allowed = (key_pos >= first) & (key_pos <= pos)
            kr = rows(j * KB, KB)
            keys, keys_last = r.ka[kr], r.kb[kr]
            peaks = []
            for h in range(NH):
                if h < NH - 1:
                    raw = dot(keys, r.qa[i, h * B : (h + 1) * B], NT)
                else:
                    raw = dot(keys_last, r.qb[i], NT)
                raw = jnp.where(allowed, raw, MASKED)
                r.score[kr, h * B : (h + 1) * B] = raw
                peaks.append(jnp.max(raw, axis=0, keepdims=True))
            return jnp.maximum(peak, jnp.concatenate(peaks, axis=1))

        peak = lax.fori_loop(0, (i + KS) // KS, scores, jnp.full((1, NH * B), MASKED, F32))
        r.att[...] = jnp.zeros_like(r.att)

        def weigh(j, total):
            totals = []
            for h in range(NH):
                cols = slice(h * B, (h + 1) * B)
                weight = jnp.exp(r.score[rows(j * KB, KB), cols] - peak[:, cols])
                totals.append(jnp.sum(weight, axis=0, keepdims=True))
                low = weight.astype(BF)
                r.e[i, rows(j * KB, KB), cols] = low
                part = slice(h * HEAD_DIM, (h + 1) * HEAD_DIM)
                r.att[part] += dot(r.vt[part, rows(j * KB, KB)], low, NN)
            return total + jnp.concatenate(totals, axis=1)

        total = lax.fori_loop(0, (i + KS) // KS, weigh, jnp.zeros((1, NH * B), F32))
        inverse = 1.0 / total
        for h in range(NH):
            part = slice(h * HEAD_DIM, (h + 1) * HEAD_DIM)
            own = inverse[:, h * B : (h + 1) * B]
            r.att[part] = r.att[part] * own
            r.inv[i, h : h + 1] = own
        out = r.att[...].T
        at = rows(i * B, B)
        r.a[at] = out
        r.al[at] = out.astype(BF)

    def attend_step(s, _):
        k = 3 - s
        i = block_of(k)
        attend(i)

        @pl.when(s == 0)
        def _():
            wg_wait(OUT)

        part = dot(r.al[rows(i * B, B)], r.wo[...], NT)

        @pl.when(s == 0)
        def _():
            rs_put(0, 3, part)
            rs_m(0, 0).start()
            grad_in()

        @pl.when(s == 1)
        def _():
            rs_put(0, 2, part)
            rs_ship(0)

        @pl.when(s == 2)
        def _():
            rs_put(0, 1, part)
            rs_m(0, 1).start()
            wg_first(FC)

        @pl.when(s == 3)
        def _():
            rs_put(0, 0, part)

        return 0

    lax.fori_loop(0, 4, attend_step, 0)
    wg_second(FC)
    ag_arrive(GF, 1)
    ag_arrive(GF, 2)
    wg_first(PROJ)

    rs_m(0, 1).wait_recv()
    for ch in range(CHUNKS):
        rs_y(0, ch).wait_recv()

        def one(s, _):
            at = rows(ch * CR + s * STEP, STEP)
            values = r.came[0, at].astype(F32) + rs_total(0, at) + r.vecs[2:3]
            r.res[at] = values
            r.h2[rows(t * B + ch * CR + s * STEP, STEP)] = norm_step(
                values, at, r.vecs[3:4], r.vecs[4:5], r.cen2, r.scale2
            )
            return 0

        lax.fori_loop(0, CR // STEP, one, 0)
        ag_send(H2, ch)
    rs_drain(0)
    wg_second(PROJ)
    ag_arrive(GF, 3)
    wg_wait(FC)
    wg_wait(PROJ)

    def feed(s, _):
        @pl.when(s == 1)
        def _():
            ag_arrive(H2, 1)

        @pl.when(s == 2)
        def _():
            ag_arrive(H2, 2)

        @pl.when(s == 3)
        def _():
            ag_arrive(H2, 3)

        at = block_rows(s)
        hidden = r.h2[at]
        grad = r.gf[at]
        for j in range(FH // 256):
            cols = slice(j * 256, (j + 1) * 256)
            u = dot(hidden, r.w1[:, cols], NN) + r.vecs[6:7, cols]
            dz = dot(grad, r.w2[:, cols], NN)
            square = u * u
            half = 0.5 + 0.5 * jnp.tanh(u * (CURVE + (CURVE * CUBE) * square))
            act = u * half
            r.zz[at, cols] = act.astype(BF)
            slope = half + act * (1.0 - half) * (2.0 * CURVE + (6.0 * CURVE * CUBE) * square)
            low = (dz * slope).astype(BF)
            r.du[at, cols] = low
            r.acc_f[:, cols] += fold(low.astype(F32))
        part = dot(r.du[at], r.w1[...], NT)

        @pl.when(s == 0)
        def _():
            rs_put(1, 0, part)

        @pl.when(s == 1)
        def _():
            rs_put(1, 1, part)
            rs_m(1, 1).start()

        @pl.when(s == 2)
        def _():
            rs_put(1, 2, part)

        @pl.when(s == 3)
        def _():
            rs_put(1, 3, part)
            rs_m(1, 0).start()

        return 0

    lax.fori_loop(0, 4, feed, 0)
    rs_ship(1)

    def grad_tiles(left, right, out, form=TN):
        def one(i, _):
            at = rows(i * 256, 256)
            out[at] = dot(left[:, at], right[...], form).astype(BF)
            return 0

        lax.fori_loop(0, D // 256, one, 0)

    grad_tiles(r.gf, r.zz, r.gw2)
    gr_start(PROJ)
    grad_tiles(r.h2, r.du, r.gw1)

    rs_m(1, 1).wait_recv()
    for ch in range(CHUNKS):
        rs_y(1, ch).wait_recv()

        def one(s, _):
            at = rows(ch * CR + s * STEP, STEP)
            back = norm_back(rs_total(1, at), at, r.vecs[3:4], r.cen2, r.scale2, 2)
            grad = r.came[1, at].astype(F32) + back
            r.dres[at] = grad
            r.acc[4] += fold(grad)
            r.dr[rows(t * B + ch * CR + s * STEP, STEP)] = grad.astype(BF)
            return 0

        lax.fori_loop(0, CR // STEP, one, 0)
        ag_send(DR, ch)
    rs_drain(1)

    def upper(s, _):
        k = 3 - s
        part = dot(r.zz[block_rows(k)], r.w2[...], NT)

        @pl.when(s == 0)
        def _():
            rs_put(3, 3, part)
            rs_m(3, 0).start()

        @pl.when(s == 1)
        def _():
            rs_put(3, 2, part)

        @pl.when(s == 2)
        def _():
            rs_put(3, 1, part)
            rs_m(3, 1).start()

        @pl.when(s == 3)
        def _():
            rs_put(3, 0, part)

        return 0

    lax.fori_loop(0, 4, upper, 0)
    gr_start(FC)

    PASS = (
        (0, PW, NH - 1, r.qa, r.ka, r.va, r.dama, r.dka, r.dva, r.dqa),
        (PW, LW, 1, r.qb, r.kb, r.vb, r.damb, r.dkb, r.dvb, r.dqb),
    )

    def attend_back(which, s):
        first, width, heads, q, k, v, dam, dk, dv, dqkv = PASS[which]
        cols = slice(first, first + width)
        i = block_of(s)
        at = rows(i * B, B)
        da = dot(r.dr[at], r.wo[:, cols], NN).astype(BF).astype(F32)
        by_row = r.inv[i].T
        if which == 0:
            scale = by_row[:, heads - 1 : heads]
            for h in range(heads - 1):
                scale = jnp.where(head_mask(h), by_row[:, h : h + 1], scale)
        else:
            scale = by_row[:, NH - 1 : NH]
        low = (da * scale).astype(BF)
        for h in range(heads):
            dam[h * B : (h + 1) * B] = (
                jnp.where(head_mask(h), low, jnp.zeros_like(low)) if which == 0 else low
            )
        if which == 0:
            lined = (low.astype(F32) * r.a[at, :PW]).T
        else:
            both = low.astype(F32) * r.a[at, PW:]
            lined = jnp.concatenate([both, both], axis=1).T
        deltas = [
            jnp.sum(lined[h * HEAD_DIM : (h + 1) * HEAD_DIM], axis=0, keepdims=True)
            for h in range(heads)
        ]
        r.att[cols] = jnp.zeros((width, B), F32)

        def over_keys(j, _):
            kr = rows(j * KB, KB)
            values = v[kr]
            base = first // HEAD_DIM * B
            for h in range(heads):
                own = slice(h * B, (h + 1) * B)
                dp = dot(values, dam[own], NT)
                weight = r.e[i, kr, base + h * B : base + (h + 1) * B]
                ds = (weight.astype(F32) * (dp - deltas[h])).astype(BF)
                r.ds[:, own] = ds
                part = slice(first + h * HEAD_DIM, first + (h + 1) * HEAD_DIM)
                r.att[part] += dot(r.kt[part, kr], ds, NN)
            dk[kr] += dot(r.ds[:, : heads * B], q[i], NN)
            dv[kr] += dot(r.e[i, kr, base : base + heads * B], dam[...], NN)
            return 0

        lax.fori_loop(0, (i + KS) // KS, over_keys, 0)
        if which == 0:
            dq = r.att[cols].T
        else:
            dq = jnp.concatenate([r.att[cols], r.att[cols]], axis=0).T[:, :width]
        dqkv[at, :width] = (dq * HEAD_DIM ** (-0.5)).astype(BF)

    def round_kv(which):
        first, width, _, _, _, _, _, dk, dv, dqkv = PASS[which]

        def one(b, _):
            at = rows(b * B, B)
            dqkv[at, width : 2 * width] = dk[at].astype(BF)
            dqkv[at, 2 * width :] = dv[at].astype(BF)
            acc = (r.acc_a, r.acc_b)[which]
            acc[...] += fold(dqkv[at].astype(F32))
            return 0

        lax.fori_loop(0, 4, one, 0)

    for zeroed in (r.dka, r.dva, r.dkb, r.dvb):
        zeroed[...] = jnp.zeros_like(zeroed)

    def pair_step(s, _):
        @pl.when(s == 1)
        def _():
            ag_arrive(DR, 1)

        @pl.when(s == 2)
        def _():
            ag_arrive(DR, 2)
            rs_ship(3)
            gr_mid(PROJ)

        @pl.when(s == 3)
        def _():
            ag_arrive(DR, 3)
            grad_tiles(r.dr, r.al, r.gwo)
            gr_start(OUT)

        attend_back(0, s)
        return 0

    lax.fori_loop(0, 4, pair_step, 0)
    round_kv(0)
    grad_tiles(r.h1, r.dqa, r.gwa)
    gr_start(PAIR)

    def upper_back():
        rs_m(3, 1).wait_recv()
        for ch in range(CHUNKS):
            rs_y(3, ch).wait_recv()

        def finish_up(s, _):
            at = rows(s * STEP, STEP)
            r.made[0, at] = (r.res[at] + rs_total(3, at) + r.vecs[5:6]).astype(BF)
            return 0

        lax.fori_loop(0, B // STEP, finish_up, 0)
        if inside:
            for k in range(1, n):
                a2a_out_copy(0, k).start()
            r.back0[hi] = r.made[0, rows(hi * PR, PR)]
        else:
            r.out_y_v[...] = r.made[0]

    def last_step(s, _):
        attend_back(1, s)

        @pl.when(s == 1)
        def _():
            gr_mid(FC)

        @pl.when(s == 2)
        def _():
            upper_back()

        return 0

    lax.fori_loop(0, 4, last_step, 0)
    round_kv(1)
    gr_mid(OUT)

    def lower(s, _):
        k = 3 - s
        at = block_rows(k)
        part = dot(r.dqa[at], r.wa[...], NT) + dot(r.dqb[at], r.wb[...], NT)

        @pl.when(s == 0)
        def _():
            rs_put(2, 3, part)
            rs_m(2, 0).start()

        @pl.when(s == 1)
        def _():
            rs_put(2, 2, part)
            rs_ship(2)

        @pl.when(s == 2)
        def _():
            rs_put(2, 1, part)
            rs_m(2, 1).start()

        @pl.when(s == 3)
        def _():
            rs_put(2, 0, part)

        return 0

    lax.fori_loop(0, 4, lower, 0)

    grad_tiles(r.h1, r.dqb, r.gwb)
    gr_start(LAST)
    gr_mid(PAIR)
    gr_far(FC)
    gr_far(OUT)

    def line(value):
        return jnp.sum(value, axis=0, keepdims=True)

    for j, at in enumerate((5, 2, 3, 4)):
        spread(0, 8 * j, line(r.acc[at]))
    spread(0, 32, line(r.acc_f[...]))
    pad = jnp.zeros((1, 256 - HC), F32)
    pair, last = line(r.acc_a[...]), line(r.acc_b[...])
    for j in range(2):
        spread(0, 40 + 2 * j, pair[:, 2 * j * PW : (2 * j + 1) * PW])
        r.slab0[t, 41 + 2 * j : 42 + 2 * j, :LW] = last[:, 2 * j * LW : (2 * j + 1) * LW]
    sm_start(0)

    rs_m(2, 1).wait_recv()
    sm_mid(0)
    gr_far(PAIR)
    gr_mid(LAST)
    for ch in range(CHUNKS):
        rs_y(2, ch).wait_recv()

        def one(s, _):
            at = rows(ch * CR + s * STEP, STEP)
            back = norm_back(rs_total(2, at), at, r.vecs[0:1], r.cen1, r.scale1, 0)
            r.made[1, at] = (r.dres[at] + back).astype(BF)
            return 0

        lax.fori_loop(0, CR // STEP, one, 0)
    rs_drain(2)
    rs_drain(3)
    if inside:
        for k in range(1, n):
            a2a_out_copy(1, k).start()
        r.back1[hi] = r.made[1, rows(hi * PR, PR)]
    else:
        r.out_x_v[...] = r.made[1]
    for j in range(2):
        spread(1, 8 * j, line(r.acc[j]))
    sm_start(1)
    sm_mid(1)
    gr_far(LAST)

    OUTS = tuple(outputs(cfg))

    def store(name):
        return pltpu.make_async_copy(r[name + "_v"], r[name], r.store_sem.at[OUTS.index(name)])

    def put_back(tag, out):
        for k in range(1, n):
            a2a_out_copy(tag, k).wait_recv()

        def one(j, _):
            out[j] = backs[tag][r.order[j]]
            return 0

        lax.fori_loop(0, n, one, 0)

    r.out_w2_v[...] = gr_finish(PROJ)
    store(OUT_W2).start()
    r.out_w1_v[...] = gr_finish(FC)
    store(OUT_W1).start()
    if inside:
        put_back(0, r.out_y_v)
    store(OUT_Y).start()
    r.turn[...] = jnp.zeros_like(r.turn)
    r.turn[:WR, :HC] = gr_finish(OUT)
    r.out_wo_v[...] = r.turn[...].T[:HC, :WR]
    store(OUT_WO).start()
    r.out_early_v[...] = sm_finish(0)
    store(OUT_EARLY).start()
    if inside:
        put_back(1, r.out_x_v)
    store(OUT_X).start()
    r.out_late_v[...] = sm_finish(1)
    store(OUT_LATE).start()
    total = gr_finish(PAIR)
    for i in range(3):
        r.out_qkv_v[i, :, :PW] = total[:, i * PW : (i + 1) * PW]
    total = gr_finish(LAST)
    for i in range(3):
        r.out_qkv_v[i, :, PW:] = total[:, i * LW : (i + 1) * LW]
    store(OUT_QKV).start()

    for name in WG:
        wg_drain(name)
        gr_drain(name)
    for name in AG:
        ag_drain(name)
    for name in OUTS:
        store(name).wait()
    for tag in range(2):
        sm_drain(tag)
        if inside:
            for k in range(1, n):
                a2a_in_copy(tag, k).wait_send()
                a2a_out_copy(tag, k).wait_send()


def settle(*refs):
    early, late = refs[6:8]
    whole, small = refs[8:14], refs[14:22]
    for i in range(6):
        whole[i][...] = refs[i][...]
    for j in range(4):
        small[j][...] = early[8 * j : 8 * j + small[j].shape[0]]
    for j in range(2):
        small[4 + j][...] = late[8 * j : 8 * j + small[4 + j].shape[0]]
    small[6][...] = early[32 : 32 + small[6].shape[0]]
    heads = small[7]
    for j in range(2):
        heads[j : j + 1, :128] = early[40 + 2 * j : 41 + 2 * j]
        heads[j : j + 1, 128:] = early[41 + 2 * j : 42 + 2 * j, : heads.shape[1] - 128]


def inputs():
    vmem = pl.BlockSpec(memory_space=pltpu.VMEM)
    smem = pl.BlockSpec(memory_space=pltpu.SMEM)
    hbm = pl.BlockSpec(memory_space=pl.ANY)
    return Refs(
        order=smem,
        lengths=smem,
        x_hbm=hbm,
        g_hbm=hbm,
        ln1g=vmem,
        ln1b=vmem,
        wqkv_hbm=hbm,
        qvb=vmem,
        wo_hbm=hbm,
        aob=vmem,
        ln2g=vmem,
        ln2b=vmem,
        w1_hbm=hbm,
        fcb=vmem,
        w2_hbm=hbm,
        pjb=vmem,
    )


def outputs(cfg):
    (n, packs, L, S, D, HC, FH, inside) = cfg
    WR = D // n
    tokens = (n, L // n, D) if inside else (L, D)
    return Refs(
        out_y=(tokens, BF),
        out_x=(tokens, BF),
        out_qkv=((3, WR, HC), F32),
        out_wo=((HC, WR), F32),
        out_w1=((WR, FH), F32),
        out_w2=((WR, FH), F32),
        out_early=((48, 128), F32),
        out_late=((16, 128), F32),
    )


def scratch(cfg):
    (n, packs, L, S, D, HC, FH, inside) = cfg
    NH = HC // HEAD_DIM
    LW = HEAD_DIM
    PW = HC - LW
    NZ = n // 2
    WR = D // n
    V = pltpu.VMEM
    sem = pltpu.SemaphoreType.DMA
    blocks = S // L
    tokens = (n, L // n, D) if inside else (L, D)
    kind = F32 if inside else BF
    made = Refs(
        came=V((2, L, D), BF),
        made=V((2, L, D), BF),
        wa=V((D, 3 * PW), BF),
        wb=V((D, 3 * LW), BF),
        wo=V((D, HC), BF),
        w1=V((D, FH), BF),
        w2=V((D, FH), BF),
        turn=V((256, 256), F32),
        vecs=V((8, D), F32),
        x_in=V(tokens, BF),
        g_in=V(tokens, BF),
        wqkv_in=V((3, WR, HC), kind),
        wo_in=V((HC, WR), kind),
        w1_in=V((WR, FH), kind),
        w2_in=V((WR, FH), kind),
        load_sem=sem((6,)),
        store_sem=sem((8,)),
        h1=V((S, D), BF),
        gf=V((S, D), BF),
        h2=V((S, D), BF),
        dr=V((S, D), BF),
        cen1=V((L, D), F32),
        cen2=V((L, D), F32),
        scale1=V((L, 1), F32),
        scale2=V((L, 1), F32),
        res=V((L, D), F32),
        dres=V((L, D), F32),
        qa=V((blocks, (NH - 1) * L, PW), BF),
        ka=V((S, PW), BF),
        va=V((S, PW), BF),
        qb=V((blocks, L, LW), BF),
        kb=V((S, LW), BF),
        vb=V((S, LW), BF),
        vbt=V((LW, 1), F32),
        kt=V((HC, S), BF),
        vt=V((HC, S), BF),
        score=V((S, NH * L), F32),
        e=V((blocks, S, NH * L), BF),
        att=V((HC, L), F32),
        inv=V((blocks, 8, L), F32),
        a=V((S, HC), F32),
        al=V((S, HC), BF),
        dama=V(((NH - 1) * L, PW), BF),
        damb=V((L, LW), BF),
        ds=V((2 * L, NH * L), BF),
        dka=V((S, PW), F32),
        dva=V((S, PW), F32),
        dkb=V((S, LW), F32),
        dvb=V((S, LW), F32),
        dqa=V((S, 3 * PW), BF),
        dqb=V((S, 3 * LW), BF),
        zz=V((S, FH), BF),
        du=V((S, FH), BF),
        acc=V((6, 8, D), F32),
        acc_f=V((8, FH), F32),
        acc_a=V((8, 3 * PW), F32),
        acc_b=V((8, 3 * LW), F32),
        slab0=V((4, 48, 128), F32),
        slab1=V((4, 16, 128), F32),
        hslab0=V((n, 48, 128), F32),
        hslab1=V((n, 16, 128), F32),
    )
    for name, (shape, dtype) in outputs(cfg).items():
        made[name + "_v"] = V(shape, dtype)
    if inside:
        made.update(
            sent=V((2, n, L // n, D), BF),
            back0=V((n, L // n, D), BF),
            back1=V((n, L // n, D), BF),
            a2a_sem=sem((2, 4, n - 1)),
        )
    for late in "cy":
        made["ms" + late] = V((2, L, D), BF)
        made["mr" + late] = V((2, L, D), BF)
        made["keep" + late] = V((2, L, D), F32)
        made["ys" + late] = V((L, D), BF)
        made["yr" + late] = V((L, D), BF)
    for name, width in ((PAIR, 3 * PW), (LAST, 3 * LW), (OUT, HC), (FC, FH), (PROJ, FH)):
        slot = (WR, width)
        made["g" + name] = V(slot[:-2] + (D, slot[-1]), BF)
        made[name + "_xr"] = V((NZ,) + slot, BF)
        made[name + "_zs"] = V((NZ - 1,) + slot, BF)
        made[name + "_zr"] = V((NZ,) + slot, BF)
    made.update(
        wg_sem=sem((2, 5, 2 * NZ)),
        gr_sem=sem((2, 5, 2 * NZ + 1)),
        ag_sem=sem((2, 4, 3, CHUNKS)),
        rs_sem=sem((2, 4, 2 + CHUNKS)),
        sm_sem=sem((2, 2, 3 + n)),
    )
    return made


def cfg_names(cfg):
    return tuple(inputs()) + tuple(outputs(cfg)) + tuple(scratch(cfg))


def local(
    n,
    block_input,
    out_cotangent,
    seq_lengths,
    pack_order,
    ln1_gain,
    ln1_bias,
    qkv_weight,
    qv_bias,
    attn_out_weight,
    attn_out_bias,
    ln2_gain,
    ln2_bias,
    fc_weight,
    fc_bias,
    proj_weight,
    proj_bias,
):
    L, D = block_input.shape
    packs = pack_order.shape[0]
    HC = qv_bias.shape[1]
    FH = fc_bias.shape[0]
    S = L * lax.axis_size("tensor")
    outer = packs // n
    inside = outer == 1
    cfg = (n, packs, L, S, D, HC, FH, inside)
    tokens = (block_input, out_cotangent)
    weights = (qkv_weight, attn_out_weight, fc_weight, proj_weight)
    if inside:
        tokens = [v.reshape(n, L // n, D) for v in tokens]
    else:
        slots = jnp.arange(packs, dtype=jnp.int32)
        chosen = (pack_order[None, :] == slots[:, None]).astype(BF)

        def pick(which, v):
            return (
                jnp.dot(which, v.reshape(packs, -1), preferred_element_type=F32)
                .astype(BF)
                .reshape(L, D)
            )

        tokens = [
            lax.all_to_all(
                pick(chosen, v), ("hi", "lo"), split_axis=0, concat_axis=0, tiled=True
            )
            for v in tokens
        ]
        weights = [
            lax.all_gather(w.astype(BF), "lo", axis=axis, tiled=True)
            for w, axis in zip(weights, (0, 1, 0, 1))
        ]
    row = lambda v: v.reshape(-1, 128)
    outs = outputs(cfg)
    made = pl.pallas_call(
        functools.partial(kernel, cfg),
        out_shape=[jax.ShapeDtypeStruct(shape, kind) for shape, kind in outs.values()],
        in_specs=list(inputs().values()),
        out_specs=[pl.BlockSpec(memory_space=pl.ANY)] * len(outs),
        scratch_shapes=list(scratch(cfg).values()),
        compiler_params=pltpu.CompilerParams(
            collective_id=0, has_side_effects=True, vmem_limit_bytes=63 * 2**20
        ),
    )(
        pack_order,
        seq_lengths.T,
        *tokens,
        row(ln1_gain),
        row(ln1_bias),
        jnp.transpose(weights[0], (1, 0, 2)),
        qv_bias,
        weights[1],
        row(attn_out_bias),
        row(ln2_gain),
        row(ln2_bias),
        weights[2],
        row(fc_bias),
        weights[3].T,
        row(proj_bias),
    )
    g = Refs(zip(outs, made))
    if not inside:
        exchange = lambda v: pick(
            chosen.T,
            lax.all_to_all(v, ("hi", "lo"), split_axis=0, concat_axis=0, tiled=True),
        )
        share = lambda v, axis: lax.psum_scatter(v, "lo", scatter_dimension=axis, tiled=True)
        g.out_y, g.out_x = exchange(g.out_y), exchange(g.out_x)
        g.out_qkv, g.out_wo = share(g.out_qkv, 1), share(g.out_wo, 1)
        g.out_w1, g.out_w2 = share(g.out_w1, 0), share(g.out_w2, 0)
        g.out_early, g.out_late = lax.psum((g.out_early, g.out_late), "lo")
    whole = [g.out_y.reshape(L, D), g.out_x.reshape(L, D), g.out_qkv, g.out_wo, g.out_w1, g.out_w2]
    vec = D // 128
    vmem = pl.BlockSpec(memory_space=pltpu.VMEM)
    settled = pl.pallas_call(
        settle,
        out_shape=[jax.ShapeDtypeStruct(v.shape, v.dtype) for v in whole]
        + [jax.ShapeDtypeStruct((vec, 128), F32)] * 6
        + [jax.ShapeDtypeStruct((FH // 128, 128), F32), jax.ShapeDtypeStruct((2, HC), F32)],
        in_specs=[vmem] * 8,
        out_specs=[vmem] * 14,
    )(*whole, g.out_early, g.out_late)
    out_y, out_x, qkv_sum, out_sum, fc_sum, proj_sum = settled[:6]
    pjb, ln2g, ln2b, aob, ln1g, ln1b = [v.reshape(D) for v in settled[6:12]]
    return (
        out_y,
        out_x,
        ln1g,
        ln1b,
        jnp.transpose(qkv_sum, (1, 0, 2)),
        settled[13],
        out_sum,
        aob,
        ln2g,
        ln2b,
        fc_sum,
        settled[12].reshape(FH),
        proj_sum.T,
        pjb,
    )


def solution(mesh):
    groups, members = mesh.shape["dp"], mesh.shape["tensor"]
    n = min(8, groups)
    cut = Mesh(mesh.devices.reshape(n, groups // n, members), ("hi", "lo", "tensor"))
    dp = ("hi", "lo")
    return jax.shard_map(
        functools.partial(local, n),
        mesh=cut,
        in_specs=(
            P(("hi", "lo", "tensor"), None),
            P(("hi", "lo", "tensor"), None),
            P(),
            P(),
            P(),
            P(),
            P(dp, None, "tensor"),
            P(None, "tensor"),
            P("tensor", dp),
            P(),
            P(),
            P(),
            P(dp, "tensor"),
            P("tensor"),
            P("tensor", dp),
            P(),
        ),
        out_specs=(
            P(("hi", "lo", "tensor"), None),
            P(("hi", "lo", "tensor"), None),
            P(),
            P(),
            P(dp, None, "tensor"),
            P(None, "tensor"),
            P("tensor", dp),
            P(),
            P(),
            P(),
            P(dp, "tensor"),
            P("tensor"),
            P("tensor", dp),
            P(),
        ),
        check_vma=False,
    )
```

```python
import functools

import jax
import jax.numpy as jnp
from jax import lax
from jax.experimental import pallas as pl
from jax.experimental.pallas import tpu as pltpu
from jax.sharding import Mesh
from jax.sharding import PartitionSpec as P

HEAD_DIM = 64
EPSILON = 1e-05
MASKED = -1e30
BF = jnp.bfloat16
F32 = jnp.float32
MESH = pl.DeviceIdType.MESH
CURVE = 0.7978845608028654
CUBE = 0.044715

CHUNKS = 2
STEP = 32

PAIR, LAST, OUT, FC, PROJ = "wa", "wb", "wo", "w1", "w2"
QKV = "wqkv"
PROJ_Z, FC_Z = "w2z", "w1z"
ZFIRST = (PROJ_Z, FC_Z)
H1, GF, H2, DR = "h1", "gf", "h2", "dr"
X_IN, G_IN = "x", "g"
OUT_Y, OUT_X, OUT_QKV, OUT_WO = "out_y", "out_x", "out_qkv", "out_wo"
OUT_W1, OUT_W2, OUT_EARLY, OUT_LATE = "out_w1", "out_w2", "out_early", "out_late"

NN = ((1,), (0,))
NT = ((1,), (1,))
TN = ((0,), (0,))


class Refs(dict):
    __getattr__ = dict.__getitem__


def dot(left_side, right_side, form):
    return lax.dot_general(
        left_side, right_side, (form, ((), ())), preferred_element_type=F32
    )


def kernel(cfg, *refs):
    (n, packs, L, S, D, HC, FH, inside) = cfg
    names = cfg_names(cfg)
    r = Refs(zip(names, refs))
    slabs, hslabs = (r.slab0, r.slab1), (r.hslab0, r.hslab1)
    backs = (r.back0, r.back1) if inside else None
    NH = HC // HEAD_DIM
    LW = HEAD_DIM
    PW = HC - LW
    NZ = n // 2
    WR = D // n
    PR = L // n
    CR = L // CHUNKS
    B = L
    KS = 2
    KB = KS * B

    hi = lax.axis_index("hi")
    lo = lax.axis_index("lo")
    t = lax.axis_index("tensor")
    z, xx = hi // 2, hi % 2
    y, c = t // 2, t % 2
    dev = lambda h, tt: (h, lo, tt)
    mate = dev(hi, 2 * y + 1 - c)
    ynb = dev(hi, 2 * (1 - y) + c)
    ymate = dev(hi, 2 * (1 - y) + 1 - c)
    xnb = dev(2 * z + 1 - xx, t)

    def zdev(k):
        return dev(2 * ((z + k) % NZ) + xx, t)

    def block_of(k):
        return 2 * ((y + k // 2) % 2) + (c + k % 2) % 2

    def rows(start, size, mult=None):
        return pl.ds(pl.multiple_of(start, mult or size), size)

    def block_rows(k):
        return rows(block_of(k) * B, B)

    def rcopy(src, dst, send, recv, target):
        return pltpu.make_async_remote_copy(
            src_ref=src,
            dst_ref=dst,
            send_sem=send,
            recv_sem=recv,
            device_id=target,
            device_id_type=MESH,
        )

    LOADS = (X_IN, G_IN, QKV, OUT, FC, PROJ)

    def load(name):
        return pltpu.make_async_copy(r[name + "_hbm"], r[name + "_in"], r.load_sem.at[LOADS.index(name)])

    for name in LOADS:
        load(name).start()

    barrier = pltpu.get_barrier_semaphore()
    peers = [dev((hi + k) % n, t) for k in range(1, n)] + [mate, ynb, ymate]
    for peer in peers:
        pl.semaphore_signal(barrier, inc=1, device_id=peer, device_id_type=MESH)

    def a2a(tag, k, source, target):
        sem = r.a2a_sem
        to = (hi + k) % n
        return rcopy(source(to), target(hi), sem.at[0, tag, k - 1], sem.at[1, tag, k - 1], dev(to, t))

    def a2a_in_copy(tag, k):
        return a2a(
            tag,
            k,
            lambda to: r.sent.at[tag, to],
            lambda me: r.came.at[tag, rows(me * PR, PR)],
        )

    def a2a_out_copy(tag, k):
        return a2a(
            2 + tag,
            k,
            lambda to: r.made.at[tag, rows(to * PR, PR)],
            lambda me: backs[tag].at[me],
        )

    def pick_pieces(tag, source):
        def one(k, _):
            where = jnp.int32(0)
            for j in range(n):
                where = jnp.where(r.order[j] == k, j, where)
            r.sent[tag, k] = source[where]
            return 0

        lax.fori_loop(0, n, one, 0)
        r.came[tag, rows(hi * PR, PR)] = r.sent[tag, hi]

    load(X_IN).wait()
    if inside:
        pick_pieces(0, r.x_in)
    pl.semaphore_wait(barrier, len(peers))
    if inside:
        for k in range(1, n):
            a2a_in_copy(0, k).start()
    else:
        r.came[0] = r.x_in[...]
    for j, vec in enumerate((r.ln1g, r.ln1b, r.aob, r.ln2g, r.ln2b, r.pjb, r.fcb)):
        for i in range(vec.shape[0]):
            r.vecs[j : j + 1, i * 128 : (i + 1) * 128] = vec[i : i + 1]

    WG = (PAIR, LAST, OUT, FC, PROJ)
    STRAIGHT = (PAIR, LAST)
    middle = (z == 1) | (z == 2)
    side = z // 2
    near, far_mid, far_end = z + 1 - 2 * (z % 2), 2 - side, 3 - 3 * side
    Z_FROM = (near, far_mid, far_end)
    near_dev = dev(2 * near + xx, t)

    def wslot(name, ref, slot):
        return ref.at[rows(slot * WR, WR, 16)]

    def wg_z(name, i):
        sem = r.wg_sem
        a = WG.index(name)
        if i < 2:
            slot = wslot(name, r[name], hi)
            target = (near_dev, dev(2 * far_mid + xx, t))[i]
            recv = (0, jnp.where(middle, 1, 2))[i]
        elif name in STRAIGHT:
            slot = wslot(name, r[name], hi)
            target = dev(2 * far_end + xx, t)
            recv = jnp.where(middle, 1, 2)
        else:
            slot = wslot(name, r[name], 2 * Z_FROM[i - 1] + xx)
            target = near_dev
            recv = i - 1
        return rcopy(slot, slot, sem.at[0, a, i], sem.at[1, a, recv], target)

    def wg_in(name, i):
        sem = r.wg_sem
        a = WG.index(name)
        slot = wslot(name, r[name], 2 * Z_FROM[i] + xx)
        return rcopy(slot, slot, sem.at[0, a, 3], sem.at[1, a, i], near_dev)

    def wg_x(name, i):
        sem = r.wg_sem
        a = WG.index(name)
        slot = wslot(name, r[name], 2 * (Z_FROM + (z,))[i] + xx)
        return rcopy(slot, slot, sem.at[0, a, 4 + i], sem.at[1, a, 4 + i], xnb)

    def wg_near(name):
        wg_in(name, 0).wait_recv()
        wg_x(name, 0).start()

    def wg_mids(name):
        @pl.when(middle)
        def _():
            for i in (1, 2):
                wg_in(name, i).wait_recv()
                wg_z(name, i + 1).start()
                wg_x(name, i).start()

    def wg_second(name):
        if name in STRAIGHT:
            for i in (1, 2):
                wg_in(name, i).wait_recv()
                wg_x(name, i).start()
            return

        @pl.when(jnp.logical_not(middle))
        def _():
            for i in (1, 2):
                wg_in(name, i).wait_recv()
                wg_x(name, i).start()

    def wg_wait(name):
        for i in range(NZ):
            wg_x(name, i).wait_recv()

    def wg_drain(name):
        for i in range(2):
            wg_z(name, i).wait_send()
        for i in range(NZ):
            wg_x(name, i).wait_send()
        if name in STRAIGHT:
            wg_z(name, 2).wait_send()
            return

        @pl.when(middle)
        def _():
            for i in (2, 3):
                wg_z(name, i).wait_send()

    own_w = rows(hi * WR, WR, 16)
    load(QKV).wait()
    for i in range(3):
        part = r.wqkv_in[i].astype(BF)
        r.wa[own_w, i * PW : (i + 1) * PW] = part[:, :PW]
        r.wb[own_w, i * LW : (i + 1) * LW] = part[:, PW:]
    for name in (PAIR, LAST):
        wg_x(name, 3).start()
        wg_z(name, 0).start()
    for name in LOADS[3:]:
        load(name).wait()
    r.w1[own_w] = r.w1_in[...].astype(BF)
    r.w2[own_w] = r.w2_in[...].astype(BF)
    r.turn[...] = jnp.zeros_like(r.turn)
    r.turn[:HC, :WR] = r.wo_in[...].astype(F32)
    r.wo[own_w] = r.turn[...].T[:WR, :HC].astype(BF)
    for name in (OUT, FC, PROJ):
        wg_x(name, 3).start()
    wg_z(OUT, 0).start()
    load(G_IN).wait()
    if inside:
        pick_pieces(1, r.g_in)
    else:
        r.came[1] = r.g_in[...]

    AG = (H1, GF, H2, DR)

    def ag(name, kind, ch):
        sem = r.ag_sem
        a = AG.index(name)
        full = r[name]
        if kind == 2:
            where = rows(block_of(2) * B + ch * CR, CR)
        else:
            where = rows(t * B + ch * CR, CR)
        target = ynb if kind == 0 else mate
        part = full.at[where]
        return rcopy(part, part, sem.at[0, a, kind, ch], sem.at[1, a, kind, ch], target)

    def ag_send(name, ch):
        ag(name, 0, ch).start()
        ag(name, 1, ch).start()

    def ag_forward(name, ch):
        ag(name, 0, ch).wait_recv()
        ag(name, 2, ch).start()

    def ag_arrive(name, k):
        for ch in range(CHUNKS):
            if k == 1:
                ag(name, 1, ch).wait_recv()
            elif k == 2:
                ag_forward(name, ch)
            else:
                ag(name, 2, ch).wait_recv()

    def ag_drain(name):
        for kind in range(3):
            for ch in range(CHUNKS):
                ag(name, kind, ch).wait_send()

    def rs_bufs(tag):
        if tag == 3:
            return r.msy, r.mry, r.keepy, r.ysy, r.yry
        return r.msc, r.mrc, r.keepc, r.ysc, r.yrc

    def rs_m(tag, i):
        ms, mr, _, _, _ = rs_bufs(tag)
        sem = r.rs_sem
        return rcopy(ms.at[i], mr.at[i], sem.at[0, tag, i], sem.at[1, tag, i], mate)

    def rs_y(tag, ch):
        _, _, _, ys, yr = rs_bufs(tag)
        sem = r.rs_sem
        where = pl.ds(ch * CR, CR)
        return rcopy(ys.at[where], yr.at[where], sem.at[0, tag, 2 + ch], sem.at[1, tag, 2 + ch], ynb)

    def rs_put(tag, k, value, at=None):
        ms, _, keep, _, _ = rs_bufs(tag)
        where = slice(None) if at is None else at
        i = 0 if k >= 2 else 1
        if k % 2:
            ms[i, where] = value.astype(BF)
        else:
            keep[i, where] = value

    def rs_ship(tag):
        _, mr, keep, ys, _ = rs_bufs(tag)
        rs_m(tag, 0).wait_recv()
        for ch in range(CHUNKS):

            def one(s, _):
                at = rows(ch * CR + s * STEP, STEP)
                ys[at] = (keep[0, at] + mr[0, at].astype(F32)).astype(BF)
                return 0

            lax.fori_loop(0, CR // STEP, one, 0)
            rs_y(tag, ch).start()

    def rs_total(tag, at):
        _, mr, keep, _, yr = rs_bufs(tag)
        return keep[1, at] + mr[1, at].astype(F32) + yr[at].astype(F32)

    def rs_drain(tag):
        for i in range(2):
            rs_m(tag, i).wait_send()
        for ch in range(CHUNKS):
            rs_y(tag, ch).wait_send()

    GS = WG + ZFIRST
    GR = {name: "g" + name for name in GS}
    HF = FH // 2

    def gr_x(name, k):
        sem = r.gr_sem
        a = GS.index(name)
        slot = wslot(name, r[GR[name]], 2 * k + 1 - xx)
        return rcopy(slot, r[name + "_xr"].at[k], sem.at[0, a, k], sem.at[1, a, k], xnb)

    def gr_z(name, i):
        sem = r.gr_sem
        a = GS.index(name)
        to_mid, to_end = dev(2 * far_mid + xx, t), dev(2 * far_end + xx, t)
        if name in ZFIRST:
            to, source = (near_dev, to_mid, to_end)[i], i
            recv = 0 if i == 0 else jnp.where(middle, 1, 2)
        else:
            to = {0: near_dev, 2: near_dev, 3: near_dev, 1: to_mid, 4: to_end}[i]
            source = {0: 0, 2: 1, 3: 2, 1: 1, 4: 2}[i]
            recv = 1 if i == 4 else i
        part = two(name, Z_FROM[source]) if name in ZFIRST else r[name + "_zs"].at[source]
        return rcopy(part, r[name + "_zr"].at[recv], sem.at[0, a, NZ + i], sem.at[1, a, NZ + recv], to)

    def gr_zin(name, i):
        sem = r.gr_sem
        a = GS.index(name)
        part = r[name + "_zr"].at[i]
        return rcopy(part, part, sem.at[0, a, NZ], sem.at[1, a, NZ + i], near_dev)

    def two(name, place):
        return r[GR[name]].at[rows(2 * place * WR, 2 * WR, 32)]

    def z_start(name):
        for i in range(3):
            gr_z(name, i).start()

    def x_last(name):
        sem = r.gr_sem
        a = GS.index(name)
        return rcopy(r[name + "_xs"], r[name + "_xr"], sem.at[0, a, 0], sem.at[1, a, 0], xnb)

    def z_end(name, out):
        zr = r[name + "_zr"]
        came = range(3)
        for i in came:
            gr_zin(name, i).wait_recv()

        def total(k):
            value = r[GR[name]][rows((2 * z + k) * WR, WR, 16)].astype(F32)
            at = rows(k * WR, WR, 16)
            for i in came:
                value = value + zr[i, at].astype(F32)
            return value

        r[name + "_xs"][...] = total(1 - xx).astype(BF)
        x_last(name).start()
        out[:, HF:] = total(xx)

    def z_finish(name, out):
        x_last(name).wait_recv()
        out[:, HF:] += r[name + "_xr"][...].astype(F32)

    def gr_start(name):
        for k in range(NZ):
            gr_x(name, k).start()

    def gr_pair(name, to):
        mine = wslot(name, r[GR[name]], 2 * to + xx)[...].astype(F32)
        return mine + r[name + "_xr"][to].astype(F32)

    def gr_mid(name):
        for k in range(NZ):
            gr_x(name, k).wait_recv()
        zs = r[name + "_zs"]
        zs[0] = gr_pair(name, near).astype(BF)
        gr_z(name, 0).start()

        @pl.when(jnp.logical_not(middle))
        def _():
            zs[1] = gr_pair(name, far_mid).astype(BF)
            gr_z(name, 2).start()
            zs[2] = gr_pair(name, far_end).astype(BF)
            gr_z(name, 3).start()

    def gr_far(name):
        @pl.when(middle)
        def _():
            zs, zr = r[name + "_zs"], r[name + "_zr"]
            gr_zin(name, 2).wait_recv()
            zs[1] = (gr_pair(name, far_mid) + zr[2].astype(F32)).astype(BF)
            gr_z(name, 1).start()
            gr_zin(name, 3).wait_recv()
            zs[2] = (gr_pair(name, far_end) + zr[3].astype(F32)).astype(BF)
            gr_z(name, 4).start()

    def gr_finish(name):
        total = gr_pair(name, z)
        for i in range(2):
            gr_zin(name, i).wait_recv()
            total = total + r[name + "_zr"][i].astype(F32)
        return total

    def gr_drain(name):
        if name in ZFIRST:
            x_last(name).wait_send()
        else:
            for k in range(NZ):
                gr_x(name, k).wait_send()
        gr_z(name, 0).wait_send()
        if name in ZFIRST:
            gr_z(name, 1).wait_send()
            gr_z(name, 2).wait_send()
            return

        @pl.when(middle)
        def _():
            gr_z(name, 1).wait_send()
            gr_z(name, 4).wait_send()

        @pl.when(jnp.logical_not(middle))
        def _():
            gr_z(name, 2).wait_send()
            gr_z(name, 3).wait_send()

    tpeers = [mate, ynb, ymate]
    SHARED = (32, 16)

    def sm_t(tag, i):
        sem = r.sm_sem
        part = slabs[tag].at[t]
        return rcopy(part, part, sem.at[0, tag, i], sem.at[1, tag, i], tpeers[i])

    def sm_h(tag, k):
        sem = r.sm_sem
        part = hslabs[tag].at[hi]
        return rcopy(part, part, sem.at[0, tag, 3 + k], sem.at[1, tag, 3 + k], dev((hi + k) % n, t))

    def spread(tag, at, value):
        for j in range(value.shape[1] // 128):
            slabs[tag][t, at + j : at + j + 1] = value[:, j * 128 : (j + 1) * 128]

    def sm_start(tag):
        for i in range(3):
            sm_t(tag, i).start()

    def sm_mid(tag):
        for i in range(3):
            sm_t(tag, i).wait_recv()
        slab, hslab = slabs[tag], hslabs[tag]
        total = slab[0]
        for i in range(1, 4):
            total = total + slab[i]
        if tag == 0:
            keep = lax.broadcasted_iota(jnp.int32, total.shape, 0) < SHARED[0]
            total = jnp.where(keep, total, slab[t])
        hslab[hi] = total.astype(BF)
        for k in range(1, n):
            sm_h(tag, k).start()

    def sm_finish(tag):
        for k in range(1, n):
            sm_h(tag, k).wait_recv()
        hslab = hslabs[tag]
        total = hslab[0].astype(F32)
        for k in range(1, n):
            total = total + hslab[k].astype(F32)
        return total

    def sm_drain(tag):
        for i in range(3):
            sm_t(tag, i).wait_send()
        for k in range(1, n):
            sm_h(tag, k).wait_send()

    def fold(value):
        return jnp.sum(value.reshape(value.shape[0] // 8, 8, value.shape[1]), axis=0)

    for slab in slabs:
        slab[t] = jnp.zeros(slab.shape[1:], F32)
    r.acc[...] = jnp.zeros_like(r.acc)
    r.acc_f[...] = jnp.zeros_like(r.acc_f)
    r.acc_a[...] = jnp.zeros_like(r.acc_a)
    r.acc_b[...] = jnp.zeros_like(r.acc_b)

    if inside:
        for k in range(1, n):
            a2a_in_copy(0, k).wait_recv()
    for name in STRAIGHT:
        wg_z(name, 1).start()
        wg_z(name, 2).start()
    wg_z(FC, 0).start()

    def norm_step(values, at, gain, bias, cen, scale):
        mean = jnp.mean(values, axis=1, keepdims=True)
        var = jnp.mean(values * values, axis=1, keepdims=True) - mean * mean
        inv = lax.rsqrt(var + EPSILON)
        centered = (values - mean) * inv
        cen[at] = centered
        scale[at] = inv
        return (centered * gain + bias).astype(BF)

    def norm_back(grad, at, gain, cen, scale, acc_at):
        centered = cen[at]
        r.acc[acc_at] += fold(grad * centered)
        r.acc[acc_at + 1] += fold(grad)
        scaled = grad * gain
        return scale[at] * (
            scaled
            - jnp.mean(scaled, axis=1, keepdims=True)
            - centered * jnp.mean(scaled * centered, axis=1, keepdims=True)
        )

    for ch in range(CHUNKS):

        def one(s, _):
            at = rows(ch * CR + s * STEP, STEP)
            values = r.came[0, at].astype(F32)
            r.h1[rows(t * B + ch * CR + s * STEP, STEP)] = norm_step(
                values, at, r.vecs[0:1], r.vecs[1:2], r.cen1, r.scale1
            )
            return 0

        lax.fori_loop(0, CR // STEP, one, 0)
        ag_send(H1, ch)

    for name in (PAIR, LAST, OUT):
        wg_near(name)
    wg_second(PAIR)
    wg_z(OUT, 1).start()
    ag_arrive(H1, 1)
    ag_arrive(H1, 2)
    wg_second(LAST)
    if inside:
        for k in range(1, n):
            a2a_in_copy(1, k).start()
    wg_wait(PAIR)
    wg_wait(LAST)
    wg_mids(OUT)
    wg_near(FC)
    wg_z(FC, 1).start()
    wg_z(PROJ, 0).start()

    lane = lax.broadcasted_iota(jnp.int32, (1, PW), 1)

    def head_mask(h):
        return (lane >= h * HEAD_DIM) & (lane < (h + 1) * HEAD_DIM)

    def project(s, _):
        @pl.when(s == 3)
        def _():
            ag_arrive(H1, 3)

        b = block_of(s)
        at = rows(b * B, B)
        hidden = r.h1[at]

        def scaled(q):
            return (q.astype(BF).astype(F32) * HEAD_DIM ** (-0.5)).astype(BF)

        both = dot(hidden, r.wa[...], NN)
        q = scaled(both[:, :PW] + r.qvb[0:1, :PW])
        for h in range(NH - 1):
            r.qa[b, h * B : (h + 1) * B] = jnp.where(head_mask(h), q, jnp.zeros_like(q))
        k = both[:, PW : 2 * PW]
        r.ka[at] = k.astype(BF)
        r.kt[:PW, at] = k.T.astype(BF)
        v = both[:, 2 * PW :] + r.qvb[1:2, :PW]
        r.va[at] = v.astype(BF)
        r.vt[:PW, at] = v.T.astype(BF)
        last = dot(hidden, r.wb[...], NN)
        r.qb[b] = scaled(last[:, :LW] + r.qvb[0:1, PW:])
        r.kb[at] = last[:, LW : 2 * LW].astype(BF)
        r.vb[at] = (last[:, 2 * LW :] + r.qvb[1:2, PW:]).astype(BF)
        turned = last.T
        r.kt[PW:, at] = turned[LW : 2 * LW].astype(BF)
        r.vt[PW:, at] = (turned[2 * LW :] + r.vbt[...]).astype(BF)
        return 0

    bias_last = jnp.concatenate([r.qvb[1:2, PW:], jnp.zeros((1, LW), F32)], axis=1)
    r.vbt[...] = jnp.broadcast_to(bias_last, (8, 2 * LW)).T[:LW, :1]
    lax.fori_loop(0, 4, project, 0)
    wg_second(OUT)
    wg_near(PROJ)
    wg_z(PROJ, 1).start()

    def own_grad(s, _):
        at = rows(s * STEP, STEP)
        value = r.came[1, at]
        r.gf[rows(t * B + s * STEP, STEP)] = value
        r.acc[5] += fold(value.astype(F32))
        return 0

    def grad_in():
        if inside:
            for k in range(1, n):
                a2a_in_copy(1, k).wait_recv()
        lax.fori_loop(0, B // STEP, own_grad, 0)
        for ch in range(CHUNKS):
            ag_send(GF, ch)


    pack = hi * (packs // n) + lo

    def attend(i):
        pos = i * B + lax.broadcasted_iota(jnp.int32, (1, B), 1)
        first = jnp.zeros((1, B), jnp.int32)
        end = jnp.int32(0)
        for s in range(r.lengths.shape[0]):
            length = r.lengths[s, pack]
            end = end + length
            first = first + jnp.where(pos >= end, length, 0)

        def scores(j, peak):
            key_pos = j * KB + lax.broadcasted_iota(jnp.int32, (KB, B), 0)
            allowed = (key_pos >= first) & (key_pos <= pos)
            kr = rows(j * KB, KB)
            keys, keys_last = r.ka[kr], r.kb[kr]
            peaks = []
            for h in range(NH):
                if h < NH - 1:
                    raw = dot(keys, r.qa[i, h * B : (h + 1) * B], NT)
                else:
                    raw = dot(keys_last, r.qb[i], NT)
                raw = jnp.where(allowed, raw, MASKED)
                r.score[kr, h * B : (h + 1) * B] = raw
                peaks.append(jnp.max(raw, axis=0, keepdims=True))
            return jnp.maximum(peak, jnp.concatenate(peaks, axis=1))

        peak = lax.fori_loop(0, (i + KS) // KS, scores, jnp.full((1, NH * B), MASKED, F32))
        r.att[...] = jnp.zeros_like(r.att)

        def weigh(j, total):
            totals = []
            for h in range(NH):
                cols = slice(h * B, (h + 1) * B)
                weight = jnp.exp(r.score[rows(j * KB, KB), cols] - peak[:, cols])
                totals.append(jnp.sum(weight, axis=0, keepdims=True))
                low = weight.astype(BF)
                r.e[i, rows(j * KB, KB), cols] = low
                part = slice(h * HEAD_DIM, (h + 1) * HEAD_DIM)
                r.att[part] += dot(r.vt[part, rows(j * KB, KB)], low, NN)
            return total + jnp.concatenate(totals, axis=1)

        total = lax.fori_loop(0, (i + KS) // KS, weigh, jnp.zeros((1, NH * B), F32))
        inverse = 1.0 / total
        for h in range(NH):
            part = slice(h * HEAD_DIM, (h + 1) * HEAD_DIM)
            own = inverse[:, h * B : (h + 1) * B]
            r.att[part] = r.att[part] * own
            r.inv[i, h : h + 1] = own
        out = r.att[...].T
        at = rows(i * B, B)
        r.a[at] = out
        r.al[at] = out.astype(BF)

    def attend_step(s, _):
        k = 3 - s
        i = block_of(k)
        attend(i)

        @pl.when(s == 0)
        def _():
            wg_wait(OUT)

        part = dot(r.al[rows(i * B, B)], r.wo[...], NT)

        @pl.when(s == 0)
        def _():
            rs_put(0, 3, part)
            rs_m(0, 0).start()

        @pl.when(s == 1)
        def _():
            rs_put(0, 2, part)
            rs_ship(0)

        @pl.when(s == 2)
        def _():
            rs_put(0, 1, part)
            rs_m(0, 1).start()
            wg_mids(PROJ)

        @pl.when(s == 3)
        def _():
            rs_put(0, 0, part)

        return 0

    grad_in()
    wg_mids(FC)
    lax.fori_loop(0, 4, attend_step, 0)
    wg_second(FC)

    rs_m(0, 1).wait_recv()
    for ch in range(CHUNKS):
        if ch == CHUNKS - 1:
            wg_second(PROJ)
        rs_y(0, ch).wait_recv()

        def one(s, _):
            at = rows(ch * CR + s * STEP, STEP)
            values = r.came[0, at].astype(F32) + rs_total(0, at) + r.vecs[2:3]
            r.res[at] = values
            r.h2[rows(t * B + ch * CR + s * STEP, STEP)] = norm_step(
                values, at, r.vecs[3:4], r.vecs[4:5], r.cen2, r.scale2
            )
            return 0

        lax.fori_loop(0, CR // STEP, one, 0)
        ag_send(H2, ch)
    rs_drain(0)
    wg_wait(FC)
    wg_wait(PROJ)

    def feed(s, _):
        @pl.when(s == 1)
        def _():
            ag_arrive(GF, 1)
            ag_arrive(H2, 1)

        @pl.when(s == 2)
        def _():
            ag_arrive(GF, 2)
            ag_arrive(H2, 2)

        @pl.when(s == 3)
        def _():
            ag_arrive(GF, 3)
            ag_arrive(H2, 3)

        at = block_rows(s)
        hidden = r.h2[at]
        grad = r.gf[at]
        for j in range(FH // 256):
            cols = slice(j * 256, (j + 1) * 256)
            u = dot(hidden, r.w1[:, cols], NN) + r.vecs[6:7, cols]
            dz = dot(grad, r.w2[:, cols], NN)
            square = u * u
            half = 0.5 + 0.5 * jnp.tanh(u * (CURVE + (CURVE * CUBE) * square))
            act = u * half
            r.zz[at, cols] = act.astype(BF)
            slope = half + act * (1.0 - half) * (2.0 * CURVE + (6.0 * CURVE * CUBE) * square)
            low = (dz * slope).astype(BF)
            r.du[at, cols] = low
            r.acc_f[:, cols] += fold(low.astype(F32))
        part = dot(r.du[at], r.w1[...], NT)

        @pl.when(s == 0)
        def _():
            rs_put(1, 0, part)

        @pl.when(s == 1)
        def _():
            rs_put(1, 1, part)
            rs_m(1, 1).start()

        @pl.when(s == 2)
        def _():
            rs_put(1, 2, part)

        @pl.when(s == 3)
        def _():
            rs_put(1, 3, part)
            rs_m(1, 0).start()

        return 0

    lax.fori_loop(0, 4, feed, 0)
    rs_ship(1)

    def grad_tiles(left, right, out, cols=slice(None)):
        def one(i, _):
            at = rows(i * 256, 256)
            out[at] = dot(left[:, at], right[:, cols], TN).astype(BF)
            return 0

        lax.fori_loop(0, D // 256, one, 0)

    grad_tiles(r.gf, r.zz, r.gw2z, slice(HF, FH))
    z_start(PROJ_Z)
    grad_tiles(r.gf, r.zz, r.gw2, slice(0, HF))
    gr_start(PROJ)
    grad_tiles(r.h2, r.du, r.gw1z, slice(HF, FH))
    z_start(FC_Z)
    grad_tiles(r.h2, r.du, r.gw1, slice(0, HF))
    gr_start(FC)

    rs_m(1, 1).wait_recv()
    for ch in range(CHUNKS):
        rs_y(1, ch).wait_recv()

        def one(s, _):
            at = rows(ch * CR + s * STEP, STEP)
            back = norm_back(rs_total(1, at), at, r.vecs[3:4], r.cen2, r.scale2, 2)
            grad = r.came[1, at].astype(F32) + back
            r.dres[at] = grad
            r.acc[4] += fold(grad)
            r.dr[rows(t * B + ch * CR + s * STEP, STEP)] = grad.astype(BF)
            return 0

        lax.fori_loop(0, CR // STEP, one, 0)
        ag_send(DR, ch)
    rs_drain(1)

    def upper(s, _):
        k = 3 - s
        part = dot(r.zz[block_rows(k)], r.w2[...], NT)

        @pl.when(s == 0)
        def _():
            rs_put(3, 3, part)
            rs_m(3, 0).start()

        @pl.when(s == 1)
        def _():
            rs_put(3, 2, part)

        @pl.when(s == 2)
        def _():
            rs_put(3, 1, part)
            rs_m(3, 1).start()

        @pl.when(s == 3)
        def _():
            rs_put(3, 0, part)

        return 0

    lax.fori_loop(0, 4, upper, 0)

    lanes = lax.broadcasted_iota(jnp.int32, (1, HC), 1)
    LB = (NH - 1) * B

    def attend_back(i):
        at = rows(i * B, B)
        da = dot(r.dr[at], r.wo[...], NN).astype(BF).astype(F32)
        by_row = r.inv[i].T
        scale = by_row[:, NH - 1 : NH]
        for h in range(NH - 1):
            scale = jnp.where(lanes // HEAD_DIM == h, by_row[:, h : h + 1], scale)
        low = (da * scale).astype(BF)
        pair = low[:, :PW]
        for h in range(NH - 1):
            r.dama[h * B : (h + 1) * B] = jnp.where(head_mask(h), pair, jnp.zeros_like(pair))
        r.damb[at] = low[:, PW:]
        lined = (low.astype(F32) * r.a[at]).T
        deltas = [
            jnp.sum(lined[h * HEAD_DIM : (h + 1) * HEAD_DIM], axis=0, keepdims=True)
            for h in range(NH)
        ]
        r.inv[i, 4:5] = deltas[NH - 1]
        r.att[:PW] = jnp.zeros((PW, B), F32)

        def over_keys(j, _):
            kr = rows(j * KB, KB)
            values = r.va[kr]
            for h in range(NH - 1):
                own = slice(h * B, (h + 1) * B)
                dp = dot(values, r.dama[own], NT)
                ds = (r.e[i, kr, own].astype(F32) * (dp - deltas[h])).astype(BF)
                r.ds[:, own] = ds
                part = slice(h * HEAD_DIM, (h + 1) * HEAD_DIM)
                r.att[part] += dot(r.kt[part, kr], ds, NN)
            r.dka[kr] += dot(r.ds[...], r.qa[i], NN)
            r.dva[kr] += dot(r.e[i, kr, :LB], r.dama[...], NN)
            return 0

        lax.fori_loop(0, (i + KS) // KS, over_keys, 0)
        r.dqa[at, :PW] = (r.att[:PW].T * HEAD_DIM ** (-0.5)).astype(BF)

    def attend_back_last():
        blocks = S // B
        for i in reversed(range(blocks)):
            at, keys = slice(i * B, (i + 1) * B), slice(0, (i + 1) * B)
            grad = r.damb[at]
            dp = dot(r.vb[keys], grad, NT)
            weight = r.e[i, keys, LB:]
            ds = (weight.astype(F32) * (dp - r.inv[i, 4:5])).astype(BF)
            dq = dot(r.kt[PW:, keys], ds, NN)
            dk, dv = dot(ds, r.qb[i], NN), dot(weight, grad, NN)
            if i == blocks - 1:
                r.dkb[...], r.dvb[...] = dk, dv
            else:
                r.dkb[keys] += dk
                r.dvb[keys] += dv
            dq = jnp.concatenate([dq, dq], axis=0).T[:, :LW]
            r.dqb[at, :LW] = (dq * HEAD_DIM ** (-0.5)).astype(BF)

    def round_kv(which):
        width, dk, dv, dqkv = ((PW, r.dka, r.dva, r.dqa), (LW, r.dkb, r.dvb, r.dqb))[which]

        def one(b, _):
            at = rows(b * B, B)
            dqkv[at, width : 2 * width] = dk[at].astype(BF)
            dqkv[at, 2 * width :] = dv[at].astype(BF)
            acc = (r.acc_a, r.acc_b)[which]
            acc[...] += fold(dqkv[at].astype(F32))
            return 0

        lax.fori_loop(0, 4, one, 0)

    for zeroed in (r.dka, r.dva):
        zeroed[...] = jnp.zeros_like(zeroed)

    def pair_step(s, _):
        @pl.when(s == 1)
        def _():
            ag_arrive(DR, 1)

        @pl.when(s == 2)
        def _():
            ag_arrive(DR, 2)
            rs_ship(3)
            gr_mid(PROJ)

        @pl.when(s == 3)
        def _():
            ag_arrive(DR, 3)
            gr_mid(FC)
            grad_tiles(r.dr, r.al, r.gwo)
            gr_start(OUT)

        attend_back(block_of(s))
        return 0

    lax.fori_loop(0, 4, pair_step, 0)
    round_kv(0)
    grad_tiles(r.h1, r.dqa, r.gwa)
    gr_start(PAIR)
    gr_far(PROJ)
    z_end(PROJ_Z, r.out_w2_v)

    def upper_back():
        rs_m(3, 1).wait_recv()
        for ch in range(CHUNKS):
            rs_y(3, ch).wait_recv()

        def finish_up(s, _):
            at = rows(s * STEP, STEP)
            r.made[0, at] = (r.res[at] + rs_total(3, at) + r.vecs[5:6]).astype(BF)
            return 0

        lax.fori_loop(0, B // STEP, finish_up, 0)
        if inside:
            for k in range(1, n):
                a2a_out_copy(0, k).start()
            r.back0[hi] = r.made[0, rows(hi * PR, PR)]
        else:
            r.out_y_v[...] = r.made[0]

    attend_back_last()
    round_kv(1)
    gr_mid(OUT)

    def lower(s, _):
        k = 3 - s
        at = block_rows(k)
        part = dot(r.dqa[at], r.wa[...], NT) + dot(r.dqb[at], r.wb[...], NT)

        @pl.when(s == 0)
        def _():
            rs_put(2, 3, part)
            rs_m(2, 0).start()

        @pl.when(s == 1)
        def _():
            rs_put(2, 2, part)
            rs_ship(2)

        @pl.when(s == 2)
        def _():
            rs_put(2, 1, part)
            rs_m(2, 1).start()

        @pl.when(s == 3)
        def _():
            rs_put(2, 0, part)

        return 0

    lax.fori_loop(0, 4, lower, 0)

    grad_tiles(r.h1, r.dqb, r.gwb)
    gr_start(LAST)
    upper_back()
    gr_far(FC)
    z_end(FC_Z, r.out_w1_v)
    gr_far(OUT)

    def line(value):
        return jnp.sum(value, axis=0, keepdims=True)

    for j, at in enumerate((5, 2, 3, 4)):
        spread(0, 8 * j, line(r.acc[at]))
    spread(0, 32, line(r.acc_f[...]))
    pad = jnp.zeros((1, 256 - HC), F32)
    pair, last = line(r.acc_a[...]), line(r.acc_b[...])
    for j in range(2):
        spread(0, 40 + 2 * j, pair[:, 2 * j * PW : (2 * j + 1) * PW])
        r.slab0[t, 41 + 2 * j : 42 + 2 * j, :LW] = last[:, 2 * j * LW : (2 * j + 1) * LW]
    sm_start(0)
    gr_mid(PAIR)

    rs_m(2, 1).wait_recv()
    for ch in range(CHUNKS):
        if ch == CHUNKS - 1:
            sm_mid(0)
        rs_y(2, ch).wait_recv()

        def one(s, _):
            at = rows(ch * CR + s * STEP, STEP)
            back = norm_back(rs_total(2, at), at, r.vecs[0:1], r.cen1, r.scale1, 0)
            r.made[1, at] = (r.dres[at] + back).astype(BF)
            return 0

        lax.fori_loop(0, CR // STEP, one, 0)
    rs_drain(2)
    rs_drain(3)
    if inside:
        for k in range(1, n):
            a2a_out_copy(1, k).start()
        r.back1[hi] = r.made[1, rows(hi * PR, PR)]
    else:
        r.out_x_v[...] = r.made[1]
    for j in range(2):
        spread(1, 8 * j, line(r.acc[j]))
    sm_start(1)
    gr_mid(LAST)
    gr_far(PAIR)
    sm_mid(1)
    gr_far(LAST)

    OUTS = tuple(outputs(cfg))

    def store(name):
        return pltpu.make_async_copy(r[name + "_v"], r[name], r.store_sem.at[OUTS.index(name)])

    def put_back(tag, out):
        for k in range(1, n):
            a2a_out_copy(tag, k).wait_recv()

        def one(j, _):
            out[j] = backs[tag][r.order[j]]
            return 0

        lax.fori_loop(0, n, one, 0)

    z_finish(PROJ_Z, r.out_w2_v)
    r.out_w2_v[:, :HF] = gr_finish(PROJ)
    store(OUT_W2).start()
    z_finish(FC_Z, r.out_w1_v)
    r.out_w1_v[:, :HF] = gr_finish(FC)
    store(OUT_W1).start()
    if inside:
        put_back(0, r.out_y_v)
    store(OUT_Y).start()
    r.turn[...] = jnp.zeros_like(r.turn)
    r.turn[:WR, :HC] = gr_finish(OUT)
    r.out_wo_v[...] = r.turn[...].T[:HC, :WR]
    store(OUT_WO).start()
    r.out_early_v[...] = sm_finish(0)
    store(OUT_EARLY).start()
    if inside:
        put_back(1, r.out_x_v)
    store(OUT_X).start()
    r.out_late_v[...] = sm_finish(1)
    store(OUT_LATE).start()
    total = gr_finish(PAIR)
    for i in range(3):
        r.out_qkv_v[i, :, :PW] = total[:, i * PW : (i + 1) * PW]
    total = gr_finish(LAST)
    for i in range(3):
        r.out_qkv_v[i, :, PW:] = total[:, i * LW : (i + 1) * LW]
    store(OUT_QKV).start()

    for name in WG:
        wg_drain(name)
    for name in GS:
        gr_drain(name)
    for name in AG:
        ag_drain(name)
    for name in OUTS:
        store(name).wait()
    for tag in range(2):
        sm_drain(tag)
        if inside:
            for k in range(1, n):
                a2a_in_copy(tag, k).wait_send()
                a2a_out_copy(tag, k).wait_send()


def settle(*refs):
    early, late = refs[6:8]
    whole, small = refs[8:14], refs[14:22]
    for i in range(6):
        whole[i][...] = refs[i][...]
    for j in range(4):
        small[j][...] = early[8 * j : 8 * j + small[j].shape[0]]
    for j in range(2):
        small[4 + j][...] = late[8 * j : 8 * j + small[4 + j].shape[0]]
    small[6][...] = early[32 : 32 + small[6].shape[0]]
    heads = small[7]
    for j in range(2):
        heads[j : j + 1, :128] = early[40 + 2 * j : 41 + 2 * j]
        heads[j : j + 1, 128:] = early[41 + 2 * j : 42 + 2 * j, : heads.shape[1] - 128]


def inputs():
    vmem = pl.BlockSpec(memory_space=pltpu.VMEM)
    smem = pl.BlockSpec(memory_space=pltpu.SMEM)
    hbm = pl.BlockSpec(memory_space=pl.ANY)
    return Refs(
        order=smem,
        lengths=smem,
        x_hbm=hbm,
        g_hbm=hbm,
        ln1g=vmem,
        ln1b=vmem,
        wqkv_hbm=hbm,
        qvb=vmem,
        wo_hbm=hbm,
        aob=vmem,
        ln2g=vmem,
        ln2b=vmem,
        w1_hbm=hbm,
        fcb=vmem,
        w2_hbm=hbm,
        pjb=vmem,
    )


def outputs(cfg):
    (n, packs, L, S, D, HC, FH, inside) = cfg
    WR = D // n
    tokens = (n, L // n, D) if inside else (L, D)
    return Refs(
        out_y=(tokens, BF),
        out_x=(tokens, BF),
        out_qkv=((3, WR, HC), F32),
        out_wo=((HC, WR), F32),
        out_w1=((WR, FH), F32),
        out_w2=((WR, FH), F32),
        out_early=((48, 128), F32),
        out_late=((16, 128), F32),
    )


def scratch(cfg):
    (n, packs, L, S, D, HC, FH, inside) = cfg
    NH = HC // HEAD_DIM
    LW = HEAD_DIM
    PW = HC - LW
    NZ = n // 2
    WR = D // n
    V = pltpu.VMEM
    sem = pltpu.SemaphoreType.DMA
    blocks = S // L
    tokens = (n, L // n, D) if inside else (L, D)
    kind = F32 if inside else BF
    made = Refs(
        came=V((2, L, D), BF),
        made=V((2, L, D), BF),
        wa=V((D, 3 * PW), BF),
        wb=V((D, 3 * LW), BF),
        wo=V((D, HC), BF),
        w1=V((D, FH), BF),
        w2=V((D, FH), BF),
        turn=V((256, 256), F32),
        vecs=V((8, D), F32),
        x_in=V(tokens, BF),
        g_in=V(tokens, BF),
        wqkv_in=V((3, WR, HC), kind),
        wo_in=V((HC, WR), kind),
        w1_in=V((WR, FH), kind),
        w2_in=V((WR, FH), kind),
        load_sem=sem((6,)),
        store_sem=sem((8,)),
        h1=V((S, D), BF),
        gf=V((S, D), BF),
        h2=V((S, D), BF),
        dr=V((S, D), BF),
        cen1=V((L, D), F32),
        cen2=V((L, D), F32),
        scale1=V((L, 1), F32),
        scale2=V((L, 1), F32),
        res=V((L, D), F32),
        dres=V((L, D), F32),
        qa=V((blocks, (NH - 1) * L, PW), BF),
        ka=V((S, PW), BF),
        va=V((S, PW), BF),
        qb=V((blocks, L, LW), BF),
        kb=V((S, LW), BF),
        vb=V((S, LW), BF),
        vbt=V((LW, 1), F32),
        kt=V((HC, S), BF),
        vt=V((HC, S), BF),
        score=V((S, NH * L), F32),
        e=V((blocks, S, NH * L), BF),
        att=V((HC, L), F32),
        inv=V((blocks, 8, L), F32),
        a=V((S, HC), F32),
        al=V((S, HC), BF),
        dama=V(((NH - 1) * L, PW), BF),
        damb=V((S, LW), BF),
        ds=V((2 * L, (NH - 1) * L), BF),
        dka=V((S, PW), F32),
        dva=V((S, PW), F32),
        dkb=V((S, LW), F32),
        dvb=V((S, LW), F32),
        dqa=V((S, 3 * PW), BF),
        dqb=V((S, 3 * LW), BF),
        zz=V((S, FH), BF),
        du=V((S, FH), BF),
        acc=V((6, 8, D), F32),
        acc_f=V((8, FH), F32),
        acc_a=V((8, 3 * PW), F32),
        acc_b=V((8, 3 * LW), F32),
        slab0=V((4, 48, 128), F32),
        slab1=V((4, 16, 128), F32),
        hslab0=V((n, 48, 128), BF),
        hslab1=V((n, 16, 128), BF),
    )
    for name, (shape, dtype) in outputs(cfg).items():
        made[name + "_v"] = V(shape, dtype)
    if inside:
        made.update(
            sent=V((2, n, L // n, D), BF),
            back0=V((n, L // n, D), BF),
            back1=V((n, L // n, D), BF),
            a2a_sem=sem((2, 4, n - 1)),
        )
    for late in "cy":
        made["ms" + late] = V((2, L, D), BF)
        made["mr" + late] = V((2, L, D), BF)
        made["keep" + late] = V((2, L, D), F32)
        made["ys" + late] = V((L, D), BF)
        made["yr" + late] = V((L, D), BF)
    for name, width in ((PAIR, 3 * PW), (LAST, 3 * LW), (OUT, HC)) + tuple((name, FH // 2) for name in (FC, PROJ) + ZFIRST):
        slot = (WR, width)
        made["g" + name] = V((D, width), BF)
        if name in ZFIRST:
            made[name + "_xs"] = V(slot, BF)
            made[name + "_xr"] = V(slot, BF)
            made[name + "_zr"] = V((3, 2 * WR, width), BF)
            continue
        made[name + "_xr"] = V((NZ,) + slot, BF)
        made[name + "_zs"] = V((NZ - 1,) + slot, BF)
        made[name + "_zr"] = V((NZ,) + slot, BF)
    made.update(
        wg_sem=sem((2, 5, 2 * NZ)),
        gr_sem=sem((2, 7, 2 * NZ + 1)),
        ag_sem=sem((2, 4, 3, CHUNKS)),
        rs_sem=sem((2, 4, 2 + CHUNKS)),
        sm_sem=sem((2, 2, 3 + n)),
    )
    return made


def cfg_names(cfg):
    return tuple(inputs()) + tuple(outputs(cfg)) + tuple(scratch(cfg))


def local(
    n,
    block_input,
    out_cotangent,
    seq_lengths,
    pack_order,
    ln1_gain,
    ln1_bias,
    qkv_weight,
    qv_bias,
    attn_out_weight,
    attn_out_bias,
    ln2_gain,
    ln2_bias,
    fc_weight,
    fc_bias,
    proj_weight,
    proj_bias,
):
    L, D = block_input.shape
    packs = pack_order.shape[0]
    HC = qv_bias.shape[1]
    FH = fc_bias.shape[0]
    S = L * lax.axis_size("tensor")
    outer = packs // n
    inside = outer == 1
    cfg = (n, packs, L, S, D, HC, FH, inside)
    tokens = (block_input, out_cotangent)
    weights = (qkv_weight, attn_out_weight, fc_weight, proj_weight)
    if inside:
        tokens = [v.reshape(n, L // n, D) for v in tokens]
    else:
        slots = jnp.arange(packs, dtype=jnp.int32)
        chosen = (pack_order[None, :] == slots[:, None]).astype(BF)

        def pick(which, v):
            return (
                jnp.dot(which, v.reshape(packs, -1), preferred_element_type=F32)
                .astype(BF)
                .reshape(L, D)
            )

        tokens = [
            lax.all_to_all(
                pick(chosen, v), ("hi", "lo"), split_axis=0, concat_axis=0, tiled=True
            )
            for v in tokens
        ]
        weights = [
            lax.all_gather(w.astype(BF), "lo", axis=axis, tiled=True)
            for w, axis in zip(weights, (0, 1, 0, 1))
        ]
    row = lambda v: v.reshape(-1, 128)
    outs = outputs(cfg)
    made = pl.pallas_call(
        functools.partial(kernel, cfg),
        out_shape=[jax.ShapeDtypeStruct(shape, kind) for shape, kind in outs.values()],
        in_specs=list(inputs().values()),
        out_specs=[pl.BlockSpec(memory_space=pl.ANY)] * len(outs),
        scratch_shapes=list(scratch(cfg).values()),
        compiler_params=pltpu.CompilerParams(
            collective_id=0, has_side_effects=True, vmem_limit_bytes=63 * 2**20
        ),
    )(
        pack_order,
        seq_lengths.T,
        *tokens,
        row(ln1_gain),
        row(ln1_bias),
        jnp.transpose(weights[0], (1, 0, 2)),
        qv_bias,
        weights[1],
        row(attn_out_bias),
        row(ln2_gain),
        row(ln2_bias),
        weights[2],
        row(fc_bias),
        weights[3].T,
        row(proj_bias),
    )
    g = Refs(zip(outs, made))
    if not inside:
        exchange = lambda v: pick(
            chosen.T,
            lax.all_to_all(v, ("hi", "lo"), split_axis=0, concat_axis=0, tiled=True),
        )
        share = lambda v, axis: lax.psum_scatter(v, "lo", scatter_dimension=axis, tiled=True)
        g.out_y, g.out_x = exchange(g.out_y), exchange(g.out_x)
        g.out_qkv, g.out_wo = share(g.out_qkv, 1), share(g.out_wo, 1)
        g.out_w1, g.out_w2 = share(g.out_w1, 0), share(g.out_w2, 0)
        g.out_early, g.out_late = lax.psum((g.out_early, g.out_late), "lo")
    whole = [g.out_y.reshape(L, D), g.out_x.reshape(L, D), g.out_qkv, g.out_wo, g.out_w1, g.out_w2]
    vec = D // 128
    vmem = pl.BlockSpec(memory_space=pltpu.VMEM)
    settled = pl.pallas_call(
        settle,
        out_shape=[jax.ShapeDtypeStruct(v.shape, v.dtype) for v in whole]
        + [jax.ShapeDtypeStruct((vec, 128), F32)] * 6
        + [jax.ShapeDtypeStruct((FH // 128, 128), F32), jax.ShapeDtypeStruct((2, HC), F32)],
        in_specs=[vmem] * 8,
        out_specs=[vmem] * 14,
    )(*whole, g.out_early, g.out_late)
    out_y, out_x, qkv_sum, out_sum, fc_sum, proj_sum = settled[:6]
    pjb, ln2g, ln2b, aob, ln1g, ln1b = [v.reshape(D) for v in settled[6:12]]
    return (
        out_y,
        out_x,
        ln1g,
        ln1b,
        jnp.transpose(qkv_sum, (1, 0, 2)),
        settled[13],
        out_sum,
        aob,
        ln2g,
        ln2b,
        fc_sum,
        settled[12].reshape(FH),
        proj_sum.T,
        pjb,
    )


def solution(mesh):
    groups, members = mesh.shape["dp"], mesh.shape["tensor"]
    n = min(8, groups)
    cut = Mesh(mesh.devices.reshape(n, groups // n, members), ("hi", "lo", "tensor"))
    dp = ("hi", "lo")
    return jax.shard_map(
        functools.partial(local, n),
        mesh=cut,
        in_specs=(
            P(("hi", "lo", "tensor"), None),
            P(("hi", "lo", "tensor"), None),
            P(),
            P(),
            P(),
            P(),
            P(dp, None, "tensor"),
            P(None, "tensor"),
            P("tensor", dp),
            P(),
            P(),
            P(),
            P(dp, "tensor"),
            P("tensor"),
            P("tensor", dp),
            P(),
        ),
        out_specs=(
            P(("hi", "lo", "tensor"), None),
            P(("hi", "lo", "tensor"), None),
            P(),
            P(),
            P(dp, None, "tensor"),
            P(None, "tensor"),
            P("tensor", dp),
            P(),
            P(),
            P(),
            P(dp, "tensor"),
            P("tensor"),
            P("tensor", dp),
            P(),
        ),
        check_vma=False,
    )
```

```python
import functools

import jax
import jax.numpy as jnp
from jax import lax
from jax.experimental import pallas as pl
from jax.experimental.pallas import tpu as pltpu
from jax.sharding import Mesh
from jax.sharding import PartitionSpec as P

HEAD_DIM = 64
EPSILON = 1e-05
MASKED = -1e30
BF = jnp.bfloat16
F32 = jnp.float32
MESH = pl.DeviceIdType.MESH
CURVE = 0.7978845608028654
CUBE = 0.044715

CHUNKS = 2
STEP = 32

PAIR, LAST, OUT, FC, PROJ = "wa", "wb", "wo", "w1", "w2"
QKV = "wqkv"
PROJ_Z, FC_Z = "w2z", "w1z"
ZFIRST = (PROJ_Z, FC_Z)
H1, GF, H2, DR = "h1", "gf", "h2", "dr"
X_IN, G_IN = "x", "g"
OUT_Y, OUT_X, OUT_QKV, OUT_WO = "out_y", "out_x", "out_qkv", "out_wo"
OUT_W1, OUT_W2, OUT_EARLY, OUT_LATE = "out_w1", "out_w2", "out_early", "out_late"

NN = ((1,), (0,))
NT = ((1,), (1,))
TN = ((0,), (0,))


class Refs(dict):
    __getattr__ = dict.__getitem__


def dot(left_side, right_side, form):
    return lax.dot_general(
        left_side, right_side, (form, ((), ())), preferred_element_type=F32
    )


def kernel(cfg, *refs):
    (n, packs, L, S, D, HC, FH, inside) = cfg
    names = cfg_names(cfg)
    r = Refs(zip(names, refs))
    slabs, hslabs = (r.slab0, r.slab1), (r.hslab0, r.hslab1)
    backs = (r.back0, r.back1) if inside else None
    NH = HC // HEAD_DIM
    LW = HEAD_DIM
    PW = HC - LW
    NZ = n // 2
    WR = D // n
    PR = L // n
    CR = L // CHUNKS
    B = L
    KS = 2
    KB = KS * B

    hi = lax.axis_index("hi")
    lo = lax.axis_index("lo")
    t = lax.axis_index("tensor")
    z, xx = hi // 2, hi % 2
    y, c = t // 2, t % 2
    dev = lambda h, tt: (h, lo, tt)
    mate = dev(hi, 2 * y + 1 - c)
    ynb = dev(hi, 2 * (1 - y) + c)
    ymate = dev(hi, 2 * (1 - y) + 1 - c)
    xnb = dev(2 * z + 1 - xx, t)

    def zdev(k):
        return dev(2 * ((z + k) % NZ) + xx, t)

    def block_of(k):
        return 2 * ((y + k // 2) % 2) + (c + k % 2) % 2

    def rows(start, size, mult=None):
        return pl.ds(pl.multiple_of(start, mult or size), size)

    def block_rows(k):
        return rows(block_of(k) * B, B)

    def rcopy(src, dst, send, recv, target):
        return pltpu.make_async_remote_copy(
            src_ref=src,
            dst_ref=dst,
            send_sem=send,
            recv_sem=recv,
            device_id=target,
            device_id_type=MESH,
        )

    LOADS = (X_IN, G_IN, QKV, OUT, FC, PROJ)

    def load(name):
        return pltpu.make_async_copy(r[name + "_hbm"], r[name + "_in"], r.load_sem.at[LOADS.index(name)])

    for name in LOADS:
        load(name).start()

    barrier = pltpu.get_barrier_semaphore()
    peers = [dev((hi + k) % n, t) for k in range(1, n)] + [mate, ynb, ymate]
    for peer in peers:
        pl.semaphore_signal(barrier, inc=1, device_id=peer, device_id_type=MESH)

    def a2a(tag, k, source, target):
        sem = r.a2a_sem
        to = (hi + k) % n
        return rcopy(source(to), target(hi), sem.at[0, tag, k - 1], sem.at[1, tag, k - 1], dev(to, t))

    def a2a_in_copy(tag, k):
        return a2a(
            tag,
            k,
            lambda to: r.sent.at[tag, to],
            lambda me: r.came.at[tag, rows(me * PR, PR)],
        )

    def a2a_out_copy(tag, k):
        return a2a(
            2 + tag,
            k,
            lambda to: r.made.at[tag, rows(to * PR, PR)],
            lambda me: backs[tag].at[me],
        )

    def pick_pieces(tag, source):
        def one(k, _):
            where = jnp.int32(0)
            for j in range(n):
                where = jnp.where(r.order[j] == k, j, where)
            r.sent[tag, k] = source[where]
            return 0

        lax.fori_loop(0, n, one, 0)
        r.came[tag, rows(hi * PR, PR)] = r.sent[tag, hi]

    load(X_IN).wait()
    if inside:
        pick_pieces(0, r.x_in)
    pl.semaphore_wait(barrier, len(peers))
    if inside:
        for k in range(1, n):
            a2a_in_copy(0, k).start()
    else:
        r.came[0] = r.x_in[...]
    for j, vec in enumerate((r.ln1g, r.ln1b, r.aob, r.ln2g, r.ln2b, r.pjb, r.fcb)):
        for i in range(vec.shape[0]):
            r.vecs[j : j + 1, i * 128 : (i + 1) * 128] = vec[i : i + 1]

    WG = (PAIR, LAST, OUT, FC, PROJ)
    STRAIGHT = (PAIR, LAST)
    middle = (z == 1) | (z == 2)
    side = z // 2
    near, far_mid, far_end = z + 1 - 2 * (z % 2), 2 - side, 3 - 3 * side
    Z_FROM = (near, far_mid, far_end)
    near_dev = dev(2 * near + xx, t)

    def wslot(name, ref, slot):
        return ref.at[rows(slot * WR, WR, 16)]

    def wg_z(name, i):
        sem = r.wg_sem
        a = WG.index(name)
        if i < 2:
            slot = wslot(name, r[name], hi)
            target = (near_dev, dev(2 * far_mid + xx, t))[i]
            recv = (0, jnp.where(middle, 1, 2))[i]
        elif name in STRAIGHT:
            slot = wslot(name, r[name], hi)
            target = dev(2 * far_end + xx, t)
            recv = jnp.where(middle, 1, 2)
        else:
            slot = wslot(name, r[name], 2 * Z_FROM[i - 1] + xx)
            target = near_dev
            recv = i - 1
        return rcopy(slot, slot, sem.at[0, a, i], sem.at[1, a, recv], target)

    def wg_in(name, i):
        sem = r.wg_sem
        a = WG.index(name)
        slot = wslot(name, r[name], 2 * Z_FROM[i] + xx)
        return rcopy(slot, slot, sem.at[0, a, 3], sem.at[1, a, i], near_dev)

    def wg_x(name, i):
        sem = r.wg_sem
        a = WG.index(name)
        slot = wslot(name, r[name], 2 * (Z_FROM + (z,))[i] + xx)
        return rcopy(slot, slot, sem.at[0, a, 4 + i], sem.at[1, a, 4 + i], xnb)

    def wg_near(name):
        wg_in(name, 0).wait_recv()
        wg_x(name, 0).start()

    def wg_mids(name):
        @pl.when(middle)
        def _():
            for i in (1, 2):
                wg_in(name, i).wait_recv()
                wg_z(name, i + 1).start()
                wg_x(name, i).start()

    def wg_second(name):
        if name in STRAIGHT:
            for i in (1, 2):
                wg_in(name, i).wait_recv()
                wg_x(name, i).start()
            return

        @pl.when(jnp.logical_not(middle))
        def _():
            for i in (1, 2):
                wg_in(name, i).wait_recv()
                wg_x(name, i).start()

    def wg_wait(name):
        for i in range(NZ):
            wg_x(name, i).wait_recv()

    def wg_drain(name):
        for i in range(2):
            wg_z(name, i).wait_send()
        for i in range(NZ):
            wg_x(name, i).wait_send()
        if name in STRAIGHT:
            wg_z(name, 2).wait_send()
            return

        @pl.when(middle)
        def _():
            for i in (2, 3):
                wg_z(name, i).wait_send()

    own_w = rows(hi * WR, WR, 16)
    load(QKV).wait()
    for i in range(3):
        part = r.wqkv_in[i].astype(BF)
        r.wa[own_w, i * PW : (i + 1) * PW] = part[:, :PW]
        r.wb[own_w, i * LW : (i + 1) * LW] = part[:, PW:]
    for name in (PAIR, LAST):
        wg_x(name, 3).start()
        wg_z(name, 0).start()
    for name in LOADS[3:]:
        load(name).wait()
    r.w1[own_w] = r.w1_in[...].astype(BF)
    r.w2[own_w] = r.w2_in[...].astype(BF)
    r.turn[...] = jnp.zeros_like(r.turn)
    r.turn[:HC, :WR] = r.wo_in[...].astype(F32)
    r.wo[own_w] = r.turn[...].T[:WR, :HC].astype(BF)
    for name in (OUT, FC, PROJ):
        wg_x(name, 3).start()
    wg_z(OUT, 0).start()
    load(G_IN).wait()
    if inside:
        pick_pieces(1, r.g_in)
    else:
        r.came[1] = r.g_in[...]

    AG = (H1, GF, H2, DR)

    def ag(name, kind, ch):
        sem = r.ag_sem
        a = AG.index(name)
        full = r[name]
        if kind == 2:
            where = rows(block_of(2) * B + ch * CR, CR)
        else:
            where = rows(t * B + ch * CR, CR)
        target = ynb if kind == 0 else mate
        part = full.at[where]
        return rcopy(part, part, sem.at[0, a, kind, ch], sem.at[1, a, kind, ch], target)

    def ag_send(name, ch):
        ag(name, 0, ch).start()
        ag(name, 1, ch).start()

    def ag_forward(name, ch):
        ag(name, 0, ch).wait_recv()
        ag(name, 2, ch).start()

    def ag_arrive(name, k):
        for ch in range(CHUNKS):
            if k == 1:
                ag(name, 1, ch).wait_recv()
            elif k == 2:
                ag_forward(name, ch)
            else:
                ag(name, 2, ch).wait_recv()

    def ag_drain(name):
        for kind in range(3):
            for ch in range(CHUNKS):
                ag(name, kind, ch).wait_send()

    def rs_bufs(tag):
        if tag == 3:
            return r.msy, r.mry, r.keepy, r.ysy, r.yry
        return r.msc, r.mrc, r.keepc, r.ysc, r.yrc

    def rs_m(tag, i):
        ms, mr, _, _, _ = rs_bufs(tag)
        sem = r.rs_sem
        return rcopy(ms.at[i], mr.at[i], sem.at[0, tag, i], sem.at[1, tag, i], mate)

    def chunk_at(tag, ch):
        return (1 - side + ch) % CHUNKS * CR if tag == 2 else ch * CR

    def rs_y(tag, ch):
        _, _, _, ys, yr = rs_bufs(tag)
        sem = r.rs_sem
        where = rows(chunk_at(tag, ch), CR)
        return rcopy(ys.at[where], yr.at[where], sem.at[0, tag, 2 + ch], sem.at[1, tag, 2 + ch], ynb)

    def rs_put(tag, k, value, at=None):
        ms, _, keep, _, _ = rs_bufs(tag)
        where = slice(None) if at is None else at
        i = 0 if k >= 2 else 1
        if k % 2:
            ms[i, where] = value.astype(BF)
        else:
            keep[i, where] = value

    def rs_ship(tag):
        _, mr, keep, ys, _ = rs_bufs(tag)
        rs_m(tag, 0).wait_recv()
        for ch in range(CHUNKS):

            def one(s, _):
                at = rows(chunk_at(tag, ch) + s * STEP, STEP)
                ys[at] = (keep[0, at] + mr[0, at].astype(F32)).astype(BF)
                return 0

            lax.fori_loop(0, CR // STEP, one, 0)
            rs_y(tag, ch).start()

    def rs_total(tag, at):
        _, mr, keep, _, yr = rs_bufs(tag)
        return keep[1, at] + mr[1, at].astype(F32) + yr[at].astype(F32)

    def rs_drain(tag):
        for i in range(2):
            rs_m(tag, i).wait_send()
        for ch in range(CHUNKS):
            rs_y(tag, ch).wait_send()

    GS = WG + ZFIRST
    GR = {name: "g" + name for name in GS}
    HF = FH // 2

    def gr_x(name, k):
        sem = r.gr_sem
        a = GS.index(name)
        slot = wslot(name, r[GR[name]], 2 * k + 1 - xx)
        return rcopy(slot, r[name + "_xr"].at[k], sem.at[0, a, k], sem.at[1, a, k], xnb)

    def gr_z(name, i):
        sem = r.gr_sem
        a = GS.index(name)
        to_mid, to_end = dev(2 * far_mid + xx, t), dev(2 * far_end + xx, t)
        if name in ZFIRST:
            to, source = (near_dev, to_mid, to_end)[i], i
            recv = 0 if i == 0 else jnp.where(middle, 1, 2)
        else:
            to = {0: near_dev, 2: near_dev, 3: near_dev, 1: to_mid, 4: to_end}[i]
            source = {0: 0, 2: 1, 3: 2, 1: 1, 4: 2}[i]
            recv = 1 if i == 4 else i
        part = two(name, Z_FROM[source]) if name in ZFIRST else r[name + "_zs"].at[source]
        return rcopy(part, r[name + "_zr"].at[recv], sem.at[0, a, NZ + i], sem.at[1, a, NZ + recv], to)

    def gr_zin(name, i):
        sem = r.gr_sem
        a = GS.index(name)
        part = r[name + "_zr"].at[i]
        return rcopy(part, part, sem.at[0, a, NZ], sem.at[1, a, NZ + i], near_dev)

    def two(name, place):
        return r[GR[name]].at[rows(2 * place * WR, 2 * WR, 32)]

    def z_start(name):
        for i in range(3):
            gr_z(name, i).start()

    def x_last(name):
        sem = r.gr_sem
        a = GS.index(name)
        return rcopy(r[name + "_xs"], r[name + "_xr"], sem.at[0, a, 0], sem.at[1, a, 0], xnb)

    def z_end(name, out):
        zr = r[name + "_zr"]
        came = range(3)
        for i in came:
            gr_zin(name, i).wait_recv()

        def total(k):
            value = r[GR[name]][rows((2 * z + k) * WR, WR, 16)].astype(F32)
            at = rows(k * WR, WR, 16)
            for i in came:
                value = value + zr[i, at].astype(F32)
            return value

        r[name + "_xs"][...] = total(1 - xx).astype(BF)
        x_last(name).start()
        out[:, HF:] = total(xx)

    def z_finish(name, out):
        x_last(name).wait_recv()
        out[:, HF:] += r[name + "_xr"][...].astype(F32)

    def gr_start(name):
        for k in range(NZ):
            gr_x(name, k).start()

    def gr_pair(name, to):
        mine = wslot(name, r[GR[name]], 2 * to + xx)[...].astype(F32)
        return mine + r[name + "_xr"][to].astype(F32)

    def gr_mid(name):
        for k in range(NZ):
            gr_x(name, k).wait_recv()
        zs = r[name + "_zs"]
        zs[0] = gr_pair(name, near).astype(BF)
        gr_z(name, 0).start()

        @pl.when(jnp.logical_not(middle))
        def _():
            zs[1] = gr_pair(name, far_mid).astype(BF)
            gr_z(name, 2).start()
            zs[2] = gr_pair(name, far_end).astype(BF)
            gr_z(name, 3).start()

    def gr_far(name):
        @pl.when(middle)
        def _():
            zs, zr = r[name + "_zs"], r[name + "_zr"]
            gr_zin(name, 2).wait_recv()
            zs[1] = (gr_pair(name, far_mid) + zr[2].astype(F32)).astype(BF)
            gr_z(name, 1).start()
            gr_zin(name, 3).wait_recv()
            zs[2] = (gr_pair(name, far_end) + zr[3].astype(F32)).astype(BF)
            gr_z(name, 4).start()

    def gr_finish(name):
        total = gr_pair(name, z)
        for i in range(2):
            gr_zin(name, i).wait_recv()
            total = total + r[name + "_zr"][i].astype(F32)
        return total

    def gr_drain(name):
        if name in ZFIRST:
            x_last(name).wait_send()
        else:
            for k in range(NZ):
                gr_x(name, k).wait_send()
        gr_z(name, 0).wait_send()
        if name in ZFIRST:
            gr_z(name, 1).wait_send()
            gr_z(name, 2).wait_send()
            return

        @pl.when(middle)
        def _():
            gr_z(name, 1).wait_send()
            gr_z(name, 4).wait_send()

        @pl.when(jnp.logical_not(middle))
        def _():
            gr_z(name, 2).wait_send()
            gr_z(name, 3).wait_send()

    tpeers = [mate, ynb, ymate]
    SHARED = (32, 16)

    def sm_t(tag, i):
        sem = r.sm_sem
        part = slabs[tag].at[t]
        return rcopy(part, part, sem.at[0, tag, i], sem.at[1, tag, i], tpeers[i])

    def sm_h(tag, k):
        sem = r.sm_sem
        part = hslabs[tag].at[hi]
        return rcopy(part, part, sem.at[0, tag, 3 + k], sem.at[1, tag, 3 + k], dev((hi + k) % n, t))

    def spread(tag, at, value):
        for j in range(value.shape[1] // 128):
            slabs[tag][t, at + j : at + j + 1] = value[:, j * 128 : (j + 1) * 128]

    def sm_start(tag):
        for i in range(3):
            sm_t(tag, i).start()

    def sm_mid(tag):
        for i in range(3):
            sm_t(tag, i).wait_recv()
        slab, hslab = slabs[tag], hslabs[tag]
        total = slab[0]
        for i in range(1, 4):
            total = total + slab[i]
        if tag == 0:
            keep = lax.broadcasted_iota(jnp.int32, total.shape, 0) < SHARED[0]
            total = jnp.where(keep, total, slab[t])
        hslab[hi] = total.astype(BF)
        for k in range(1, n):
            sm_h(tag, k).start()

    def sm_finish(tag):
        for k in range(1, n):
            sm_h(tag, k).wait_recv()
        hslab = hslabs[tag]
        total = hslab[0].astype(F32)
        for k in range(1, n):
            total = total + hslab[k].astype(F32)
        return total

    def sm_drain(tag):
        for i in range(3):
            sm_t(tag, i).wait_send()
        for k in range(1, n):
            sm_h(tag, k).wait_send()

    def fold(value):
        return jnp.sum(value.reshape(value.shape[0] // 8, 8, value.shape[1]), axis=0)

    for slab in slabs:
        slab[t] = jnp.zeros(slab.shape[1:], F32)
    r.acc[...] = jnp.zeros_like(r.acc)
    r.acc_f[...] = jnp.zeros_like(r.acc_f)
    r.acc_a[...] = jnp.zeros_like(r.acc_a)
    r.acc_b[...] = jnp.zeros_like(r.acc_b)

    if inside:
        for k in range(1, n):
            a2a_in_copy(0, k).wait_recv()
    for name in STRAIGHT:
        wg_z(name, 1).start()
        wg_z(name, 2).start()
    wg_z(FC, 0).start()

    def norm_step(values, at, gain, bias, cen, scale):
        mean = jnp.mean(values, axis=1, keepdims=True)
        var = jnp.mean(values * values, axis=1, keepdims=True) - mean * mean
        inv = lax.rsqrt(var + EPSILON)
        centered = (values - mean) * inv
        cen[at] = centered
        scale[at] = inv
        return (centered * gain + bias).astype(BF)

    def norm_back(grad, at, gain, cen, scale, acc_at):
        centered = cen[at]
        r.acc[acc_at] += fold(grad * centered)
        r.acc[acc_at + 1] += fold(grad)
        scaled = grad * gain
        return scale[at] * (
            scaled
            - jnp.mean(scaled, axis=1, keepdims=True)
            - centered * jnp.mean(scaled * centered, axis=1, keepdims=True)
        )

    for ch in range(CHUNKS):

        def one(s, _):
            at = rows(ch * CR + s * STEP, STEP)
            values = r.came[0, at].astype(F32)
            r.h1[rows(t * B + ch * CR + s * STEP, STEP)] = norm_step(
                values, at, r.vecs[0:1], r.vecs[1:2], r.cen1, r.scale1
            )
            return 0

        lax.fori_loop(0, CR // STEP, one, 0)
        ag_send(H1, ch)

    for name in (PAIR, LAST, OUT):
        wg_near(name)
    wg_second(PAIR)
    wg_z(OUT, 1).start()
    ag_arrive(H1, 1)
    ag_arrive(H1, 2)
    wg_second(LAST)
    if inside:
        for k in range(1, n):
            a2a_in_copy(1, k).start()
    wg_wait(PAIR)
    wg_wait(LAST)
    wg_mids(OUT)
    wg_near(FC)
    wg_z(FC, 1).start()
    wg_z(PROJ, 0).start()

    lane = lax.broadcasted_iota(jnp.int32, (1, PW), 1)

    def head_mask(h):
        return (lane >= h * HEAD_DIM) & (lane < (h + 1) * HEAD_DIM)

    def project(s, _):
        @pl.when(s == 3)
        def _():
            ag_arrive(H1, 3)

        b = block_of(s)
        at = rows(b * B, B)
        hidden = r.h1[at]

        def scaled(q):
            return (q.astype(BF).astype(F32) * HEAD_DIM ** (-0.5)).astype(BF)

        both = dot(hidden, r.wa[...], NN)
        q = scaled(both[:, :PW] + r.qvb[0:1, :PW])
        for h in range(NH - 1):
            r.qa[b, h * B : (h + 1) * B] = jnp.where(head_mask(h), q, jnp.zeros_like(q))
        k = both[:, PW : 2 * PW]
        r.ka[at] = k.astype(BF)
        r.kt[:PW, at] = k.T.astype(BF)
        v = both[:, 2 * PW :] + r.qvb[1:2, :PW]
        r.va[at] = v.astype(BF)
        r.vt[:PW, at] = v.T.astype(BF)
        last = dot(hidden, r.wb[...], NN)
        r.qb[b] = scaled(last[:, :LW] + r.qvb[0:1, PW:])
        r.kb[at] = last[:, LW : 2 * LW].astype(BF)
        r.vb[at] = (last[:, 2 * LW :] + r.qvb[1:2, PW:]).astype(BF)
        turned = last.T
        r.kt[PW:, at] = turned[LW : 2 * LW].astype(BF)
        r.vt[PW:, at] = (turned[2 * LW :] + r.vbt[...]).astype(BF)
        return 0

    bias_last = jnp.concatenate([r.qvb[1:2, PW:], jnp.zeros((1, LW), F32)], axis=1)
    r.vbt[...] = jnp.broadcast_to(bias_last, (8, 2 * LW)).T[:LW, :1]
    lax.fori_loop(0, 4, project, 0)
    wg_second(OUT)
    wg_near(PROJ)
    wg_z(PROJ, 1).start()

    def own_grad(s, _):
        at = rows(s * STEP, STEP)
        value = r.came[1, at]
        r.gf[rows(t * B + s * STEP, STEP)] = value
        r.acc[5] += fold(value.astype(F32))
        return 0

    def grad_in():
        if inside:
            for k in range(1, n):
                a2a_in_copy(1, k).wait_recv()
        lax.fori_loop(0, B // STEP, own_grad, 0)
        for ch in range(CHUNKS):
            ag_send(GF, ch)


    pack = hi * (packs // n) + lo

    def attend(i):
        pos = i * B + lax.broadcasted_iota(jnp.int32, (1, B), 1)
        first = jnp.zeros((1, B), jnp.int32)
        end = jnp.int32(0)
        for s in range(r.lengths.shape[0]):
            length = r.lengths[s, pack]
            end = end + length
            first = first + jnp.where(pos >= end, length, 0)

        def scores(j, peak):
            key_pos = j * KB + lax.broadcasted_iota(jnp.int32, (KB, B), 0)
            allowed = (key_pos >= first) & (key_pos <= pos)
            kr = rows(j * KB, KB)
            keys, keys_last = r.ka[kr], r.kb[kr]
            peaks = []
            for h in range(NH):
                if h < NH - 1:
                    raw = dot(keys, r.qa[i, h * B : (h + 1) * B], NT)
                else:
                    raw = dot(keys_last, r.qb[i], NT)
                raw = jnp.where(allowed, raw, MASKED)
                r.score[kr, h * B : (h + 1) * B] = raw
                peaks.append(jnp.max(raw, axis=0, keepdims=True))
            return jnp.maximum(peak, jnp.concatenate(peaks, axis=1))

        peak = lax.fori_loop(0, (i + KS) // KS, scores, jnp.full((1, NH * B), MASKED, F32))
        r.att[...] = jnp.zeros_like(r.att)

        def weigh(j, total):
            totals = []
            for h in range(NH):
                cols = slice(h * B, (h + 1) * B)
                weight = jnp.exp(r.score[rows(j * KB, KB), cols] - peak[:, cols])
                totals.append(jnp.sum(weight, axis=0, keepdims=True))
                low = weight.astype(BF)
                r.e[i, rows(j * KB, KB), cols] = low
                part = slice(h * HEAD_DIM, (h + 1) * HEAD_DIM)
                r.att[part] += dot(r.vt[part, rows(j * KB, KB)], low, NN)
            return total + jnp.concatenate(totals, axis=1)

        total = lax.fori_loop(0, (i + KS) // KS, weigh, jnp.zeros((1, NH * B), F32))
        inverse = 1.0 / total
        for h in range(NH):
            part = slice(h * HEAD_DIM, (h + 1) * HEAD_DIM)
            own = inverse[:, h * B : (h + 1) * B]
            r.att[part] = r.att[part] * own
            r.inv[i, h : h + 1] = own
        out = r.att[...].T
        at = rows(i * B, B)
        r.a[at] = out
        r.al[at] = out.astype(BF)

    def attend_step(s, _):
        k = 3 - s
        i = block_of(k)
        attend(i)

        @pl.when(s == 0)
        def _():
            wg_wait(OUT)

        part = dot(r.al[rows(i * B, B)], r.wo[...], NT)

        @pl.when(s == 0)
        def _():
            rs_put(0, 3, part)
            rs_m(0, 0).start()
            wg_mids(FC)

        @pl.when(s == 1)
        def _():
            rs_put(0, 2, part)
            rs_ship(0)

        @pl.when(s == 2)
        def _():
            rs_put(0, 1, part)
            rs_m(0, 1).start()
            wg_mids(PROJ)

        @pl.when(s == 3)
        def _():
            rs_put(0, 0, part)

        return 0

    grad_in()
    lax.fori_loop(0, 4, attend_step, 0)
    wg_second(FC)

    rs_m(0, 1).wait_recv()
    for ch in range(CHUNKS):
        if ch == CHUNKS - 1:
            wg_second(PROJ)
        rs_y(0, ch).wait_recv()

        def one(s, _):
            at = rows(ch * CR + s * STEP, STEP)
            values = r.came[0, at].astype(F32) + rs_total(0, at) + r.vecs[2:3]
            r.res[at] = values
            r.h2[rows(t * B + ch * CR + s * STEP, STEP)] = norm_step(
                values, at, r.vecs[3:4], r.vecs[4:5], r.cen2, r.scale2
            )
            return 0

        lax.fori_loop(0, CR // STEP, one, 0)
        ag_send(H2, ch)
    rs_drain(0)
    wg_wait(FC)
    wg_wait(PROJ)

    def feed(s, _):
        @pl.when(s == 1)
        def _():
            ag_arrive(GF, 1)
            ag_arrive(H2, 1)

        @pl.when(s == 2)
        def _():
            ag_arrive(GF, 2)
            ag_arrive(H2, 2)

        @pl.when(s == 3)
        def _():
            ag_arrive(GF, 3)
            ag_arrive(H2, 3)

        at = block_rows(s)
        hidden = r.h2[at]
        grad = r.gf[at]
        for j in range(FH // 256):
            cols = slice(j * 256, (j + 1) * 256)
            u = dot(hidden, r.w1[:, cols], NN) + r.vecs[6:7, cols]
            dz = dot(grad, r.w2[:, cols], NN)
            square = u * u
            half = 0.5 + 0.5 * jnp.tanh(u * (CURVE + (CURVE * CUBE) * square))
            act = u * half
            r.zz[at, cols] = act.astype(BF)
            slope = half + act * (1.0 - half) * (2.0 * CURVE + (6.0 * CURVE * CUBE) * square)
            low = (dz * slope).astype(BF)
            r.du[at, cols] = low
            r.acc_f[:, cols] += fold(low.astype(F32))
        part = dot(r.du[at], r.w1[...], NT)

        @pl.when(s == 0)
        def _():
            rs_put(1, 0, part)

        @pl.when(s == 1)
        def _():
            rs_put(1, 1, part)
            rs_m(1, 1).start()

        @pl.when(s == 2)
        def _():
            rs_put(1, 2, part)

        @pl.when(s == 3)
        def _():
            rs_put(1, 3, part)
            rs_m(1, 0).start()

        return 0

    lax.fori_loop(0, 4, feed, 0)
    rs_ship(1)

    def grad_tiles(left, right, out, cols=slice(None)):
        def one(i, _):
            at = rows(i * 256, 256)
            out[at] = dot(left[:, at], right[:, cols], TN).astype(BF)
            return 0

        lax.fori_loop(0, D // 256, one, 0)

    grad_tiles(r.gf, r.zz, r.gw2z, slice(HF, FH))
    z_start(PROJ_Z)
    grad_tiles(r.gf, r.zz, r.gw2, slice(0, HF))
    gr_start(PROJ)
    grad_tiles(r.h2, r.du, r.gw1z, slice(HF, FH))
    z_start(FC_Z)
    grad_tiles(r.h2, r.du, r.gw1, slice(0, HF))
    gr_start(FC)

    rs_m(1, 1).wait_recv()
    for ch in range(CHUNKS):
        rs_y(1, ch).wait_recv()

        def one(s, _):
            at = rows(ch * CR + s * STEP, STEP)
            back = norm_back(rs_total(1, at), at, r.vecs[3:4], r.cen2, r.scale2, 2)
            grad = r.came[1, at].astype(F32) + back
            r.dres[at] = grad
            r.acc[4] += fold(grad)
            r.dr[rows(t * B + ch * CR + s * STEP, STEP)] = grad.astype(BF)
            return 0

        lax.fori_loop(0, CR // STEP, one, 0)
        ag_send(DR, ch)
    rs_drain(1)

    def upper(s, _):
        k = 3 - s
        part = dot(r.zz[block_rows(k)], r.w2[...], NT)

        @pl.when(s == 0)
        def _():
            rs_put(3, 3, part)
            rs_m(3, 0).start()

        @pl.when(s == 1)
        def _():
            rs_put(3, 2, part)

        @pl.when(s == 2)
        def _():
            rs_put(3, 1, part)
            rs_m(3, 1).start()

        @pl.when(s == 3)
        def _():
            rs_put(3, 0, part)

        return 0

    lax.fori_loop(0, 4, upper, 0)

    lanes = lax.broadcasted_iota(jnp.int32, (1, HC), 1)
    LB = (NH - 1) * B

    def attend_back(i):
        at = rows(i * B, B)
        da = dot(r.dr[at], r.wo[...], NN).astype(BF).astype(F32)
        by_row = r.inv[i].T
        scale = by_row[:, NH - 1 : NH]
        for h in range(NH - 1):
            scale = jnp.where(lanes // HEAD_DIM == h, by_row[:, h : h + 1], scale)
        low = (da * scale).astype(BF)
        pair = low[:, :PW]
        for h in range(NH - 1):
            r.dama[h * B : (h + 1) * B] = jnp.where(head_mask(h), pair, jnp.zeros_like(pair))
        r.damb[at] = low[:, PW:]
        lined = (low.astype(F32) * r.a[at]).T
        deltas = [
            jnp.sum(lined[h * HEAD_DIM : (h + 1) * HEAD_DIM], axis=0, keepdims=True)
            for h in range(NH)
        ]
        r.inv[i, 4:5] = deltas[NH - 1]
        r.att[:PW] = jnp.zeros((PW, B), F32)

        def over_keys(j, _):
            kr = rows(j * KB, KB)
            values = r.va[kr]
            for h in range(NH - 1):
                own = slice(h * B, (h + 1) * B)
                dp = dot(values, r.dama[own], NT)
                ds = (r.e[i, kr, own].astype(F32) * (dp - deltas[h])).astype(BF)
                r.ds[:, own] = ds
                part = slice(h * HEAD_DIM, (h + 1) * HEAD_DIM)
                r.att[part] += dot(r.kt[part, kr], ds, NN)
            r.dka[kr] += dot(r.ds[...], r.qa[i], NN)
            r.dva[kr] += dot(r.e[i, kr, :LB], r.dama[...], NN)
            return 0

        lax.fori_loop(0, (i + KS) // KS, over_keys, 0)
        r.dqa[at, :PW] = (r.att[:PW].T * HEAD_DIM ** (-0.5)).astype(BF)

    def attend_back_last():
        blocks = S // B
        for i in reversed(range(blocks)):
            at, keys = slice(i * B, (i + 1) * B), slice(0, (i + 1) * B)
            grad = r.damb[at]
            dp = dot(r.vb[keys], grad, NT)
            weight = r.e[i, keys, LB:]
            ds = (weight.astype(F32) * (dp - r.inv[i, 4:5])).astype(BF)
            dq = dot(r.kt[PW:, keys], ds, NN)
            dk, dv = dot(ds, r.qb[i], NN), dot(weight, grad, NN)
            if i == blocks - 1:
                r.dkb[...], r.dvb[...] = dk, dv
            else:
                r.dkb[keys] += dk
                r.dvb[keys] += dv
            dq = jnp.concatenate([dq, dq], axis=0).T[:, :LW]
            r.dqb[at, :LW] = (dq * HEAD_DIM ** (-0.5)).astype(BF)

    def round_kv(which):
        width, dk, dv, dqkv = ((PW, r.dka, r.dva, r.dqa), (LW, r.dkb, r.dvb, r.dqb))[which]

        def one(b, _):
            at = rows(b * B, B)
            dqkv[at, width : 2 * width] = dk[at].astype(BF)
            dqkv[at, 2 * width :] = dv[at].astype(BF)
            acc = (r.acc_a, r.acc_b)[which]
            acc[...] += fold(dqkv[at].astype(F32))
            return 0

        lax.fori_loop(0, 4, one, 0)

    for zeroed in (r.dka, r.dva):
        zeroed[...] = jnp.zeros_like(zeroed)

    def pair_step(s, _):
        @pl.when(s == 1)
        def _():
            ag_arrive(DR, 1)

        @pl.when(s == 2)
        def _():
            ag_arrive(DR, 2)
            rs_ship(3)
            gr_mid(PROJ)

        @pl.when(s == 3)
        def _():
            ag_arrive(DR, 3)
            gr_mid(FC)
            grad_tiles(r.dr, r.al, r.gwo)
            gr_start(OUT)

        attend_back(block_of(s))
        return 0

    lax.fori_loop(0, 4, pair_step, 0)
    round_kv(0)
    grad_tiles(r.h1, r.dqa, r.gwa)
    gr_start(PAIR)
    gr_far(PROJ)
    z_end(PROJ_Z, r.out_w2_v)

    def upper_back():
        rs_m(3, 1).wait_recv()
        for ch in range(CHUNKS):
            rs_y(3, ch).wait_recv()

        def finish_up(s, _):
            at = rows(s * STEP, STEP)
            r.made[0, at] = (r.res[at] + rs_total(3, at) + r.vecs[5:6]).astype(BF)
            return 0

        lax.fori_loop(0, B // STEP, finish_up, 0)
        if inside:
            for k in range(1, n):
                a2a_out_copy(0, k).start()
            r.back0[hi] = r.made[0, rows(hi * PR, PR)]
        else:
            r.out_y_v[...] = r.made[0]

    attend_back_last()
    round_kv(1)
    gr_mid(OUT)
    upper_back()

    def lower(s, _):
        k = 3 - s
        at = block_rows(k)
        part = dot(r.dqa[at], r.wa[...], NT) + dot(r.dqb[at], r.wb[...], NT)

        @pl.when(s == 0)
        def _():
            rs_put(2, 3, part)
            rs_m(2, 0).start()

        @pl.when(s == 1)
        def _():
            rs_put(2, 2, part)
            rs_ship(2)

        @pl.when(s == 2)
        def _():
            rs_put(2, 1, part)
            rs_m(2, 1).start()

        @pl.when(s == 3)
        def _():
            rs_put(2, 0, part)

        return 0

    lax.fori_loop(0, 4, lower, 0)

    grad_tiles(r.h1, r.dqb, r.gwb)
    gr_start(LAST)
    gr_far(FC)
    z_end(FC_Z, r.out_w1_v)
    gr_far(OUT)

    def line(value):
        return jnp.sum(value, axis=0, keepdims=True)

    for j, at in enumerate((5, 2, 3, 4)):
        spread(0, 8 * j, line(r.acc[at]))
    spread(0, 32, line(r.acc_f[...]))
    pad = jnp.zeros((1, 256 - HC), F32)
    pair, last = line(r.acc_a[...]), line(r.acc_b[...])
    for j in range(2):
        spread(0, 40 + 2 * j, pair[:, 2 * j * PW : (2 * j + 1) * PW])
        r.slab0[t, 41 + 2 * j : 42 + 2 * j, :LW] = last[:, 2 * j * LW : (2 * j + 1) * LW]
    sm_start(0)
    gr_mid(PAIR)

    rs_m(2, 1).wait_recv()
    for ch in range(CHUNKS):
        if ch == CHUNKS - 1:
            sm_mid(0)
        rs_y(2, ch).wait_recv()

        def one(s, _):
            at = rows(chunk_at(2, ch) + s * STEP, STEP)
            back = norm_back(rs_total(2, at), at, r.vecs[0:1], r.cen1, r.scale1, 0)
            r.made[1, at] = (r.dres[at] + back).astype(BF)
            return 0

        lax.fori_loop(0, CR // STEP, one, 0)
        if inside:

            def send(j, _):
                to = chunk_at(2, ch) // PR + j

                @pl.when(to != hi)
                def _():
                    a2a_out_copy(1, (to - hi + n) % n).start()

                return 0

            lax.fori_loop(0, CR // PR, send, 0)

    rs_drain(2)
    rs_drain(3)
    if inside:
        r.back1[hi] = r.made[1, rows(hi * PR, PR)]
    else:
        r.out_x_v[...] = r.made[1]
    for j in range(2):
        spread(1, 8 * j, line(r.acc[j]))
    sm_start(1)
    gr_mid(LAST)
    gr_far(PAIR)
    sm_mid(1)
    gr_far(LAST)

    OUTS = tuple(outputs(cfg))

    def store(name):
        return pltpu.make_async_copy(r[name + "_v"], r[name], r.store_sem.at[OUTS.index(name)])

    def put_back(tag, out):
        for k in range(1, n):
            a2a_out_copy(tag, k).wait_recv()

        def one(j, _):
            out[j] = backs[tag][r.order[j]]
            return 0

        lax.fori_loop(0, n, one, 0)

    z_finish(PROJ_Z, r.out_w2_v)
    r.out_w2_v[:, :HF] = gr_finish(PROJ)
    store(OUT_W2).start()
    z_finish(FC_Z, r.out_w1_v)
    r.out_w1_v[:, :HF] = gr_finish(FC)
    store(OUT_W1).start()
    if inside:
        put_back(0, r.out_y_v)
    store(OUT_Y).start()
    r.turn[...] = jnp.zeros_like(r.turn)
    r.turn[:WR, :HC] = gr_finish(OUT)
    r.out_wo_v[...] = r.turn[...].T[:HC, :WR]
    store(OUT_WO).start()
    r.out_early_v[...] = sm_finish(0)
    store(OUT_EARLY).start()
    if inside:
        put_back(1, r.out_x_v)
    store(OUT_X).start()
    r.out_late_v[...] = sm_finish(1)
    store(OUT_LATE).start()
    total = gr_finish(PAIR)
    for i in range(3):
        r.out_qkv_v[i, :, :PW] = total[:, i * PW : (i + 1) * PW]
    total = gr_finish(LAST)
    for i in range(3):
        r.out_qkv_v[i, :, PW:] = total[:, i * LW : (i + 1) * LW]
    store(OUT_QKV).start()

    for name in WG:
        wg_drain(name)
    for name in GS:
        gr_drain(name)
    for name in AG:
        ag_drain(name)
    for name in OUTS:
        store(name).wait()
    for tag in range(2):
        sm_drain(tag)
        if inside:
            for k in range(1, n):
                a2a_in_copy(tag, k).wait_send()
                a2a_out_copy(tag, k).wait_send()


def settle(*refs):
    early, late = refs[6:8]
    whole, small = refs[8:14], refs[14:22]
    for i in range(6):
        whole[i][...] = refs[i][...]
    for j in range(4):
        small[j][...] = early[8 * j : 8 * j + small[j].shape[0]]
    for j in range(2):
        small[4 + j][...] = late[8 * j : 8 * j + small[4 + j].shape[0]]
    small[6][...] = early[32 : 32 + small[6].shape[0]]
    heads = small[7]
    for j in range(2):
        heads[j : j + 1, :128] = early[40 + 2 * j : 41 + 2 * j]
        heads[j : j + 1, 128:] = early[41 + 2 * j : 42 + 2 * j, : heads.shape[1] - 128]


def inputs():
    vmem = pl.BlockSpec(memory_space=pltpu.VMEM)
    smem = pl.BlockSpec(memory_space=pltpu.SMEM)
    hbm = pl.BlockSpec(memory_space=pl.ANY)
    return Refs(
        order=smem,
        lengths=smem,
        x_hbm=hbm,
        g_hbm=hbm,
        ln1g=vmem,
        ln1b=vmem,
        wqkv_hbm=hbm,
        qvb=vmem,
        wo_hbm=hbm,
        aob=vmem,
        ln2g=vmem,
        ln2b=vmem,
        w1_hbm=hbm,
        fcb=vmem,
        w2_hbm=hbm,
        pjb=vmem,
    )


def outputs(cfg):
    (n, packs, L, S, D, HC, FH, inside) = cfg
    WR = D // n
    tokens = (n, L // n, D) if inside else (L, D)
    return Refs(
        out_y=(tokens, BF),
        out_x=(tokens, BF),
        out_qkv=((3, WR, HC), F32),
        out_wo=((HC, WR), F32),
        out_w1=((WR, FH), F32),
        out_w2=((WR, FH), F32),
        out_early=((48, 128), F32),
        out_late=((16, 128), F32),
    )


def scratch(cfg):
    (n, packs, L, S, D, HC, FH, inside) = cfg
    NH = HC // HEAD_DIM
    LW = HEAD_DIM
    PW = HC - LW
    NZ = n // 2
    WR = D // n
    V = pltpu.VMEM
    sem = pltpu.SemaphoreType.DMA
    blocks = S // L
    tokens = (n, L // n, D) if inside else (L, D)
    kind = F32 if inside else BF
    made = Refs(
        came=V((2, L, D), BF),
        made=V((2, L, D), BF),
        wa=V((D, 3 * PW), BF),
        wb=V((D, 3 * LW), BF),
        wo=V((D, HC), BF),
        w1=V((D, FH), BF),
        w2=V((D, FH), BF),
        turn=V((256, 256), F32),
        vecs=V((8, D), F32),
        x_in=V(tokens, BF),
        g_in=V(tokens, BF),
        wqkv_in=V((3, WR, HC), kind),
        wo_in=V((HC, WR), kind),
        w1_in=V((WR, FH), kind),
        w2_in=V((WR, FH), kind),
        load_sem=sem((6,)),
        store_sem=sem((8,)),
        h1=V((S, D), BF),
        gf=V((S, D), BF),
        h2=V((S, D), BF),
        dr=V((S, D), BF),
        cen1=V((L, D), F32),
        cen2=V((L, D), F32),
        scale1=V((L, 1), F32),
        scale2=V((L, 1), F32),
        res=V((L, D), F32),
        dres=V((L, D), F32),
        qa=V((blocks, (NH - 1) * L, PW), BF),
        ka=V((S, PW), BF),
        va=V((S, PW), BF),
        qb=V((blocks, L, LW), BF),
        kb=V((S, LW), BF),
        vb=V((S, LW), BF),
        vbt=V((LW, 1), F32),
        kt=V((HC, S), BF),
        vt=V((HC, S), BF),
        score=V((S, NH * L), F32),
        e=V((blocks, S, NH * L), BF),
        att=V((HC, L), F32),
        inv=V((blocks, 8, L), F32),
        a=V((S, HC), F32),
        al=V((S, HC), BF),
        dama=V(((NH - 1) * L, PW), BF),
        damb=V((S, LW), BF),
        ds=V((2 * L, (NH - 1) * L), BF),
        dka=V((S, PW), F32),
        dva=V((S, PW), F32),
        dkb=V((S, LW), F32),
        dvb=V((S, LW), F32),
        dqa=V((S, 3 * PW), BF),
        dqb=V((S, 3 * LW), BF),
        zz=V((S, FH), BF),
        du=V((S, FH), BF),
        acc=V((6, 8, D), F32),
        acc_f=V((8, FH), F32),
        acc_a=V((8, 3 * PW), F32),
        acc_b=V((8, 3 * LW), F32),
        slab0=V((4, 48, 128), F32),
        slab1=V((4, 16, 128), F32),
        hslab0=V((n, 48, 128), BF),
        hslab1=V((n, 16, 128), BF),
    )
    for name, (shape, dtype) in outputs(cfg).items():
        made[name + "_v"] = V(shape, dtype)
    if inside:
        made.update(
            sent=V((2, n, L // n, D), BF),
            back0=V((n, L // n, D), BF),
            back1=V((n, L // n, D), BF),
            a2a_sem=sem((2, 4, n - 1)),
        )
    for late in "cy":
        made["ms" + late] = V((2, L, D), BF)
        made["mr" + late] = V((2, L, D), BF)
        made["keep" + late] = V((2, L, D), F32)
        made["ys" + late] = V((L, D), BF)
        made["yr" + late] = V((L, D), BF)
    for name, width in ((PAIR, 3 * PW), (LAST, 3 * LW), (OUT, HC)) + tuple((name, FH // 2) for name in (FC, PROJ) + ZFIRST):
        slot = (WR, width)
        made["g" + name] = V((D, width), BF)
        if name in ZFIRST:
            made[name + "_xs"] = V(slot, BF)
            made[name + "_xr"] = V(slot, BF)
            made[name + "_zr"] = V((3, 2 * WR, width), BF)
            continue
        made[name + "_xr"] = V((NZ,) + slot, BF)
        made[name + "_zs"] = V((NZ - 1,) + slot, BF)
        made[name + "_zr"] = V((NZ,) + slot, BF)
    made.update(
        wg_sem=sem((2, 5, 2 * NZ)),
        gr_sem=sem((2, 7, 2 * NZ + 1)),
        ag_sem=sem((2, 4, 3, CHUNKS)),
        rs_sem=sem((2, 4, 2 + CHUNKS)),
        sm_sem=sem((2, 2, 3 + n)),
    )
    return made


def cfg_names(cfg):
    return tuple(inputs()) + tuple(outputs(cfg)) + tuple(scratch(cfg))


def local(
    n,
    block_input,
    out_cotangent,
    seq_lengths,
    pack_order,
    ln1_gain,
    ln1_bias,
    qkv_weight,
    qv_bias,
    attn_out_weight,
    attn_out_bias,
    ln2_gain,
    ln2_bias,
    fc_weight,
    fc_bias,
    proj_weight,
    proj_bias,
):
    L, D = block_input.shape
    packs = pack_order.shape[0]
    HC = qv_bias.shape[1]
    FH = fc_bias.shape[0]
    S = L * lax.axis_size("tensor")
    outer = packs // n
    inside = outer == 1
    cfg = (n, packs, L, S, D, HC, FH, inside)
    tokens = (block_input, out_cotangent)
    weights = (qkv_weight, attn_out_weight, fc_weight, proj_weight)
    if inside:
        tokens = [v.reshape(n, L // n, D) for v in tokens]
    else:
        slots = jnp.arange(packs, dtype=jnp.int32)
        chosen = (pack_order[None, :] == slots[:, None]).astype(BF)

        def pick(which, v):
            return (
                jnp.dot(which, v.reshape(packs, -1), preferred_element_type=F32)
                .astype(BF)
                .reshape(L, D)
            )

        tokens = [
            lax.all_to_all(
                pick(chosen, v), ("hi", "lo"), split_axis=0, concat_axis=0, tiled=True
            )
            for v in tokens
        ]
        weights = [
            lax.all_gather(w.astype(BF), "lo", axis=axis, tiled=True)
            for w, axis in zip(weights, (0, 1, 0, 1))
        ]
    row = lambda v: v.reshape(-1, 128)
    outs = outputs(cfg)
    made = pl.pallas_call(
        functools.partial(kernel, cfg),
        out_shape=[jax.ShapeDtypeStruct(shape, kind) for shape, kind in outs.values()],
        in_specs=list(inputs().values()),
        out_specs=[pl.BlockSpec(memory_space=pl.ANY)] * len(outs),
        scratch_shapes=list(scratch(cfg).values()),
        compiler_params=pltpu.CompilerParams(
            collective_id=0, has_side_effects=True, vmem_limit_bytes=63 * 2**20
        ),
    )(
        pack_order,
        seq_lengths.T,
        *tokens,
        row(ln1_gain),
        row(ln1_bias),
        jnp.transpose(weights[0], (1, 0, 2)),
        qv_bias,
        weights[1],
        row(attn_out_bias),
        row(ln2_gain),
        row(ln2_bias),
        weights[2],
        row(fc_bias),
        weights[3].T,
        row(proj_bias),
    )
    g = Refs(zip(outs, made))
    if not inside:
        exchange = lambda v: pick(
            chosen.T,
            lax.all_to_all(v, ("hi", "lo"), split_axis=0, concat_axis=0, tiled=True),
        )
        share = lambda v, axis: lax.psum_scatter(v, "lo", scatter_dimension=axis, tiled=True)
        g.out_y, g.out_x = exchange(g.out_y), exchange(g.out_x)
        g.out_qkv, g.out_wo = share(g.out_qkv, 1), share(g.out_wo, 1)
        g.out_w1, g.out_w2 = share(g.out_w1, 0), share(g.out_w2, 0)
        g.out_early, g.out_late = lax.psum((g.out_early, g.out_late), "lo")
    whole = [g.out_y.reshape(L, D), g.out_x.reshape(L, D), g.out_qkv, g.out_wo, g.out_w1, g.out_w2]
    vec = D // 128
    vmem = pl.BlockSpec(memory_space=pltpu.VMEM)
    settled = pl.pallas_call(
        settle,
        out_shape=[jax.ShapeDtypeStruct(v.shape, v.dtype) for v in whole]
        + [jax.ShapeDtypeStruct((vec, 128), F32)] * 6
        + [jax.ShapeDtypeStruct((FH // 128, 128), F32), jax.ShapeDtypeStruct((2, HC), F32)],
        in_specs=[vmem] * 8,
        out_specs=[vmem] * 14,
    )(*whole, g.out_early, g.out_late)
    out_y, out_x, qkv_sum, out_sum, fc_sum, proj_sum = settled[:6]
    pjb, ln2g, ln2b, aob, ln1g, ln1b = [v.reshape(D) for v in settled[6:12]]
    return (
        out_y,
        out_x,
        ln1g,
        ln1b,
        jnp.transpose(qkv_sum, (1, 0, 2)),
        settled[13],
        out_sum,
        aob,
        ln2g,
        ln2b,
        fc_sum,
        settled[12].reshape(FH),
        proj_sum.T,
        pjb,
    )


def solution(mesh):
    groups, members = mesh.shape["dp"], mesh.shape["tensor"]
    n = min(8, groups)
    cut = Mesh(mesh.devices.reshape(n, groups // n, members), ("hi", "lo", "tensor"))
    dp = ("hi", "lo")
    return jax.shard_map(
        functools.partial(local, n),
        mesh=cut,
        in_specs=(
            P(("hi", "lo", "tensor"), None),
            P(("hi", "lo", "tensor"), None),
            P(),
            P(),
            P(),
            P(),
            P(dp, None, "tensor"),
            P(None, "tensor"),
            P("tensor", dp),
            P(),
            P(),
            P(),
            P(dp, "tensor"),
            P("tensor"),
            P("tensor", dp),
            P(),
        ),
        out_specs=(
            P(("hi", "lo", "tensor"), None),
            P(("hi", "lo", "tensor"), None),
            P(),
            P(),
            P(dp, None, "tensor"),
            P(None, "tensor"),
            P("tensor", dp),
            P(),
            P(),
            P(),
            P(dp, "tensor"),
            P("tensor"),
            P("tensor", dp),
            P(),
        ),
        check_vma=False,
    )
```

```python
import functools

import jax
import jax.numpy as jnp
from jax import lax
from jax.experimental import pallas as pl
from jax.experimental.pallas import tpu as pltpu
from jax.sharding import Mesh
from jax.sharding import PartitionSpec as P

HEAD_DIM = 64
EPSILON = 1e-05
MASKED = -1e30
BF = jnp.bfloat16
F32 = jnp.float32
MESH = pl.DeviceIdType.MESH
CURVE = 0.7978845608028654
CUBE = 0.044715

CHUNKS = 2
STEP = 32

PAIR, LAST, OUT, FC, PROJ = "wa", "wb", "wo", "w1", "w2"
QKV = "wqkv"
PROJ_Z, FC_Z = "w2z", "w1z"
ZFIRST = (PROJ_Z, FC_Z)
H1, GF, H2, DR = "h1", "gf", "h2", "dr"
X_IN, G_IN = "x", "g"
OUT_Y, OUT_X, OUT_QKV, OUT_WO = "out_y", "out_x", "out_qkv", "out_wo"
OUT_W1, OUT_W2, OUT_EARLY, OUT_LATE = "out_w1", "out_w2", "out_early", "out_late"

NN = ((1,), (0,))
NT = ((1,), (1,))
TN = ((0,), (0,))


class Refs(dict):
    __getattr__ = dict.__getitem__


def dot(left_side, right_side, form):
    return lax.dot_general(
        left_side, right_side, (form, ((), ())), preferred_element_type=F32
    )


def kernel(cfg, *refs):
    (n, packs, L, S, D, HC, FH, inside) = cfg
    names = cfg_names(cfg)
    r = Refs(zip(names, refs))
    slabs, hslabs = (r.slab0, r.slab1), (r.hslab0, r.hslab1)
    backs = (r.back0, r.back1) if inside else None
    NH = HC // HEAD_DIM
    LW = HEAD_DIM
    PW = HC - LW
    NZ = n // 2
    WR = D // n
    PR = L // n
    CR = L // CHUNKS
    B = L
    KS = 2
    KB = KS * B

    hi = lax.axis_index("hi")
    lo = lax.axis_index("lo")
    t = lax.axis_index("tensor")
    z, xx = hi // 2, hi % 2
    y, c = t // 2, t % 2
    dev = lambda h, tt: (h, lo, tt)
    mate = dev(hi, 2 * y + 1 - c)
    ynb = dev(hi, 2 * (1 - y) + c)
    ymate = dev(hi, 2 * (1 - y) + 1 - c)
    xnb = dev(2 * z + 1 - xx, t)

    def zdev(k):
        return dev(2 * ((z + k) % NZ) + xx, t)

    def block_of(k):
        return 2 * ((y + k // 2) % 2) + (c + k % 2) % 2

    def rows(start, size, mult=None):
        return pl.ds(pl.multiple_of(start, mult or size), size)

    def block_rows(k):
        return rows(block_of(k) * B, B)

    def rcopy(src, dst, send, recv, target):
        return pltpu.make_async_remote_copy(
            src_ref=src,
            dst_ref=dst,
            send_sem=send,
            recv_sem=recv,
            device_id=target,
            device_id_type=MESH,
        )

    LOADS = (X_IN, G_IN, QKV, OUT, FC, PROJ)

    def load(name):
        return pltpu.make_async_copy(r[name + "_hbm"], r[name + "_in"], r.load_sem.at[LOADS.index(name)])

    for name in LOADS:
        load(name).start()

    barrier = pltpu.get_barrier_semaphore()
    peers = [dev((hi + k) % n, t) for k in range(1, n)] + [mate, ynb, ymate]
    for peer in peers:
        pl.semaphore_signal(barrier, inc=1, device_id=peer, device_id_type=MESH)

    def a2a(tag, k, source, target):
        sem = r.a2a_sem
        to = (hi + k) % n
        return rcopy(source(to), target(hi), sem.at[0, tag, k - 1], sem.at[1, tag, k - 1], dev(to, t))

    def a2a_in_copy(tag, k):
        return a2a(
            tag,
            k,
            lambda to: r.sent.at[tag, to],
            lambda me: r.came.at[tag, rows(me * PR, PR)],
        )

    def a2a_out_copy(tag, k):
        return a2a(
            2 + tag,
            k,
            lambda to: r.made.at[tag, rows(to * PR, PR)],
            lambda me: backs[tag].at[me],
        )

    def pick_pieces(tag, source):
        def one(k, _):
            where = jnp.int32(0)
            for j in range(n):
                where = jnp.where(r.order[j] == k, j, where)
            r.sent[tag, k] = source[where]
            return 0

        lax.fori_loop(0, n, one, 0)
        r.came[tag, rows(hi * PR, PR)] = r.sent[tag, hi]

    load(X_IN).wait()
    if inside:
        pick_pieces(0, r.x_in)
    pl.semaphore_wait(barrier, len(peers))
    if inside:
        for k in range(1, n):
            a2a_in_copy(0, k).start()
    else:
        r.came[0] = r.x_in[...]
    for j, vec in enumerate((r.ln1g, r.ln1b, r.aob, r.ln2g, r.ln2b, r.pjb, r.fcb)):
        for i in range(vec.shape[0]):
            r.vecs[j : j + 1, i * 128 : (i + 1) * 128] = vec[i : i + 1]

    WG = (PAIR, LAST, OUT, FC, PROJ)
    STRAIGHT = (PAIR,)
    middle = (z == 1) | (z == 2)
    side = z // 2
    near, far_mid, far_end = z + 1 - 2 * (z % 2), 2 - side, 3 - 3 * side
    Z_FROM = (near, far_mid, far_end)
    near_dev = dev(2 * near + xx, t)

    def wslot(name, ref, slot):
        return ref.at[rows(slot * WR, WR, 16)]

    def gslot(name, slot):
        high = WR // 2 if name in (LAST, OUT) else WR
        return r[GR[name]].at[rows(slot * high, high, 16)]

    def wg_z(name, i):
        sem = r.wg_sem
        a = WG.index(name)
        if i < 2:
            slot = wslot(name, r[name], hi)
            target = (near_dev, dev(2 * far_mid + xx, t))[i]
            recv = (0, jnp.where(middle, 1, 2))[i]
        elif name in STRAIGHT:
            slot = wslot(name, r[name], hi)
            target = dev(2 * far_end + xx, t)
            recv = jnp.where(middle, 1, 2)
        else:
            slot = wslot(name, r[name], 2 * Z_FROM[i - 1] + xx)
            target = near_dev
            recv = i - 1
        return rcopy(slot, slot, sem.at[0, a, i], sem.at[1, a, recv], target)

    def wg_in(name, i):
        sem = r.wg_sem
        a = WG.index(name)
        slot = wslot(name, r[name], 2 * Z_FROM[i] + xx)
        return rcopy(slot, slot, sem.at[0, a, 3], sem.at[1, a, i], near_dev)

    def wg_x(name, i):
        sem = r.wg_sem
        a = WG.index(name)
        slot = wslot(name, r[name], 2 * (Z_FROM + (z,))[i] + xx)
        return rcopy(slot, slot, sem.at[0, a, 4 + i], sem.at[1, a, 4 + i], xnb)

    def wg_near(name):
        wg_in(name, 0).wait_recv()
        wg_x(name, 0).start()

    def wg_mids(name):
        @pl.when(middle)
        def _():
            for i in (1, 2):
                wg_in(name, i).wait_recv()
                wg_z(name, i + 1).start()
                wg_x(name, i).start()

    def wg_second(name):
        if name in STRAIGHT:
            for i in (1, 2):
                wg_in(name, i).wait_recv()
                wg_x(name, i).start()
            return

        @pl.when(jnp.logical_not(middle))
        def _():
            for i in (1, 2):
                wg_in(name, i).wait_recv()
                wg_x(name, i).start()

    def wg_wait(name):
        for i in range(NZ):
            wg_x(name, i).wait_recv()

    def wg_drain(name):
        for i in range(2):
            wg_z(name, i).wait_send()
        for i in range(NZ):
            wg_x(name, i).wait_send()
        if name in STRAIGHT:
            wg_z(name, 2).wait_send()
            return

        @pl.when(middle)
        def _():
            for i in (2, 3):
                wg_z(name, i).wait_send()

    own_w = rows(hi * WR, WR, 16)
    load(QKV).wait()
    for i in range(3):
        part = r.wqkv_in[i].astype(BF)
        r.wa[own_w, i * PW : (i + 1) * PW] = part[:, :PW]
        r.wb[own_w, i * LW : (i + 1) * LW] = part[:, PW:]
    for name in (PAIR, LAST):
        wg_x(name, 3).start()
        wg_z(name, 0).start()
    for name in LOADS[3:]:
        load(name).wait()
    r.w1[own_w] = r.w1_in[...].astype(BF)
    r.w2[own_w] = r.w2_in[...].astype(BF)
    r.turn[...] = jnp.zeros_like(r.turn)
    r.turn[:HC, :WR] = r.wo_in[...].astype(F32)
    r.wo[own_w] = r.turn[...].T[:WR, :HC].astype(BF)
    for name in (OUT, FC, PROJ):
        wg_x(name, 3).start()
    wg_z(OUT, 0).start()
    load(G_IN).wait()
    if inside:
        pick_pieces(1, r.g_in)
    else:
        r.came[1] = r.g_in[...]

    AG = (H1, GF, H2, DR)

    def ag(name, kind, ch):
        sem = r.ag_sem
        a = AG.index(name)
        full = r[name]
        if kind == 2:
            where = rows(block_of(2) * B + ch * CR, CR)
        else:
            where = rows(t * B + ch * CR, CR)
        target = ynb if kind == 0 else mate
        part = full.at[where]
        return rcopy(part, part, sem.at[0, a, kind, ch], sem.at[1, a, kind, ch], target)

    def ag_send(name, ch):
        ag(name, 0, ch).start()
        ag(name, 1, ch).start()

    def ag_forward(name, ch):
        ag(name, 0, ch).wait_recv()
        ag(name, 2, ch).start()

    def ag_arrive(name, k):
        for ch in range(CHUNKS):
            if k == 1:
                ag(name, 1, ch).wait_recv()
            elif k == 2:
                ag_forward(name, ch)
            else:
                ag(name, 2, ch).wait_recv()

    def ag_drain(name):
        for kind in range(3):
            for ch in range(CHUNKS):
                ag(name, kind, ch).wait_send()

    def rs_bufs(tag):
        if tag == 3:
            return r.msy, r.mry, r.keepy, r.ysy, r.yry
        return r.msc, r.mrc, r.keepc, r.ysc, r.yrc

    def rs_m(tag, i):
        ms, mr, _, _, _ = rs_bufs(tag)
        sem = r.rs_sem
        return rcopy(ms.at[i], mr.at[i], sem.at[0, tag, i], sem.at[1, tag, i], mate)

    def chunk_at(tag, ch):
        return (1 - side + ch) % CHUNKS * CR if tag == 2 else ch * CR

    def rs_y(tag, ch):
        _, _, _, ys, yr = rs_bufs(tag)
        sem = r.rs_sem
        where = rows(chunk_at(tag, ch), CR)
        return rcopy(ys.at[where], yr.at[where], sem.at[0, tag, 2 + ch], sem.at[1, tag, 2 + ch], ynb)

    def rs_put(tag, k, value, at=None):
        ms, _, keep, _, _ = rs_bufs(tag)
        where = slice(None) if at is None else at
        i = 0 if k >= 2 else 1
        if k % 2:
            ms[i, where] = value.astype(BF)
        else:
            keep[i, where] = value

    def rs_ship(tag):
        _, mr, keep, ys, _ = rs_bufs(tag)
        rs_m(tag, 0).wait_recv()
        for ch in range(CHUNKS):

            def one(s, _):
                at = rows(chunk_at(tag, ch) + s * STEP, STEP)
                ys[at] = (keep[0, at] + mr[0, at].astype(F32)).astype(BF)
                return 0

            lax.fori_loop(0, CR // STEP, one, 0)
            rs_y(tag, ch).start()

    def rs_total(tag, at):
        _, mr, keep, _, yr = rs_bufs(tag)
        return keep[1, at] + mr[1, at].astype(F32) + yr[at].astype(F32)

    def rs_drain(tag):
        for i in range(2):
            rs_m(tag, i).wait_send()
        for ch in range(CHUNKS):
            rs_y(tag, ch).wait_send()

    GS = WG + ZFIRST
    GR = {name: "g" + name for name in GS}
    HF = FH // 2

    def gr_x(name, k):
        sem = r.gr_sem
        a = GS.index(name)
        slot = gslot(name, 2 * k + 1 - xx)
        return rcopy(slot, r[name + "_xr"].at[k], sem.at[0, a, k], sem.at[1, a, k], xnb)

    def gr_z(name, i):
        sem = r.gr_sem
        a = GS.index(name)
        to_mid, to_end = dev(2 * far_mid + xx, t), dev(2 * far_end + xx, t)
        if name in ZFIRST:
            to, source = (near_dev, to_mid, to_end)[i], i
            recv = 0 if i == 0 else jnp.where(middle, 1, 2)
        else:
            to = {0: near_dev, 2: near_dev, 3: near_dev, 1: to_mid, 4: to_end}[i]
            source = {0: 0, 2: 1, 3: 2, 1: 1, 4: 2}[i]
            recv = 1 if i == 4 else i
        part = two(name, Z_FROM[source]) if name in ZFIRST else r[name + "_zs"].at[source]
        return rcopy(part, r[name + "_zr"].at[recv], sem.at[0, a, NZ + i], sem.at[1, a, NZ + recv], to)

    def gr_zin(name, i):
        sem = r.gr_sem
        a = GS.index(name)
        part = r[name + "_zr"].at[i]
        return rcopy(part, part, sem.at[0, a, NZ], sem.at[1, a, NZ + i], near_dev)

    def two(name, place):
        return r[GR[name]].at[rows(2 * place * WR, 2 * WR, 32)]

    def z_start(name):
        for i in range(3):
            gr_z(name, i).start()

    def x_last(name):
        sem = r.gr_sem
        a = GS.index(name)
        return rcopy(r[name + "_xs"], r[name + "_xr"], sem.at[0, a, 0], sem.at[1, a, 0], xnb)

    def z_end(name, out):
        zr = r[name + "_zr"]
        came = range(3)
        for i in came:
            gr_zin(name, i).wait_recv()

        def total(k):
            value = r[GR[name]][rows((2 * z + k) * WR, WR, 16)].astype(F32)
            at = rows(k * WR, WR, 16)
            for i in came:
                value = value + zr[i, at].astype(F32)
            return value

        r[name + "_xs"][...] = total(1 - xx).astype(BF)
        x_last(name).start()
        out[:, HF:] = total(xx)

    def z_finish(name, out):
        x_last(name).wait_recv()
        out[:, HF:] += r[name + "_xr"][...].astype(F32)

    def gr_start(name):
        for k in range(NZ):
            gr_x(name, k).start()

    def gr_pair(name, to):
        mine = gslot(name, 2 * to + xx)[...].astype(F32)
        return mine + r[name + "_xr"][to].astype(F32)

    def gr_mid(name):
        for k in range(NZ):
            gr_x(name, k).wait_recv()
        zs = r[name + "_zs"]
        zs[0] = gr_pair(name, near).astype(BF)
        gr_z(name, 0).start()

        @pl.when(jnp.logical_not(middle))
        def _():
            zs[1] = gr_pair(name, far_mid).astype(BF)
            gr_z(name, 2).start()
            zs[2] = gr_pair(name, far_end).astype(BF)
            gr_z(name, 3).start()

    def gr_far(name):
        @pl.when(middle)
        def _():
            zs, zr = r[name + "_zs"], r[name + "_zr"]
            gr_zin(name, 2).wait_recv()
            zs[1] = (gr_pair(name, far_mid) + zr[2].astype(F32)).astype(BF)
            gr_z(name, 1).start()
            gr_zin(name, 3).wait_recv()
            zs[2] = (gr_pair(name, far_end) + zr[3].astype(F32)).astype(BF)
            gr_z(name, 4).start()

    def gr_finish(name):
        total = gr_pair(name, z)
        for i in range(2):
            gr_zin(name, i).wait_recv()
            total = total + r[name + "_zr"][i].astype(F32)
        return total

    def gr_drain(name):
        if name in ZFIRST:
            x_last(name).wait_send()
        else:
            for k in range(NZ):
                gr_x(name, k).wait_send()
        gr_z(name, 0).wait_send()
        if name in ZFIRST:
            gr_z(name, 1).wait_send()
            gr_z(name, 2).wait_send()
            return

        @pl.when(middle)
        def _():
            gr_z(name, 1).wait_send()
            gr_z(name, 4).wait_send()

        @pl.when(jnp.logical_not(middle))
        def _():
            gr_z(name, 2).wait_send()
            gr_z(name, 3).wait_send()

    tpeers = [mate, ynb, ymate]
    SHARED = (32, 16)

    def sm_t(tag, i):
        sem = r.sm_sem
        part = slabs[tag].at[t]
        return rcopy(part, part, sem.at[0, tag, i], sem.at[1, tag, i], tpeers[i])

    def sm_h(tag, k):
        sem = r.sm_sem
        part = hslabs[tag].at[hi]
        return rcopy(part, part, sem.at[0, tag, 3 + k], sem.at[1, tag, 3 + k], dev((hi + k) % n, t))

    def spread(tag, at, value):
        for j in range(value.shape[1] // 128):
            slabs[tag][t, at + j : at + j + 1] = value[:, j * 128 : (j + 1) * 128]

    def sm_start(tag):
        for i in range(3):
            sm_t(tag, i).start()

    def sm_mid(tag):
        for i in range(3):
            sm_t(tag, i).wait_recv()
        slab, hslab = slabs[tag], hslabs[tag]
        total = slab[0]
        for i in range(1, 4):
            total = total + slab[i]
        if tag == 0:
            keep = lax.broadcasted_iota(jnp.int32, total.shape, 0) < SHARED[0]
            total = jnp.where(keep, total, slab[t])
        hslab[hi] = total.astype(BF)
        for k in range(1, n):
            sm_h(tag, k).start()

    def sm_finish(tag):
        for k in range(1, n):
            sm_h(tag, k).wait_recv()
        hslab = hslabs[tag]
        total = hslab[0].astype(F32)
        for k in range(1, n):
            total = total + hslab[k].astype(F32)
        return total

    def sm_drain(tag):
        for i in range(3):
            sm_t(tag, i).wait_send()
        for k in range(1, n):
            sm_h(tag, k).wait_send()

    def fold(value):
        return jnp.sum(value.reshape(value.shape[0] // 8, 8, value.shape[1]), axis=0)

    for slab in slabs:
        slab[t] = jnp.zeros(slab.shape[1:], F32)
    r.acc[...] = jnp.zeros_like(r.acc)
    r.acc_f[...] = jnp.zeros_like(r.acc_f)
    r.acc_a[...] = jnp.zeros_like(r.acc_a)
    r.acc_b[...] = jnp.zeros_like(r.acc_b)

    if inside:
        for k in range(1, n):
            a2a_in_copy(0, k).wait_recv()
    for name in STRAIGHT:
        wg_z(name, 1).start()
        wg_z(name, 2).start()
    wg_z(LAST, 1).start()
    wg_z(FC, 0).start()

    def norm_step(values, at, gain, bias, cen, scale):
        mean = jnp.mean(values, axis=1, keepdims=True)
        var = jnp.mean(values * values, axis=1, keepdims=True) - mean * mean
        inv = lax.rsqrt(var + EPSILON)
        centered = (values - mean) * inv
        cen[at] = centered
        scale[at] = inv
        return (centered * gain + bias).astype(BF)

    def norm_back(grad, at, gain, cen, scale, acc_at):
        centered = cen[at]
        r.acc[acc_at] += fold(grad * centered)
        r.acc[acc_at + 1] += fold(grad)
        scaled = grad * gain
        return scale[at] * (
            scaled
            - jnp.mean(scaled, axis=1, keepdims=True)
            - centered * jnp.mean(scaled * centered, axis=1, keepdims=True)
        )

    for ch in range(CHUNKS):

        def one(s, _):
            at = rows(ch * CR + s * STEP, STEP)
            values = r.came[0, at].astype(F32)
            r.h1[rows(t * B + ch * CR + s * STEP, STEP)] = norm_step(
                values, at, r.vecs[0:1], r.vecs[1:2], r.cen1, r.scale1
            )
            return 0

        lax.fori_loop(0, CR // STEP, one, 0)
        ag_send(H1, ch)

    for name in (PAIR, LAST, OUT):
        wg_near(name)
    wg_second(PAIR)
    wg_mids(LAST)
    wg_z(OUT, 1).start()
    ag_arrive(H1, 1)
    ag_arrive(H1, 2)
    wg_second(LAST)
    if inside:
        for k in range(1, n):
            a2a_in_copy(1, k).start()
    wg_wait(PAIR)
    wg_wait(LAST)
    wg_mids(OUT)
    wg_near(FC)
    wg_z(FC, 1).start()
    wg_z(PROJ, 0).start()

    lane = lax.broadcasted_iota(jnp.int32, (1, PW), 1)

    def head_mask(h):
        return (lane >= h * HEAD_DIM) & (lane < (h + 1) * HEAD_DIM)

    def project(s, _):
        @pl.when(s == 3)
        def _():
            ag_arrive(H1, 3)

        b = block_of(s)
        at = rows(b * B, B)
        hidden = r.h1[at]

        def scaled(q):
            return (q.astype(BF).astype(F32) * HEAD_DIM ** (-0.5)).astype(BF)

        both = dot(hidden, r.wa[...], NN)
        q = scaled(both[:, :PW] + r.qvb[0:1, :PW])
        for h in range(NH - 1):
            r.qa[b, h * B : (h + 1) * B] = jnp.where(head_mask(h), q, jnp.zeros_like(q))
        k = both[:, PW : 2 * PW]
        r.ka[at] = k.astype(BF)
        r.kt[:PW, at] = k.T.astype(BF)
        v = both[:, 2 * PW :] + r.qvb[1:2, :PW]
        r.va[at] = v.astype(BF)
        r.vt[:PW, at] = v.T.astype(BF)
        last = dot(hidden, r.wb[...], NN)
        r.qb[b] = scaled(last[:, :LW] + r.qvb[0:1, PW:])
        r.kb[at] = last[:, LW : 2 * LW].astype(BF)
        r.vb[at] = (last[:, 2 * LW :] + r.qvb[1:2, PW:]).astype(BF)
        turned = last.T
        r.kt[PW:, at] = turned[LW : 2 * LW].astype(BF)
        r.vt[PW:, at] = (turned[2 * LW :] + r.vbt[...]).astype(BF)
        return 0

    bias_last = jnp.concatenate([r.qvb[1:2, PW:], jnp.zeros((1, LW), F32)], axis=1)
    r.vbt[...] = jnp.broadcast_to(bias_last, (8, 2 * LW)).T[:LW, :1]
    lax.fori_loop(0, 4, project, 0)
    wg_second(OUT)
    wg_near(PROJ)
    wg_z(PROJ, 1).start()

    def own_grad(s, _):
        at = rows(s * STEP, STEP)
        value = r.came[1, at]
        r.gf[rows(t * B + s * STEP, STEP)] = value
        r.acc[5] += fold(value.astype(F32))
        return 0

    def grad_in():
        if inside:
            for k in range(1, n):
                a2a_in_copy(1, k).wait_recv()
        lax.fori_loop(0, B // STEP, own_grad, 0)
        for ch in range(CHUNKS):
            ag_send(GF, ch)


    pack = hi * (packs // n) + lo

    def attend(i):
        pos = i * B + lax.broadcasted_iota(jnp.int32, (1, B), 1)
        first = jnp.zeros((1, B), jnp.int32)
        end = jnp.int32(0)
        for s in range(r.lengths.shape[0]):
            length = r.lengths[s, pack]
            end = end + length
            first = first + jnp.where(pos >= end, length, 0)

        def scores(j, peak):
            key_pos = j * KB + lax.broadcasted_iota(jnp.int32, (KB, B), 0)
            allowed = (key_pos >= first) & (key_pos <= pos)
            kr = rows(j * KB, KB)
            keys, keys_last = r.ka[kr], r.kb[kr]
            peaks = []
            for h in range(NH):
                if h < NH - 1:
                    raw = dot(keys, r.qa[i, h * B : (h + 1) * B], NT)
                else:
                    raw = dot(keys_last, r.qb[i], NT)
                raw = jnp.where(allowed, raw, MASKED)
                r.score[kr, h * B : (h + 1) * B] = raw
                peaks.append(jnp.max(raw, axis=0, keepdims=True))
            return jnp.maximum(peak, jnp.concatenate(peaks, axis=1))

        peak = lax.fori_loop(0, (i + KS) // KS, scores, jnp.full((1, NH * B), MASKED, F32))
        r.att[...] = jnp.zeros_like(r.att)

        def weigh(j, total):
            totals = []
            for h in range(NH):
                cols = slice(h * B, (h + 1) * B)
                weight = jnp.exp(r.score[rows(j * KB, KB), cols] - peak[:, cols])
                totals.append(jnp.sum(weight, axis=0, keepdims=True))
                low = weight.astype(BF)
                r.e[i, rows(j * KB, KB), cols] = low
                part = slice(h * HEAD_DIM, (h + 1) * HEAD_DIM)
                r.att[part] += dot(r.vt[part, rows(j * KB, KB)], low, NN)
            return total + jnp.concatenate(totals, axis=1)

        total = lax.fori_loop(0, (i + KS) // KS, weigh, jnp.zeros((1, NH * B), F32))
        inverse = 1.0 / total
        for h in range(NH):
            part = slice(h * HEAD_DIM, (h + 1) * HEAD_DIM)
            own = inverse[:, h * B : (h + 1) * B]
            r.att[part] = r.att[part] * own
            r.inv[i, h : h + 1] = own
        out = r.att[...].T
        at = rows(i * B, B)
        r.a[at] = out
        r.al[at] = out.astype(BF)

    def attend_step(s, _):
        k = 3 - s
        i = block_of(k)
        attend(i)

        @pl.when(s == 0)
        def _():
            wg_wait(OUT)

        part = dot(r.al[rows(i * B, B)], r.wo[...], NT)

        @pl.when(s == 0)
        def _():
            rs_put(0, 3, part)
            rs_m(0, 0).start()
            wg_mids(FC)

        @pl.when(s == 1)
        def _():
            rs_put(0, 2, part)
            rs_ship(0)

        @pl.when(s == 2)
        def _():
            rs_put(0, 1, part)
            rs_m(0, 1).start()
            wg_mids(PROJ)

        @pl.when(s == 3)
        def _():
            rs_put(0, 0, part)

        return 0

    grad_in()
    lax.fori_loop(0, 4, attend_step, 0)
    wg_second(FC)

    rs_m(0, 1).wait_recv()
    for ch in range(CHUNKS):
        if ch == CHUNKS - 1:
            wg_second(PROJ)
        rs_y(0, ch).wait_recv()

        def one(s, _):
            at = rows(ch * CR + s * STEP, STEP)
            values = r.came[0, at].astype(F32) + rs_total(0, at) + r.vecs[2:3]
            r.res[at] = values
            r.h2[rows(t * B + ch * CR + s * STEP, STEP)] = norm_step(
                values, at, r.vecs[3:4], r.vecs[4:5], r.cen2, r.scale2
            )
            return 0

        lax.fori_loop(0, CR // STEP, one, 0)
        ag_send(H2, ch)
    rs_drain(0)
    wg_wait(FC)
    wg_wait(PROJ)

    def feed(s, _):
        @pl.when(s == 1)
        def _():
            ag_arrive(GF, 1)
            ag_arrive(H2, 1)

        @pl.when(s == 2)
        def _():
            ag_arrive(GF, 2)
            ag_arrive(H2, 2)

        @pl.when(s == 3)
        def _():
            ag_arrive(GF, 3)
            ag_arrive(H2, 3)

        at = block_rows(s)
        hidden = r.h2[at]
        grad = r.gf[at]
        for j in range(FH // 256):
            cols = slice(j * 256, (j + 1) * 256)
            u = dot(hidden, r.w1[:, cols], NN) + r.vecs[6:7, cols]
            dz = dot(grad, r.w2[:, cols], NN)
            square = u * u
            half = 0.5 + 0.5 * jnp.tanh(u * (CURVE + (CURVE * CUBE) * square))
            act = u * half
            r.zz[at, cols] = act.astype(BF)
            slope = half + act * (1.0 - half) * (2.0 * CURVE + (6.0 * CURVE * CUBE) * square)
            low = (dz * slope).astype(BF)
            r.du[at, cols] = low
            r.acc_f[:, cols] += fold(low.astype(F32))
        part = dot(r.du[at], r.w1[...], NT)

        @pl.when(s == 0)
        def _():
            rs_put(1, 0, part)

        @pl.when(s == 1)
        def _():
            rs_put(1, 1, part)
            rs_m(1, 1).start()

        @pl.when(s == 2)
        def _():
            rs_put(1, 2, part)

        @pl.when(s == 3)
        def _():
            rs_put(1, 3, part)
            rs_m(1, 0).start()

        return 0

    lax.fori_loop(0, 4, feed, 0)
    rs_ship(1)

    def grad_halves(left, right, out):
        def one(i, _):
            value = dot(left[:, rows(i * 384, 384)], right[...], TN)
            for j in range(384 // WR):
                first, second = (2 * j) * WR // 2, (2 * j + 1) * WR // 2
                both = jnp.concatenate(
                    [value[first : first + WR // 2], value[second : second + WR // 2]], axis=1
                )
                out[rows((i * (384 // WR) + j) * (WR // 2), WR // 2, 16)] = both.astype(BF)
            return 0

        lax.fori_loop(0, D // 384, one, 0)

    def grad_tiles(left, right, out, cols=slice(None)):
        def one(i, _):
            at = rows(i * 256, 256)
            out[at] = dot(left[:, at], right[:, cols], TN).astype(BF)
            return 0

        lax.fori_loop(0, D // 256, one, 0)

    grad_tiles(r.gf, r.zz, r.gw2z, slice(HF, FH))
    z_start(PROJ_Z)
    grad_tiles(r.gf, r.zz, r.gw2, slice(0, HF))
    gr_start(PROJ)
    grad_tiles(r.h2, r.du, r.gw1z, slice(HF, FH))
    z_start(FC_Z)
    grad_tiles(r.h2, r.du, r.gw1, slice(0, HF))
    gr_start(FC)

    rs_m(1, 1).wait_recv()
    for ch in range(CHUNKS):
        rs_y(1, ch).wait_recv()

        def one(s, _):
            at = rows(ch * CR + s * STEP, STEP)
            back = norm_back(rs_total(1, at), at, r.vecs[3:4], r.cen2, r.scale2, 2)
            grad = r.came[1, at].astype(F32) + back
            r.dres[at] = grad
            r.acc[4] += fold(grad)
            r.dr[rows(t * B + ch * CR + s * STEP, STEP)] = grad.astype(BF)
            return 0

        lax.fori_loop(0, CR // STEP, one, 0)
        ag_send(DR, ch)
    rs_drain(1)

    def upper(s, _):
        k = 3 - s
        part = dot(r.zz[block_rows(k)], r.w2[...], NT)

        @pl.when(s == 0)
        def _():
            rs_put(3, 3, part)
            rs_m(3, 0).start()

        @pl.when(s == 1)
        def _():
            rs_put(3, 2, part)

        @pl.when(s == 2)
        def _():
            rs_put(3, 1, part)
            rs_m(3, 1).start()

        @pl.when(s == 3)
        def _():
            rs_put(3, 0, part)

        return 0

    lax.fori_loop(0, 4, upper, 0)

    lanes = lax.broadcasted_iota(jnp.int32, (1, HC), 1)
    LB = (NH - 1) * B

    def attend_back(i):
        at = rows(i * B, B)
        da = dot(r.dr[at], r.wo[...], NN).astype(BF).astype(F32)
        by_row = r.inv[i].T
        scale = by_row[:, NH - 1 : NH]
        for h in range(NH - 1):
            scale = jnp.where(lanes // HEAD_DIM == h, by_row[:, h : h + 1], scale)
        low = (da * scale).astype(BF)
        pair = low[:, :PW]
        for h in range(NH - 1):
            r.dama[h * B : (h + 1) * B] = jnp.where(head_mask(h), pair, jnp.zeros_like(pair))
        r.damb[at] = low[:, PW:]
        lined = (low.astype(F32) * r.a[at]).T
        deltas = [
            jnp.sum(lined[h * HEAD_DIM : (h + 1) * HEAD_DIM], axis=0, keepdims=True)
            for h in range(NH)
        ]
        r.inv[i, 4:5] = deltas[NH - 1]
        r.att[:PW] = jnp.zeros((PW, B), F32)

        def over_keys(j, _):
            kr = rows(j * KB, KB)
            values = r.va[kr]
            for h in range(NH - 1):
                own = slice(h * B, (h + 1) * B)
                dp = dot(values, r.dama[own], NT)
                ds = (r.e[i, kr, own].astype(F32) * (dp - deltas[h])).astype(BF)
                r.ds[:, own] = ds
                part = slice(h * HEAD_DIM, (h + 1) * HEAD_DIM)
                r.att[part] += dot(r.kt[part, kr], ds, NN)
            r.dka[kr] += dot(r.ds[...], r.qa[i], NN)
            r.dva[kr] += dot(r.e[i, kr, :LB], r.dama[...], NN)
            return 0

        lax.fori_loop(0, (i + KS) // KS, over_keys, 0)
        r.dqa[at, :PW] = (r.att[:PW].T * HEAD_DIM ** (-0.5)).astype(BF)

    def attend_back_last():
        blocks = S // B
        for i in reversed(range(blocks)):
            at, keys = slice(i * B, (i + 1) * B), slice(0, (i + 1) * B)
            grad = r.damb[at]
            dp = dot(r.vb[keys], grad, NT)
            weight = r.e[i, keys, LB:]
            ds = (weight.astype(F32) * (dp - r.inv[i, 4:5])).astype(BF)
            dq = dot(r.kt[PW:, keys], ds, NN)
            dk, dv = dot(ds, r.qb[i], NN), dot(weight, grad, NN)
            if i == blocks - 1:
                r.dkb[...], r.dvb[...] = dk, dv
            else:
                r.dkb[keys] += dk
                r.dvb[keys] += dv
            dq = jnp.concatenate([dq, dq], axis=0).T[:, :LW]
            r.dqb[at, :LW] = (dq * HEAD_DIM ** (-0.5)).astype(BF)

    def round_kv(which):
        width, dk, dv, dqkv = ((PW, r.dka, r.dva, r.dqa), (LW, r.dkb, r.dvb, r.dqb))[which]

        def one(b, _):
            at = rows(b * B, B)
            dqkv[at, width : 2 * width] = dk[at].astype(BF)
            dqkv[at, 2 * width :] = dv[at].astype(BF)
            acc = (r.acc_a, r.acc_b)[which]
            acc[...] += fold(dqkv[at].astype(F32))
            return 0

        lax.fori_loop(0, 4, one, 0)

    for zeroed in (r.dka, r.dva):
        zeroed[...] = jnp.zeros_like(zeroed)

    def pair_step(s, _):
        @pl.when(s == 1)
        def _():
            ag_arrive(DR, 1)

        @pl.when(s == 2)
        def _():
            ag_arrive(DR, 2)
            rs_ship(3)
            gr_mid(PROJ)

        @pl.when(s == 3)
        def _():
            ag_arrive(DR, 3)
            gr_mid(FC)
            grad_halves(r.dr, r.al, r.gwo)
            gr_start(OUT)

        attend_back(block_of(s))
        return 0

    lax.fori_loop(0, 4, pair_step, 0)
    round_kv(0)
    grad_tiles(r.h1, r.dqa, r.gwa)
    gr_start(PAIR)
    gr_far(PROJ)
    z_end(PROJ_Z, r.out_w2_v)

    def upper_back():
        rs_m(3, 1).wait_recv()
        for ch in range(CHUNKS):
            rs_y(3, ch).wait_recv()

        def finish_up(s, _):
            at = rows(s * STEP, STEP)
            r.made[0, at] = (r.res[at] + rs_total(3, at) + r.vecs[5:6]).astype(BF)
            return 0

        lax.fori_loop(0, B // STEP, finish_up, 0)
        if inside:
            for k in range(1, n):
                a2a_out_copy(0, k).start()
            r.back0[hi] = r.made[0, rows(hi * PR, PR)]
        else:
            r.out_y_v[...] = r.made[0]

    attend_back_last()
    round_kv(1)
    gr_mid(OUT)
    upper_back()

    def lower(s, _):
        k = 3 - s
        at = block_rows(k)
        part = dot(r.dqa[at], r.wa[...], NT) + dot(r.dqb[at], r.wb[...], NT)

        @pl.when(s == 0)
        def _():
            rs_put(2, 3, part)
            rs_m(2, 0).start()

        @pl.when(s == 1)
        def _():
            rs_put(2, 2, part)
            rs_ship(2)

        @pl.when(s == 2)
        def _():
            rs_put(2, 1, part)
            rs_m(2, 1).start()

        @pl.when(s == 3)
        def _():
            rs_put(2, 0, part)

        return 0

    lax.fori_loop(0, 4, lower, 0)

    grad_halves(r.h1, r.dqb, r.gwb)
    gr_start(LAST)
    gr_far(FC)
    z_end(FC_Z, r.out_w1_v)
    gr_far(OUT)

    def line(value):
        return jnp.sum(value, axis=0, keepdims=True)

    for j, at in enumerate((5, 2, 3, 4)):
        spread(0, 8 * j, line(r.acc[at]))
    spread(0, 32, line(r.acc_f[...]))
    pad = jnp.zeros((1, 256 - HC), F32)
    pair, last = line(r.acc_a[...]), line(r.acc_b[...])
    for j in range(2):
        spread(0, 40 + 2 * j, pair[:, 2 * j * PW : (2 * j + 1) * PW])
        r.slab0[t, 41 + 2 * j : 42 + 2 * j, :LW] = last[:, 2 * j * LW : (2 * j + 1) * LW]
    sm_start(0)
    gr_mid(PAIR)

    rs_m(2, 1).wait_recv()
    for ch in range(CHUNKS):
        if ch == CHUNKS - 1:
            sm_mid(0)
        rs_y(2, ch).wait_recv()

        def one(s, _):
            at = rows(chunk_at(2, ch) + s * STEP, STEP)
            back = norm_back(rs_total(2, at), at, r.vecs[0:1], r.cen1, r.scale1, 0)
            r.made[1, at] = (r.dres[at] + back).astype(BF)
            return 0

        lax.fori_loop(0, CR // STEP, one, 0)
        if inside:

            def send(j, _):
                to = chunk_at(2, ch) // PR + j

                @pl.when(to != hi)
                def _():
                    a2a_out_copy(1, (to - hi + n) % n).start()

                return 0

            lax.fori_loop(0, CR // PR, send, 0)

    rs_drain(2)
    rs_drain(3)
    if inside:
        r.back1[hi] = r.made[1, rows(hi * PR, PR)]
    else:
        r.out_x_v[...] = r.made[1]
    for j in range(2):
        spread(1, 8 * j, line(r.acc[j]))
    sm_start(1)
    gr_mid(LAST)
    gr_far(PAIR)
    sm_mid(1)
    gr_far(LAST)

    OUTS = tuple(outputs(cfg))

    def store(name):
        return pltpu.make_async_copy(r[name + "_v"], r[name], r.store_sem.at[OUTS.index(name)])

    def put_back(tag, out):
        for k in range(1, n):
            a2a_out_copy(tag, k).wait_recv()

        def one(j, _):
            out[j] = backs[tag][r.order[j]]
            return 0

        lax.fori_loop(0, n, one, 0)

    z_finish(PROJ_Z, r.out_w2_v)
    r.out_w2_v[:, :HF] = gr_finish(PROJ)
    store(OUT_W2).start()
    z_finish(FC_Z, r.out_w1_v)
    r.out_w1_v[:, :HF] = gr_finish(FC)
    store(OUT_W1).start()
    if inside:
        put_back(0, r.out_y_v)
    store(OUT_Y).start()
    r.turn[...] = jnp.zeros_like(r.turn)
    packed = gr_finish(OUT)
    r.turn[: WR // 2, :HC] = packed[:, :HC]
    r.turn[WR // 2 : WR, :HC] = packed[:, HC:]
    r.out_wo_v[...] = r.turn[...].T[:HC, :WR]
    store(OUT_WO).start()
    r.out_early_v[...] = sm_finish(0)
    store(OUT_EARLY).start()
    if inside:
        put_back(1, r.out_x_v)
    store(OUT_X).start()
    r.out_late_v[...] = sm_finish(1)
    store(OUT_LATE).start()
    total = gr_finish(PAIR)
    for i in range(3):
        r.out_qkv_v[i, :, :PW] = total[:, i * PW : (i + 1) * PW]
    packed = gr_finish(LAST)
    total = jnp.concatenate([packed[:, : 3 * LW], packed[:, 3 * LW :]], axis=0)
    for i in range(3):
        r.out_qkv_v[i, :, PW:] = total[:, i * LW : (i + 1) * LW]
    store(OUT_QKV).start()

    for name in WG:
        wg_drain(name)
    for name in GS:
        gr_drain(name)
    for name in AG:
        ag_drain(name)
    for name in OUTS:
        store(name).wait()
    for tag in range(2):
        sm_drain(tag)
        if inside:
            for k in range(1, n):
                a2a_in_copy(tag, k).wait_send()
                a2a_out_copy(tag, k).wait_send()


def settle(*refs):
    early, late = refs[6:8]
    whole, small = refs[8:14], refs[14:22]
    for i in range(6):
        whole[i][...] = refs[i][...]
    for j in range(4):
        small[j][...] = early[8 * j : 8 * j + small[j].shape[0]]
    for j in range(2):
        small[4 + j][...] = late[8 * j : 8 * j + small[4 + j].shape[0]]
    small[6][...] = early[32 : 32 + small[6].shape[0]]
    heads = small[7]
    for j in range(2):
        heads[j : j + 1, :128] = early[40 + 2 * j : 41 + 2 * j]
        heads[j : j + 1, 128:] = early[41 + 2 * j : 42 + 2 * j, : heads.shape[1] - 128]


def inputs():
    vmem = pl.BlockSpec(memory_space=pltpu.VMEM)
    smem = pl.BlockSpec(memory_space=pltpu.SMEM)
    hbm = pl.BlockSpec(memory_space=pl.ANY)
    return Refs(
        order=smem,
        lengths=smem,
        x_hbm=hbm,
        g_hbm=hbm,
        ln1g=vmem,
        ln1b=vmem,
        wqkv_hbm=hbm,
        qvb=vmem,
        wo_hbm=hbm,
        aob=vmem,
        ln2g=vmem,
        ln2b=vmem,
        w1_hbm=hbm,
        fcb=vmem,
        w2_hbm=hbm,
        pjb=vmem,
    )


def outputs(cfg):
    (n, packs, L, S, D, HC, FH, inside) = cfg
    WR = D // n
    tokens = (n, L // n, D) if inside else (L, D)
    return Refs(
        out_y=(tokens, BF),
        out_x=(tokens, BF),
        out_qkv=((3, WR, HC), F32),
        out_wo=((HC, WR), F32),
        out_w1=((WR, FH), F32),
        out_w2=((WR, FH), F32),
        out_early=((48, 128), F32),
        out_late=((16, 128), F32),
    )


def scratch(cfg):
    (n, packs, L, S, D, HC, FH, inside) = cfg
    NH = HC // HEAD_DIM
    LW = HEAD_DIM
    PW = HC - LW
    NZ = n // 2
    WR = D // n
    V = pltpu.VMEM
    sem = pltpu.SemaphoreType.DMA
    blocks = S // L
    tokens = (n, L // n, D) if inside else (L, D)
    kind = F32 if inside else BF
    made = Refs(
        came=V((2, L, D), BF),
        made=V((2, L, D), BF),
        wa=V((D, 3 * PW), BF),
        wb=V((D, 3 * LW), BF),
        wo=V((D, HC), BF),
        w1=V((D, FH), BF),
        w2=V((D, FH), BF),
        turn=V((256, 256), F32),
        vecs=V((8, D), F32),
        x_in=V(tokens, BF),
        g_in=V(tokens, BF),
        wqkv_in=V((3, WR, HC), kind),
        wo_in=V((HC, WR), kind),
        w1_in=V((WR, FH), kind),
        w2_in=V((WR, FH), kind),
        load_sem=sem((6,)),
        store_sem=sem((8,)),
        h1=V((S, D), BF),
        gf=V((S, D), BF),
        h2=V((S, D), BF),
        dr=V((S, D), BF),
        cen1=V((L, D), F32),
        cen2=V((L, D), F32),
        scale1=V((L, 1), F32),
        scale2=V((L, 1), F32),
        res=V((L, D), F32),
        dres=V((L, D), F32),
        qa=V((blocks, (NH - 1) * L, PW), BF),
        ka=V((S, PW), BF),
        va=V((S, PW), BF),
        qb=V((blocks, L, LW), BF),
        kb=V((S, LW), BF),
        vb=V((S, LW), BF),
        vbt=V((LW, 1), F32),
        kt=V((HC, S), BF),
        vt=V((HC, S), BF),
        score=V((S, NH * L), F32),
        e=V((blocks, S, NH * L), BF),
        att=V((HC, L), F32),
        inv=V((blocks, 8, L), F32),
        a=V((S, HC), F32),
        al=V((S, HC), BF),
        dama=V(((NH - 1) * L, PW), BF),
        damb=V((S, LW), BF),
        ds=V((2 * L, (NH - 1) * L), BF),
        dka=V((S, PW), F32),
        dva=V((S, PW), F32),
        dkb=V((S, LW), F32),
        dvb=V((S, LW), F32),
        dqa=V((S, 3 * PW), BF),
        dqb=V((S, 3 * LW), BF),
        zz=V((S, FH), BF),
        du=V((S, FH), BF),
        acc=V((6, 8, D), F32),
        acc_f=V((8, FH), F32),
        acc_a=V((8, 3 * PW), F32),
        acc_b=V((8, 3 * LW), F32),
        slab0=V((4, 48, 128), F32),
        slab1=V((4, 16, 128), F32),
        hslab0=V((n, 48, 128), BF),
        hslab1=V((n, 16, 128), BF),
    )
    for name, (shape, dtype) in outputs(cfg).items():
        made[name + "_v"] = V(shape, dtype)
    if inside:
        made.update(
            sent=V((2, n, L // n, D), BF),
            back0=V((n, L // n, D), BF),
            back1=V((n, L // n, D), BF),
            a2a_sem=sem((2, 4, n - 1)),
        )
    for late in "cy":
        made["ms" + late] = V((2, L, D), BF)
        made["mr" + late] = V((2, L, D), BF)
        made["keep" + late] = V((2, L, D), F32)
        made["ys" + late] = V((L, D), BF)
        made["yr" + late] = V((L, D), BF)
    for name, width in ((PAIR, 3 * PW), (LAST, 3 * LW), (OUT, HC)) + tuple((name, FH // 2) for name in (FC, PROJ) + ZFIRST):
        packed = 2 if name in (LAST, OUT) else 1
        slot = (WR // packed, width * packed)
        made["g" + name] = V((D // packed, width * packed), BF)
        if name in ZFIRST:
            made[name + "_xs"] = V(slot, BF)
            made[name + "_xr"] = V(slot, BF)
            made[name + "_zr"] = V((3, 2 * WR, width), BF)
            continue
        made[name + "_xr"] = V((NZ,) + slot, BF)
        made[name + "_zs"] = V((NZ - 1,) + slot, BF)
        made[name + "_zr"] = V((NZ,) + slot, BF)
    made.update(
        wg_sem=sem((2, 5, 2 * NZ)),
        gr_sem=sem((2, 7, 2 * NZ + 1)),
        ag_sem=sem((2, 4, 3, CHUNKS)),
        rs_sem=sem((2, 4, 2 + CHUNKS)),
        sm_sem=sem((2, 2, 3 + n)),
    )
    return made


def cfg_names(cfg):
    return tuple(inputs()) + tuple(outputs(cfg)) + tuple(scratch(cfg))


def local(
    n,
    block_input,
    out_cotangent,
    seq_lengths,
    pack_order,
    ln1_gain,
    ln1_bias,
    qkv_weight,
    qv_bias,
    attn_out_weight,
    attn_out_bias,
    ln2_gain,
    ln2_bias,
    fc_weight,
    fc_bias,
    proj_weight,
    proj_bias,
):
    L, D = block_input.shape
    packs = pack_order.shape[0]
    HC = qv_bias.shape[1]
    FH = fc_bias.shape[0]
    S = L * lax.axis_size("tensor")
    outer = packs // n
    inside = outer == 1
    cfg = (n, packs, L, S, D, HC, FH, inside)
    tokens = (block_input, out_cotangent)
    weights = (qkv_weight, attn_out_weight, fc_weight, proj_weight)
    if inside:
        tokens = [v.reshape(n, L // n, D) for v in tokens]
    else:
        slots = jnp.arange(packs, dtype=jnp.int32)
        chosen = (pack_order[None, :] == slots[:, None]).astype(BF)

        def pick(which, v):
            return (
                jnp.dot(which, v.reshape(packs, -1), preferred_element_type=F32)
                .astype(BF)
                .reshape(L, D)
            )

        tokens = [
            lax.all_to_all(
                pick(chosen, v), ("hi", "lo"), split_axis=0, concat_axis=0, tiled=True
            )
            for v in tokens
        ]
        weights = [
            lax.all_gather(w.astype(BF), "lo", axis=axis, tiled=True)
            for w, axis in zip(weights, (0, 1, 0, 1))
        ]
    row = lambda v: v.reshape(-1, 128)
    outs = outputs(cfg)
    made = pl.pallas_call(
        functools.partial(kernel, cfg),
        out_shape=[jax.ShapeDtypeStruct(shape, kind) for shape, kind in outs.values()],
        in_specs=list(inputs().values()),
        out_specs=[pl.BlockSpec(memory_space=pl.ANY)] * len(outs),
        scratch_shapes=list(scratch(cfg).values()),
        compiler_params=pltpu.CompilerParams(
            collective_id=0, has_side_effects=True, vmem_limit_bytes=63 * 2**20
        ),
    )(
        pack_order,
        seq_lengths.T,
        *tokens,
        row(ln1_gain),
        row(ln1_bias),
        jnp.transpose(weights[0], (1, 0, 2)),
        qv_bias,
        weights[1],
        row(attn_out_bias),
        row(ln2_gain),
        row(ln2_bias),
        weights[2],
        row(fc_bias),
        weights[3].T,
        row(proj_bias),
    )
    g = Refs(zip(outs, made))
    if not inside:
        exchange = lambda v: pick(
            chosen.T,
            lax.all_to_all(v, ("hi", "lo"), split_axis=0, concat_axis=0, tiled=True),
        )
        share = lambda v, axis: lax.psum_scatter(v, "lo", scatter_dimension=axis, tiled=True)
        g.out_y, g.out_x = exchange(g.out_y), exchange(g.out_x)
        g.out_qkv, g.out_wo = share(g.out_qkv, 1), share(g.out_wo, 1)
        g.out_w1, g.out_w2 = share(g.out_w1, 0), share(g.out_w2, 0)
        g.out_early, g.out_late = lax.psum((g.out_early, g.out_late), "lo")
    whole = [g.out_y.reshape(L, D), g.out_x.reshape(L, D), g.out_qkv, g.out_wo, g.out_w1, g.out_w2]
    vec = D // 128
    vmem = pl.BlockSpec(memory_space=pltpu.VMEM)
    settled = pl.pallas_call(
        settle,
        out_shape=[jax.ShapeDtypeStruct(v.shape, v.dtype) for v in whole]
        + [jax.ShapeDtypeStruct((vec, 128), F32)] * 6
        + [jax.ShapeDtypeStruct((FH // 128, 128), F32), jax.ShapeDtypeStruct((2, HC), F32)],
        in_specs=[vmem] * 8,
        out_specs=[vmem] * 14,
    )(*whole, g.out_early, g.out_late)
    out_y, out_x, qkv_sum, out_sum, fc_sum, proj_sum = settled[:6]
    pjb, ln2g, ln2b, aob, ln1g, ln1b = [v.reshape(D) for v in settled[6:12]]
    return (
        out_y,
        out_x,
        ln1g,
        ln1b,
        jnp.transpose(qkv_sum, (1, 0, 2)),
        settled[13],
        out_sum,
        aob,
        ln2g,
        ln2b,
        fc_sum,
        settled[12].reshape(FH),
        proj_sum.T,
        pjb,
    )


def solution(mesh):
    groups, members = mesh.shape["dp"], mesh.shape["tensor"]
    n = min(8, groups)
    cut = Mesh(mesh.devices.reshape(n, groups // n, members), ("hi", "lo", "tensor"))
    dp = ("hi", "lo")
    return jax.shard_map(
        functools.partial(local, n),
        mesh=cut,
        in_specs=(
            P(("hi", "lo", "tensor"), None),
            P(("hi", "lo", "tensor"), None),
            P(),
            P(),
            P(),
            P(),
            P(dp, None, "tensor"),
            P(None, "tensor"),
            P("tensor", dp),
            P(),
            P(),
            P(),
            P(dp, "tensor"),
            P("tensor"),
            P("tensor", dp),
            P(),
        ),
        out_specs=(
            P(("hi", "lo", "tensor"), None),
            P(("hi", "lo", "tensor"), None),
            P(),
            P(),
            P(dp, None, "tensor"),
            P(None, "tensor"),
            P("tensor", dp),
            P(),
            P(),
            P(),
            P(dp, "tensor"),
            P("tensor"),
            P("tensor", dp),
            P(),
        ),
        check_vma=False,
    )
```
